32 devices in a mesh: row: 8 (over z, core), col: 4 (over y, x).
Axes of the slice: x: 2, y: 2, z: 4, core: 2. Of those that a mesh axis runs over, the one named last changes fastest.
Arguments:
- tokens: bfloat16 [8192, 2048], P('row', 'col'), may hold values from -6 to 6
- attn_gain: float32 [2048], P('col'), may hold values from 0.5 to 1.5
- qkv_weight: bfloat16 [3, 2048, 2048], P(None, 'col', 'row'), may hold values from -0.125 to 0.125
- query_gain: float32 [128], replicated, may hold values from 0.5 to 1.5
- key_gain: float32 [128], replicated, may hold values from 0.5 to 1.5
- out_weight: bfloat16 [2048, 2048], P('row', 'col'), may hold values from -1.5 to 1.5
- moe_gain: float32 [2048], P('col'), may hold values from 0.5 to 1.5
- gate_up_weight: bfloat16 [64, 2048, 2048], P('row', 'col'), may hold values from -0.125 to 0.125
- down_weight: bfloat16 [64, 1024, 2048], P('row', None, 'col'), may hold values from -0.75 to 0.75
- segments: int32 [8, 1024], P('col'), may hold values from 0 to 3, never falling along the last dimension, each value on 1 to 800 neighbouring positions
- routes: int32 [8192, 8], replicated, may hold values from 0 to 63, all different within a row; in each aligned block of 8192 rows (0 to 8191, 8192 to 16383, ...) at most 2048 rows name the same one
- route_gates: float32 [8192, 8], replicated, may hold values from 0.06 to 0.19
- cotangent: bfloat16 [8192, 2048], P('row', 'col'), may hold values from -6 to 6
Outputs:
- output: bfloat16 [8192, 2048], P('row', 'col')
- grad_tokens: bfloat16 [8192, 2048], P('row', 'col')
- grad_attn_gain: float32 [2048], P('col')
- grad_qkv: float32 [3, 2048, 2048], P(None, 'col', 'row')
- grad_query_gain: float32 [128], replicated
- grad_key_gain: float32 [128], replicated
- grad_out_weight: float32 [2048, 2048], P('row', 'col')
- grad_moe_gain: float32 [2048], P('col')
- grad_gate_up: float32 [64, 2048, 2048], P('row', 'col')
- grad_down: float32 [64, 1024, 2048], P('row', None, 'col')
The draws below stay inside these ranges and needn't reach their ends.
Inputs may be any that keep to these rules, and one draw needn't show every extreme that they name: `routes`: each row names 8 different experts; each expert is named by at most 2048 rows in all, a bound that some block reaches. `segments`: in each sequence the numbers never fall and each of 0 to 3 appears; a document has at most 800 tokens, and some document has exactly 800.
All inputs are finite; a program needn't handle non-finite values.
Results may differ from the reference program's by a relative error of at most 0.028.
Values may be sent and summed in bfloat16 or wider, within the bound.
No kernel may reach another device: no remote copies, remote signals or barrier semaphores. Data moves between devices by JAX's collectives and lax.ppermute only.
A program may use at most 448 MiB of HBM per device.

```python
import math
import jax
import jax.numpy as jnp
import numpy as np
from jax import lax

D = 2048
H = 16
HD = 128
FF = 1024
E = 64
TOPK = 8
LEN = 1024
DOCS = 4
DOC_MAX = 800
SEQS = 8
TOKENS = 8192
CAP = 2048


def level_of(rng, extent, shards, low, top_value):
    loudness = 1.0
    for dim, parts in shards:
        heights = jax.random.uniform(jax.random.fold_in(jax.random.fold_in(rng, 6), dim), (parts,), jnp.float32, low / len(shards), top_value / len(shards))
        loudness = loudness * jnp.repeat(jnp.exp(heights), extent[dim] // parts).reshape((-1,) + (1,) * (len(extent) - 1 - dim))
    return loudness


def profile(count, total, reach, skew):
    loads = [(1 << 20) // math.isqrt(standing ** skew) + 1 for standing in range(2, count + 1)]
    surplus, given = total - reach - (count - 1), [1] * (count - 1)
    while surplus > 0:
        movable = [i for i in range(count - 1) if given[i] < reach]
        pool, left = sum([loads[i] for i in movable]), surplus
        for i in movable:
            extra = min(reach - given[i], max(1, left * loads[i] // pool), surplus)
            given[i] = given[i] + extra
            surplus = surplus - extra
    return np.array([reach] + given)


def ragged_sizes(own_key, amount, total, most, slope):
    if amount == 2:
        one = jax.random.randint(own_key, (), max(1, total - most), min(most, total - 1) + 1)
        return jnp.stack([one, total - one])
    sizes = jnp.asarray(profile(amount, total, most, slope), jnp.int32)
    couples = (amount - 1) // 2
    donor, taker = sizes[1:1 + 2 * couples:2], sizes[2:2 + 2 * couples:2]
    margin = jnp.minimum(donor - 1, most - taker)
    moved = jax.random.randint(jax.random.fold_in(own_key, 1), (couples,), 0, 1 << 20) % (margin + 1)
    sizes = sizes.at[1:1 + 2 * couples:2].set(donor - moved).at[2:2 + 2 * couples:2].set(taker + moved)
    return sizes[jax.random.permutation(jax.random.fold_in(own_key, 2), amount)]


def shared_out(stream_key, own, number, rows, amount, top, most, skew):
    ranking = jax.random.permutation(stream_key, amount)
    crowded, usual = load_shares(amount, rows * top, most, skew, True), load_shares(amount, rows * top, most, skew, False)
    places = jnp.arange(amount)

    def named(tallies, turn):
        used = int((tallies > 0).sum())
        fixed = max(1, used // 4)
        passed = fixed + (places - fixed + turn * (used - fixed)) % max(1, amount - fixed)
        return jnp.zeros((amount,), jnp.int32).at[ranking[jnp.where(places < fixed, places, passed)]].set(jnp.asarray(tallies, jnp.int32))

    tallies = jnp.where(number % 4 == 0, named(crowded, number // 4), named(usual, number - number // 4 - 1))
    mixed = jax.random.permutation(jax.random.fold_in(own, 3), amount)
    donor, taker = mixed[0:amount // 2 * 2:2], mixed[1:amount // 2 * 2:2]
    margin = jnp.minimum(tallies[donor] - 1, most - tallies[taker]) // 2
    margin = jnp.where((donor == ranking[0]) | (taker == ranking[0]) | (tallies[taker] == 0), 0, jnp.maximum(margin, 0))
    passed = jax.random.randint(jax.random.fold_in(own, 4), (amount // 2,), 0, 1 << 20) % (margin + 1)
    tallies = tallies.at[donor].add(-passed).at[taker].add(passed)
    items = jnp.searchsorted(jnp.cumsum(tallies), jnp.arange(rows * top), side="right").astype(jnp.int32)
    listing = items.reshape(top, rows).T
    listing = listing[jax.random.permutation(jax.random.fold_in(own, 1), rows)]
    turn = jax.random.randint(jax.random.fold_in(own, 2), (rows, 1), 0, top)
    return jnp.take_along_axis(listing, (jnp.arange(top)[None, :] + turn) % top, axis=1)


def load_shares(amount, total, reach, lean, full):
    loads = [(1 << 20) // math.isqrt(grade ** lean) + 1 for grade in range(1, amount + 1)]
    largest = reach if full else min(reach, max(-(-total // amount), total * loads[0] // sum(loads)))
    least = 1 if total - largest >= amount - 1 else 0
    given, rest = [largest] + [least] * (amount - 1), total - largest - least * (amount - 1)
    while rest > 0:
        movable = [i for i in range(1, amount) if given[i] < largest] or [i for i in range(1, amount) if given[i] < reach]
        pool, budget = sum([loads[i] for i in movable]), rest
        for i in movable:
            extra = min(reach - given[i], max(1, budget * loads[i] // pool), rest)
            given[i] = given[i] + extra
            rest = rest - extra
    return np.array(given)


def noise(key, dims, spread, most, cuts=(), kind=jnp.bfloat16):
    array = spread * jax.random.normal(key, dims, jnp.float32)
    if cuts:
        array = array * level_of(key, dims, cuts, -0.22, 0.18)
    return jnp.clip(array, -most, most).astype(kind)


def setup_inputs(seed: int = 0) -> dict:
    splits = jax.random.split(jax.random.key(seed), 14)
    tokens = noise(splits[0], (TOKENS, D), 1.0, 6.0, ((0, 8), (1, 4)))
    attn_gain = jnp.clip(1.0 + 0.1 * jax.random.normal(splits[1], (D,), jnp.float32), 0.5, 1.5)
    qkv_weight = noise(splits[2], (3, D, D), D ** -0.5, 0.125, ((1, 4), (2, 8)))
    query_gain = jnp.clip(1.0 + 0.1 * jax.random.normal(splits[3], (HD,), jnp.float32), 0.5, 1.5)
    key_gain = jnp.clip(1.0 + 0.1 * jax.random.normal(splits[4], (HD,), jnp.float32), 0.5, 1.5)
    out_weight = noise(splits[5], (D, D), (D // 128) ** -0.5, 1.5, ((0, 8), (1, 4)))
    moe_gain = jnp.clip(1.0 + 0.1 * jax.random.normal(splits[6], (D,), jnp.float32), 0.5, 1.5)
    gate_up_weight = noise(splits[7], (E, D, 2 * FF), D ** -0.5, 0.125, ((0, 8), (1, 4)))
    down_weight = noise(splits[8], (E, FF, D), (FF // 16) ** -0.5, 0.75, ((0, 8), (2, 4)))
    segments = jax.vmap(lambda own: jnp.searchsorted(jnp.cumsum(ragged_sizes(own, DOCS, LEN, DOC_MAX, 1)), jnp.arange(LEN), side="right"))(jax.random.split(splits[9], SEQS)).reshape((SEQS, LEN)).astype(jnp.int32)
    routes_keys = jax.random.split(jax.random.fold_in(splits[10], 1), TOKENS // TOKENS)
    routes_turns = jax.random.permutation(jax.random.fold_in(splits[10], 3), TOKENS // TOKENS)
    routes = jax.vmap(lambda own, number: shared_out(jax.random.fold_in(splits[10], 2), own, number, TOKENS, E, TOPK, CAP, 1))(routes_keys, routes_turns).reshape((TOKENS, TOPK))
    route_gates = jnp.clip(jax.random.uniform(splits[11], (TOKENS, TOPK), jnp.float32, 0.06, 0.19), 0.06, 0.19)
    cotangent = noise(splits[12], (TOKENS, D), 1.0, 6.0, ((0, 8), (1, 4)))
    return dict(tokens=tokens, attn_gain=attn_gain, qkv_weight=qkv_weight, query_gain=query_gain, key_gain=key_gain, out_weight=out_weight, moe_gain=moe_gain, gate_up_weight=gate_up_weight, down_weight=down_weight, segments=segments, routes=routes, route_gates=route_gates, cotangent=cotangent)


epsilon = 1e-06
rope_base = 10000.0
neg_large = -1e+30
highest = lax.Precision.HIGHEST

@jax.custom_vjp
def low(v):
    return lax.optimization_barrier(v.astype(jnp.bfloat16)).astype(jnp.float32)

@jax.custom_vjp
def low_back(v):
    return v

def low_keep(v):
    return (low(v), None)

def low_pass(kept, grad):
    return (grad,)

def back_keep(v):
    return (v, None)

def back_low(kept, grad):
    return (low(grad),)
low.defvjp(low_keep, low_pass)
low_back.defvjp(back_keep, back_low)

def scaled(values, gain):
    return values * lax.rsqrt(lax.optimization_barrier(jnp.mean(values * values, axis=-1, keepdims=True)) + epsilon) * gain

def rotate(values, cosine, sine):
    half_size = values.shape[-1] // 2
    turned = jnp.concatenate([-values[..., half_size:], values[..., :half_size]], axis=-1)
    return values * cosine + turned * sine

def rope_tables(segments, head_size):
    onehot = (segments[..., None] == jnp.arange(DOCS, dtype=jnp.int32)).astype(jnp.int32)
    counts = lax.optimization_barrier(jnp.sum(onehot, axis=1))
    starts = jnp.cumsum(counts, axis=-1) - counts
    first_index = lax.optimization_barrier(jnp.sum(onehot * starts[:, None, :], axis=-1))
    places = (jnp.arange(segments.shape[1], dtype=jnp.int32)[None, :] - first_index).astype(jnp.float32)
    rates = rope_base ** (-jnp.arange(0, head_size, 2, dtype=jnp.float32) / head_size)
    angles = places[..., None] * rates
    angles = jnp.concatenate([angles, angles], axis=-1)
    return (jnp.cos(angles), jnp.sin(angles))

def slot_tables(routes, route_gates):
    flat_routes = routes.reshape(-1)
    expert_ids = jnp.arange(E, dtype=jnp.int32)
    hits = (flat_routes[None, :] == expert_ids[:, None]).astype(jnp.int32)
    places = jnp.cumsum(hits, axis=1) - 1
    targets = jnp.where(hits == 1, places, CAP)
    owners = jnp.broadcast_to((jnp.arange(TOKENS * TOPK, dtype=jnp.int32) // TOPK)[None, :], hits.shape)
    gate_flat = jnp.broadcast_to(route_gates.reshape(-1)[None, :], hits.shape)
    expert_rows = jnp.broadcast_to(expert_ids[:, None], hits.shape)
    slot_token = jnp.zeros((E, CAP), jnp.int32).at[expert_rows, targets].set(owners, mode='drop')
    slot_gate = jnp.zeros((E, CAP), route_gates.dtype).at[expert_rows, targets].set(gate_flat, mode='drop')
    return (slot_token, slot_gate)

def reference(tokens, attn_gain, qkv_weight, query_gain, key_gain, out_weight, moe_gain, gate_up_weight, down_weight, segments, routes, route_gates, cotangent):
    cosine, sine = rope_tables(segments, HD)
    cosine = cosine.reshape(TOKENS, 1, HD)
    sine = sine.reshape(TOKENS, 1, HD)
    slot_token, slot_gate = slot_tables(routes, route_gates.astype(jnp.float32))
    factor = HD ** (-0.5)

    def attend_seq(packed):
        query, key, value, seg_row = packed
        raw_scores = jnp.einsum('qhd,khd->hqk', query, key, precision=highest)
        scores = low_back(raw_scores * factor)
        same = seg_row[:, None] == seg_row[None, :]
        scores = jnp.where(same[None], scores, neg_large)
        probs = jax.nn.softmax(scores, axis=-1)
        return jnp.einsum('hqk,khd->qhd', low(probs), value, precision=highest)

    def forward(stream, g_attn, w_qkv, g_query, g_key, w_out, g_moe, w_gate_up, w_down):
        normed = low(scaled(stream, g_attn))

        def project(index):
            return low_back(jnp.dot(normed, w_qkv[index], precision=highest)).reshape(TOKENS, H, HD)
        query = low(rotate(scaled(project(0), g_query), cosine, sine))
        key = low(rotate(scaled(project(1), g_key), cosine, sine))
        value = low(project(2))

        def by_seq(values):
            return values.reshape(SEQS, LEN, H, HD)
        attended = lax.map(jax.checkpoint(attend_seq), (by_seq(query), by_seq(key), by_seq(value), segments))
        heads_low = low(low_back(attended.reshape(TOKENS, D)))
        hidden_one = stream + low_back(jnp.dot(heads_low, w_out, precision=highest))
        moe_in = low(scaled(hidden_one, g_moe))

        def expert_step(packed):
            weight_in, weight_back, token_ids, gate_row = packed
            inner = jnp.dot(moe_in[token_ids], weight_in, precision=highest)
            gate_part = low_back(inner[:, :FF])
            up_part = low_back(inner[:, FF:])
            hidden = low(jax.nn.silu(gate_part) * up_part)
            result = low_back(jnp.dot(hidden, weight_back, precision=highest))
            return result * gate_row[:, None]
        expert_out = lax.map(jax.checkpoint(expert_step), (w_gate_up, w_down, slot_token, slot_gate))
        combined = jnp.zeros((TOKENS, D), jnp.float32).at[slot_token.reshape(-1)].add(expert_out.reshape(-1, D))
        return hidden_one + combined
    primals = (tokens.astype(jnp.float32), attn_gain.astype(jnp.float32), qkv_weight.astype(jnp.float32), query_gain.astype(jnp.float32), key_gain.astype(jnp.float32), out_weight.astype(jnp.float32), moe_gain.astype(jnp.float32), gate_up_weight.astype(jnp.float32), down_weight.astype(jnp.float32))
    result, pullback = jax.vjp(forward, *primals)
    grads = pullback(cotangent.astype(jnp.float32))
    return (result.astype(jnp.bfloat16), grads[0].astype(jnp.bfloat16), grads[1], grads[2], grads[3], grads[4], grads[5], grads[6], grads[7], grads[8])
```

```python
from functools import partial

import jax
import jax.numpy as jnp
from jax import lax
from jax.experimental import pallas as pl
from jax.experimental.pallas import tpu as pltpu
from jax.sharding import Mesh, PartitionSpec as P

DOCS = 4
epsilon = 1e-06
rope_base = 10000.0
neg_large = -1e30

ROW = ("chip", "core")
ALL = ("chip", "core", "col")
TILE = 256
BLOCK = 512
VMEM_BYTES = 58 * 1024 * 1024
F32 = jnp.float32
BF16 = jnp.bfloat16


def rotate(values, cosine, sine):
    half_size = values.shape[-1] // 2
    turned = jnp.concatenate([-values[..., half_size:], values[..., :half_size]], axis=-1)
    return values * cosine + turned * sine


def rotate_back(grads, cosine, sine):
    half_size = grads.shape[-1] // 2
    moved = grads * sine
    turned = jnp.concatenate([moved[..., half_size:], -moved[..., :half_size]], axis=-1)
    return grads * cosine + turned


def rope_tables(seg_row, head_size):
    docs = jnp.arange(DOCS, dtype=jnp.int32)
    starts = jnp.sum((seg_row[:, None] < docs[None, :]).astype(jnp.int32), axis=0)
    first_index = jnp.sum(
        jnp.where(seg_row[:, None] == docs[None, :], starts[None, :], 0), axis=-1
    )
    places = (jnp.arange(seg_row.shape[0], dtype=jnp.int32) - first_index).astype(F32)
    rates = rope_base ** (-jnp.arange(0, head_size, 2, dtype=F32) / head_size)
    angles = places[..., None] * rates
    angles = jnp.concatenate([angles, angles], axis=-1)
    return (jnp.cos(angles), jnp.sin(angles))


def width_total(values):
    return lax.psum(values, "col")


def norm_back(grad_normed, stream, rate, gain, model_width):
    scaled_grad = grad_normed * gain
    across = width_total(jnp.sum(scaled_grad * stream, axis=-1))[:, None]
    return rate * scaled_grad - stream * rate * rate * rate * across / model_width


def head_norm_back(grad_rot, normed, rate, gain, cosine, sine):
    grad_normed = rotate_back(grad_rot, cosine, sine)
    gain_grad = jnp.sum(grad_normed * normed, axis=(0, 1))
    scaled_grad = grad_normed * gain
    grad_raw = rate * (
        scaled_grad - normed * jnp.mean(scaled_grad * normed, axis=-1, keepdims=True)
    )
    return (grad_raw, gain_grad)


def attend_forward(factor, seg_row, packed):
    query, key, value = packed
    same = seg_row[:, None] == seg_row[None, :]
    scores = jnp.einsum("qd,kd->qk", query, key, preferred_element_type=F32) * factor
    scores = jnp.where(same, scores, neg_large)
    top_score = jnp.max(scores, axis=-1, keepdims=True)
    totals = jnp.sum(jnp.exp(scores - top_score), axis=-1, keepdims=True)
    log_total = top_score + jnp.log(totals)
    probs = jnp.exp(scores - log_total)
    result = jnp.einsum("qk,kd->qd", probs.astype(BF16), value, preferred_element_type=F32)
    return (result.astype(BF16), log_total[:, 0])


def attend_backward(factor, seg_row, packed):
    query, key, value, grad_out, log_total = packed
    same = seg_row[:, None] == seg_row[None, :]
    scores = jnp.einsum("qd,kd->qk", query, key, preferred_element_type=F32) * factor
    scores = jnp.where(same, scores, neg_large)
    probs = jnp.exp(scores - log_total[:, None])
    grad_probs = jnp.einsum("qd,kd->qk", grad_out, value, preferred_element_type=F32)
    center = jnp.sum(probs * grad_probs, axis=-1, keepdims=True)
    grad_scores = (probs * (grad_probs - center)).astype(BF16)
    grad_query = jnp.einsum("qk,kd->qd", grad_scores, key, preferred_element_type=F32) * factor
    grad_key = jnp.einsum("qk,qd->kd", grad_scores, query, preferred_element_type=F32) * factor
    grad_value = jnp.einsum("qk,qd->kd", probs.astype(BF16), grad_out, preferred_element_type=F32)
    return (grad_query, grad_key, grad_value.astype(BF16))


def slot_places(routes, route_gates, expert_ids):
    chosen = routes[None] == expert_ids[:, None, None]
    hit = jnp.any(chosen, axis=-1)
    gate = jnp.sum(jnp.where(chosen, route_gates[None], 0.0), axis=-1)
    count, tok_total = hit.shape
    grouped = hit.astype(BF16).reshape(count, tok_total // 128, 128)
    lane = jnp.arange(128)
    before = (lane[:, None] < lane[None, :]).astype(BF16)
    inside = jnp.einsum("egt,tu->egu", grouped, before, preferred_element_type=F32)
    totals = jnp.sum(grouped.astype(F32), axis=-1).astype(BF16)
    group = jnp.arange(tok_total // 128)
    earlier = (group[:, None] < group[None, :]).astype(BF16)
    offset = jnp.einsum("eg,gh->eh", totals, earlier, preferred_element_type=F32)
    place = (inside + offset[..., None]).reshape(count, tok_total).astype(jnp.int32)
    per_block = jnp.sum(hit.astype(jnp.int32).reshape(count, tok_total // BLOCK, BLOCK), axis=-1)
    begin = place.reshape(count, tok_total // BLOCK, BLOCK)[:, :, 0]
    end = begin + per_block
    low = begin // TILE
    high = jnp.where(end > begin, (end + TILE - 1) // TILE, low)
    return (jnp.where(hit, place, -1), gate, low, high)


def gather_kernel(scaled, low_ref, high_ref, rows_ref, place_ref, gate_ref, slots_ref):
    step = pl.program_id(0)
    experts = slots_ref.shape[0]
    parts, width = rows_ref.shape[1], rows_ref.shape[3]

    @pl.when(step == 0)
    def _():
        slots_ref[...] = jnp.zeros_like(slots_ref)

    for e in range(experts):
        place = place_ref[e, 0]
        gate = gate_ref[e, 0]

        def body(i, carry):
            base = pl.multiple_of(i * TILE, TILE)
            wanted = lax.broadcasted_iota(jnp.int32, (TILE, BLOCK), 0) + base
            mask = place == wanted
            onehot = mask.astype(F32).astype(BF16)
            if scaled:
                factor = jnp.sum(jnp.where(mask, gate, 0.0), axis=1, keepdims=True)
            for c in range(parts):
                picked = jnp.dot(onehot, rows_ref[0, c], preferred_element_type=F32)
                if scaled:
                    picked = picked * factor
                where = (e, pl.ds(base, TILE), slice(c * width, (c + 1) * width))
                slots_ref[where] = slots_ref[where] + picked.astype(BF16)
            return carry

        lax.fori_loop(low_ref[e, step], high_ref[e, step], body, 0)


def gather_slots(rows, place, gate, low, high, capacity, scaled):
    row_count, parts, per_row, width = rows.shape
    experts = place.shape[0]
    blocks = row_count * per_row // BLOCK
    each = per_row // BLOCK
    return pl.pallas_call(
        partial(gather_kernel, scaled),
        grid_spec=pltpu.PrefetchScalarGridSpec(
            num_scalar_prefetch=2,
            grid=(blocks,),
            in_specs=[
                pl.BlockSpec((1, parts, BLOCK, width), lambda b, *_: (b // each, 0, b % each, 0)),
                pl.BlockSpec((experts, 1, 1, BLOCK), lambda b, *_: (0, b, 0, 0)),
                pl.BlockSpec((experts, 1, 1, BLOCK), lambda b, *_: (0, b, 0, 0)),
            ],
            out_specs=pl.BlockSpec((experts, capacity, parts * width), lambda b, *_: (0, 0, 0)),
        ),
        out_shape=jax.ShapeDtypeStruct((experts, capacity, parts * width), BF16),
        compiler_params=pltpu.CompilerParams(vmem_limit_bytes=VMEM_BYTES),
        cost_estimate=pl.CostEstimate(
            flops=2 * 24 * experts * TILE * BLOCK * parts * width,
            bytes_accessed=rows.size * 2 + experts * capacity * parts * width * 2,
            transcendentals=0,
        ),
        name="gather_slots",
    )(
        low,
        high,
        rows,
        place.reshape(experts, blocks, 1, BLOCK),
        gate.reshape(experts, blocks, 1, BLOCK),
    )


def combine_kernel(scaled, each, low_ref, high_ref, core_ref, slots_ref, place_ref, gate_ref, out_ref, total_ref):
    chip, piece = pl.program_id(0), pl.program_id(1)
    block = (2 * chip + core_ref[0]) * each + piece
    experts = slots_ref.shape[0]
    parts, width = out_ref.shape[0], out_ref.shape[3]
    total_ref[...] = jnp.zeros_like(total_ref)
    for e in range(experts):
        place = jnp.broadcast_to(place_ref[e, 0].astype(F32), (8, BLOCK)).T[:, :1]
        if scaled:
            gate = jnp.broadcast_to(gate_ref[e, 0], (8, BLOCK)).T[:, :1]

        def body(i, carry):
            base = pl.multiple_of(i * TILE, TILE)
            wanted = lax.broadcasted_iota(jnp.int32, (BLOCK, TILE), 1) + base
            onehot = (place == wanted.astype(F32)).astype(F32).astype(BF16)
            for c in range(parts):
                columns = slice(c * width, (c + 1) * width)
                picked = jnp.dot(
                    onehot, slots_ref[e, pl.ds(base, TILE), columns], preferred_element_type=F32
                )
                if scaled:
                    picked = picked * gate
                total_ref[:, columns] = total_ref[:, columns] + picked
            return carry

        lax.fori_loop(low_ref[e, block], high_ref[e, block], body, 0)
    for c in range(parts):
        out_ref[c, 0] = total_ref[:, c * width : (c + 1) * width].astype(BF16)


def combine_slots(slots, place, gate, low, high, core, chips, per_row, parts, scaled):
    experts, capacity, model_width = slots.shape
    width = model_width // parts
    each = per_row // BLOCK
    blocks = place.shape[1] // BLOCK

    def token_block(z, j, low_ref, high_ref, core_ref):
        return (0, (2 * z + core_ref[0]) * each + j, 0, 0)

    return pl.pallas_call(
        partial(combine_kernel, scaled, each),
        grid_spec=pltpu.PrefetchScalarGridSpec(
            num_scalar_prefetch=3,
            grid=(chips, each),
            in_specs=[
                pl.BlockSpec(
                    (experts, capacity, model_width),
                    lambda *_: (0, 0, 0),
                    pipeline_mode=pl.Buffered(1),
                ),
                pl.BlockSpec((experts, 1, 1, BLOCK), token_block),
                pl.BlockSpec((experts, 1, 1, BLOCK), token_block),
            ],
            out_specs=pl.BlockSpec((parts, 1, BLOCK, width), lambda z, j, *_: (0, z, j, 0)),
            scratch_shapes=[pltpu.VMEM((BLOCK, model_width), F32)],
        ),
        out_shape=jax.ShapeDtypeStruct((parts, chips, per_row, width), BF16),
        compiler_params=pltpu.CompilerParams(vmem_limit_bytes=VMEM_BYTES),
        cost_estimate=pl.CostEstimate(
            flops=24 * experts * TILE * BLOCK * model_width,
            bytes_accessed=slots.size * 2 + parts * chips * per_row * width * 2,
            transcendentals=0,
        ),
        name="combine_slots",
    )(
        low,
        high,
        core,
        slots,
        place.reshape(experts, blocks, 1, BLOCK),
        gate.reshape(experts, blocks, 1, BLOCK),
    )


def swap_cores(values):
    return lax.ppermute(values, "core", [(0, 1), (1, 0)])


def swap_cols(values, mask):
    count = lax.axis_size("col")
    return lax.ppermute(values, "col", [(i, i ^ mask) for i in range(count)])


def spread_parts(parts, axis_out):
    count = lax.axis_size("col")
    me = lax.axis_index("col")
    size = parts.shape[1:][axis_out]
    shape = list(parts.shape[1:])
    shape[axis_out] = size * count
    result = jnp.zeros(shape, parts.dtype)
    for mask in range(count):
        there = me ^ mask
        piece = lax.dynamic_index_in_dim(parts, there, 0, keepdims=False)
        if mask:
            piece = swap_cols(piece, mask)
        result = lax.dynamic_update_slice_in_dim(result, piece, there * size, axis_out)
    return result


def sum_over_devices(other, mine):
    total = mine + swap_cores(other)
    total = lax.psum_scatter(total, "col", scatter_dimension=0, tiled=True)[0]
    return lax.psum_scatter(total, "chip", scatter_dimension=0, tiled=True)[0].astype(F32)


def heads_in(weight, ratio):
    chips, cols = lax.axis_size("chip"), lax.axis_size("col")
    rows = 2 * chips
    row = 2 * lax.axis_index("chip") + lax.axis_index("core")
    kinds, features, width = weight.shape
    block = features // ratio
    halves = weight.reshape(kinds, ratio, block, width).transpose(1, 2, 0, 3)
    joined = jnp.zeros((block, kinds, ratio, width), weight.dtype)
    for k in range(ratio):
        pairs = []
        for r in range(rows):
            for c in range(cols):
                h = (k + r) % ratio
                pairs.append((r * cols + c, (ratio * c + h) * cols + r // ratio))
        piece = lax.dynamic_index_in_dim(halves, (k + row) % ratio, 0, keepdims=False)
        piece = lax.ppermute(piece, ALL, pairs)
        place = (row % ratio - k) % ratio
        joined = lax.dynamic_update_slice_in_dim(joined, piece[:, :, None], place, 2)
    joined = joined.reshape(block, kinds * ratio * width)
    return lax.all_gather(joined, ROW, axis=0, tiled=True)


def heads_out(grad, kinds, ratio):
    chips, cols = lax.axis_size("chip"), lax.axis_size("col")
    rows = 2 * chips
    row = 2 * lax.axis_index("chip") + lax.axis_index("core")
    block = grad.shape[0] // rows
    mine = lax.psum_scatter(grad, ROW, scatter_dimension=0, tiled=True)
    width = grad.shape[1] // (kinds * ratio)
    mine = mine.reshape(block, kinds, ratio, width)
    result = jnp.zeros((kinds, ratio, block, width), grad.dtype)
    for k in range(ratio):
        pairs = []
        for r in range(rows):
            for c in range(cols):
                s = (r % ratio - k) % ratio
                pairs.append((r * cols + c, (ratio * c + s) * cols + r // ratio))
        piece = lax.dynamic_index_in_dim(mine, (row % ratio - k) % ratio, 2, keepdims=False)
        piece = lax.ppermute(piece, ALL, pairs).transpose(1, 0, 2)
        result = lax.dynamic_update_slice_in_dim(result, piece[:, None], (k + row) % ratio, 1)
    return result.reshape(kinds, ratio * block, width).astype(F32)


def local(
    tokens,
    attn_gain,
    qkv_weight,
    query_gain,
    key_gain,
    out_weight,
    moe_gain,
    gate_up_weight,
    down_weight,
    segments,
    routes,
    route_gates,
    cotangent,
):
    cols = lax.axis_size("col")
    chips = lax.axis_size("chip")
    rows = 2 * chips
    col = lax.axis_index("col")
    core = lax.axis_index("core")
    row = 2 * lax.axis_index("chip") + core
    per_row, col_width = tokens.shape
    model_width = col_width * cols
    head_size = query_gain.shape[0]
    ratio = rows // cols
    head_width = model_width // cols
    head_count = head_width // head_size
    factor = head_size ** (-0.5)

    experts_here, _, double_units = gate_up_weight.shape
    units = double_units // 2
    split = max(1, cols // experts_here)
    mine_count = experts_here * split // cols
    part_units = units // split
    capacity = 2 * rows * per_row * routes.shape[1] // (experts_here * rows)

    gate_up_parts = (
        gate_up_weight.reshape(experts_here, col_width, 2, split, part_units)
        .transpose(0, 3, 1, 2, 4)
        .reshape(cols, mine_count, col_width, 2 * part_units)
    )
    down_parts = down_weight.reshape(cols, mine_count, part_units, col_width)

    tokens_all = lax.all_gather(tokens, "col", axis=0)
    qkv_all = heads_in(qkv_weight, ratio)
    out_all = lax.all_gather(out_weight, ROW, axis=0, tiled=True)
    segs = lax.all_gather(segments, "col", axis=0, tiled=True)
    seg_row = lax.dynamic_index_in_dim(segs, row, 0, keepdims=False)
    gain_all = lax.all_gather(attn_gain, "col", axis=0)
    gate_up = spread_parts(gate_up_parts, 1)
    down = spread_parts(down_parts, 2)
    cot_all = lax.all_gather(cotangent, ALL, axis=0).reshape(rows, cols, per_row, col_width)

    cosine, sine = rope_tables(seg_row, head_size)
    cosine = cosine[:, None, :]
    sine = sine[:, None, :]
    stream_all = tokens_all.astype(F32)
    rate_one = lax.rsqrt(jnp.sum(stream_all * stream_all, axis=(0, 2)) / model_width + epsilon)
    normed_all = (stream_all * rate_one[None, :, None] * gain_all[:, None, :]).astype(BF16)
    normed_all = normed_all.transpose(1, 0, 2).reshape(per_row, model_width)
    rate_one = rate_one[:, None]
    qkv = jnp.dot(normed_all, qkv_all, preferred_element_type=F32)
    qkv = qkv.reshape(per_row, 3, head_count, head_size)
    query_raw, key_raw, value_raw = qkv[:, 0], qkv[:, 1], qkv[:, 2]
    query_rate = lax.rsqrt(jnp.mean(query_raw * query_raw, axis=-1, keepdims=True) + epsilon)
    key_rate = lax.rsqrt(jnp.mean(key_raw * key_raw, axis=-1, keepdims=True) + epsilon)
    query_normed = query_raw * query_rate
    key_normed = key_raw * key_rate
    query_items = rotate(query_normed * query_gain, cosine, sine).astype(BF16).transpose(1, 0, 2)
    key_items = rotate(key_normed * key_gain, cosine, sine).astype(BF16).transpose(1, 0, 2)
    value_items = value_raw.astype(BF16).transpose(1, 0, 2)
    attended, log_totals = lax.map(
        partial(attend_forward, factor, seg_row), (query_items, key_items, value_items)
    )
    heads_low = attended.transpose(1, 0, 2).reshape(per_row, head_width)
    heads_all = lax.all_gather(heads_low, "col", axis=0)
    out_split = out_all.reshape(cols, head_width, col_width)
    stream = tokens.astype(F32)
    hidden_one = stream + jnp.einsum("ctk,ckd->td", heads_all, out_split, preferred_element_type=F32)
    rate_two = lax.rsqrt(
        width_total(jnp.sum(hidden_one * hidden_one, axis=-1)) / model_width + epsilon
    )[:, None]
    moe_in = (hidden_one * rate_two * moe_gain).astype(BF16)

    moe_all = lax.all_gather(moe_in, ALL, axis=0).reshape(rows, cols, per_row, col_width)
    first = lax.axis_index("chip") * 2 * experts_here + core * experts_here
    expert_ids = first + (col * mine_count + jnp.arange(mine_count, dtype=jnp.int32)) // split
    place, gate, low, high = slot_places(routes, route_gates, expert_ids)
    grad_slot = gather_slots(cot_all, place, gate, low, high, capacity, True)
    slot_inputs = gather_slots(moe_all, place, gate, low, high, capacity, False)

    gate_weight = gate_up[..., :part_units]
    up_weight = gate_up[..., part_units:]
    gate_pre = jnp.einsum(
        "ecd,edf->ecf", slot_inputs, gate_weight, preferred_element_type=F32
    ).astype(BF16)
    up_pre = jnp.einsum(
        "ecd,edf->ecf", slot_inputs, up_weight, preferred_element_type=F32
    ).astype(BF16)
    grad_hidden = jnp.einsum("ecd,efd->ecf", grad_slot, down, preferred_element_type=F32)
    gate_wide = gate_pre.astype(F32)
    up_wide = up_pre.astype(F32)
    sigmoid_gate = jax.nn.sigmoid(gate_wide)
    activated = gate_wide * sigmoid_gate
    hidden = (activated * up_wide).astype(BF16)
    grad_gate_pre = (
        grad_hidden * up_wide * sigmoid_gate * (1.0 + gate_wide * (1.0 - sigmoid_gate))
    ).astype(BF16)
    grad_up_pre = (grad_hidden * activated).astype(BF16)
    grad_inner = jnp.concatenate([grad_gate_pre, grad_up_pre], axis=-1)
    grad_slot_in = jnp.einsum(
        "ecf,edf->ecd", grad_inner, gate_up, preferred_element_type=F32
    ).astype(BF16)
    mine = jnp.reshape(core, (1,))
    others = 1 - mine

    def give_back(slots, scaled):
        gather = partial(
            combine_slots, slots, place, gate, low, high,
            chips=chips, per_row=per_row, parts=cols, scaled=scaled,
        )
        return sum_over_devices(gather(core=others), gather(core=mine))

    grad_moe_in = give_back(grad_slot_in, False)
    expert_out = jnp.einsum("ecf,efd->ecd", hidden, down, preferred_element_type=F32).astype(BF16)
    moe_result = give_back(expert_out, True)
    output = (hidden_one + moe_result).astype(BF16)
    grad_down_parts = jnp.einsum(
        "ecf,ecd->efd", hidden, grad_slot, preferred_element_type=F32
    ).astype(BF16)
    grad_gate_up_parts = jnp.einsum(
        "ecd,ecf->edf", slot_inputs, grad_inner, preferred_element_type=F32
    ).astype(BF16)

    def collect(parts):
        result = spread_parts(parts[:, None], 0)
        return result

    grad_gate_up = collect(
        grad_gate_up_parts.reshape(mine_count, cols, col_width, 2 * part_units).transpose(1, 0, 2, 3)
    )
    grad_gate_up = (
        grad_gate_up.reshape(experts_here, split, col_width, 2, part_units)
        .transpose(0, 2, 3, 1, 4)
        .reshape(experts_here, col_width, double_units)
        .astype(F32)
    )
    grad_down = collect(
        grad_down_parts.reshape(mine_count, part_units, cols, col_width).transpose(2, 0, 1, 3)
    )
    grad_down = grad_down.reshape(experts_here, units, col_width).astype(F32)

    gain_two = jnp.sum(grad_moe_in * hidden_one * rate_two, axis=0)
    grad_hidden_one = cotangent.astype(F32) + norm_back(
        grad_moe_in, hidden_one, rate_two, moe_gain, model_width
    )
    grad_branch = grad_hidden_one.astype(BF16)
    grad_heads = lax.psum_scatter(
        jnp.einsum("td,ckd->ctk", grad_branch, out_split, preferred_element_type=F32).astype(BF16),
        "col",
        scatter_dimension=0,
        tiled=True,
    )[0]
    grad_out_weight = lax.psum_scatter(
        jnp.einsum("ctk,td->ckd", heads_all, grad_branch, preferred_element_type=F32)
        .astype(BF16)
        .reshape(model_width, col_width),
        ROW,
        scatter_dimension=0,
        tiled=True,
    ).astype(F32)
    grad_att_items = grad_heads.reshape(per_row, head_count, head_size).transpose(1, 0, 2)
    grad_query_items, grad_key_items, grad_value_items = lax.map(
        partial(attend_backward, factor, seg_row),
        (query_items, key_items, value_items, grad_att_items, log_totals),
    )
    grad_query_raw, gain_query = head_norm_back(
        grad_query_items.transpose(1, 0, 2), query_normed, query_rate, query_gain, cosine, sine
    )
    grad_key_raw, gain_key = head_norm_back(
        grad_key_items.transpose(1, 0, 2), key_normed, key_rate, key_gain, cosine, sine
    )
    grad_projected = jnp.concatenate(
        [
            grad_query_raw.astype(BF16),
            grad_key_raw.astype(BF16),
            grad_value_items.transpose(1, 0, 2),
        ],
        axis=1,
    ).reshape(per_row, 3 * head_width)
    grad_normed = lax.psum_scatter(
        jnp.einsum(
            "tk,cfk->ctf",
            grad_projected,
            qkv_all.reshape(cols, col_width, 3 * head_width),
            preferred_element_type=F32,
        ).astype(BF16),
        "col",
        scatter_dimension=0,
        tiled=True,
    )[0].astype(F32)
    grad_qkv = heads_out(
        jnp.einsum("td,tk->dk", normed_all, grad_projected, preferred_element_type=F32).astype(BF16),
        3,
        ratio,
    )
    gain_one = jnp.sum(grad_normed * stream * rate_one, axis=0)
    grad_tokens = (
        grad_hidden_one + norm_back(grad_normed, stream, rate_one, attn_gain, model_width)
    ).astype(BF16)
    grad_attn_gain, grad_moe_gain = lax.psum((gain_one, gain_two), ROW)
    grad_query_gain, grad_key_gain = lax.psum((gain_query, gain_key), ALL)
    return (
        output,
        grad_tokens,
        grad_attn_gain,
        grad_qkv,
        grad_query_gain,
        grad_key_gain,
        grad_out_weight,
        grad_moe_gain,
        grad_gate_up,
        grad_down,
    )


def solution(mesh):
    rows, cols = mesh.devices.shape
    fine = Mesh(mesh.devices.reshape(rows // 2, 2, cols), ("chip", "core", "col"))
    return jax.shard_map(
        local,
        mesh=fine,
        in_specs=(
            P(ROW, "col"),
            P("col"),
            P(None, "col", ROW),
            P(),
            P(),
            P(ROW, "col"),
            P("col"),
            P(ROW, "col", None),
            P(ROW, None, "col"),
            P("col", None),
            P(),
            P(),
            P(ROW, "col"),
        ),
        out_specs=(
            P(ROW, "col"),
            P(ROW, "col"),
            P("col"),
            P(None, "col", ROW),
            P(),
            P(),
            P(ROW, "col"),
            P("col"),
            P(ROW, "col", None),
            P(ROW, None, "col"),
        ),
        check_vma=False,
    )
```

```python
from functools import partial

import jax
import jax.numpy as jnp
from jax import lax
from jax.experimental import pallas as pl
from jax.experimental.layout import Layout, with_layout_constraint
from jax.experimental.pallas import tpu as pltpu
from jax.sharding import Mesh, PartitionSpec as P

DOCS = 4
epsilon = 1e-06
rope_base = 10000.0
neg_large = -1e30

ROW = ("chip", "core")
ALL = ("chip", "core", "col")
TILE = 256
BLOCK = 512
VMEM_BYTES = 58 * 1024 * 1024
F32 = jnp.float32
BF16 = jnp.bfloat16


def rope_tables(seg_row, head_size):
    docs = jnp.arange(DOCS, dtype=jnp.int32)
    starts = jnp.sum((seg_row[:, None] < docs[None, :]).astype(jnp.int32), axis=0)
    first_index = jnp.sum(
        jnp.where(seg_row[:, None] == docs[None, :], starts[None, :], 0), axis=-1
    )
    places = (jnp.arange(seg_row.shape[0], dtype=jnp.int32) - first_index).astype(F32)
    rates = rope_base ** (-jnp.arange(0, head_size, 2, dtype=F32) / head_size)
    angles = places[..., None] * rates
    angles = jnp.concatenate([angles, angles], axis=-1)
    return (jnp.cos(angles), jnp.sin(angles))


def width_total(values):
    return lax.psum(values, "col")


def norm_back(grad_normed, stream, rate, gain, model_width):
    scaled_grad = grad_normed * gain
    across = width_total(jnp.sum(scaled_grad * stream, axis=-1))[:, None]
    return rate * scaled_grad - stream * rate * rate * rate * across / model_width


def half_turn(values, sign):
    lane = lax.broadcasted_iota(jnp.int32, values.shape, 1)
    half = values.shape[1] // 2
    return jnp.where(lane < half, sign, -sign) * pltpu.roll(values, half, 1)


def head_norm(raw, gain, cosine, sine):
    rate = lax.rsqrt(jnp.mean(raw * raw, axis=-1, keepdims=True) + epsilon)
    normed = raw * rate
    gained = normed * gain
    return normed, rate, (gained * cosine + half_turn(gained, -1.0) * sine).astype(BF16)


def masked_scores(query, key, seg_col, seg_row, factor):
    scores = lax.dot_general(
        query, key, (((1,), (1,)), ((), ())), preferred_element_type=F32
    ) * factor
    return jnp.where(seg_col == seg_row, scores, neg_large)


def attend_kernel(
    factor, query_ref, key_ref, value_ref, cos_ref, sin_ref, row_ref, col_ref, gains_ref,
    out_ref, log_ref, low_ref,
):
    cosine, sine = cos_ref[...], sin_ref[...]
    low_ref[...] = head_norm(query_ref[...], gains_ref[0:1], cosine, sine)[2]
    key = head_norm(key_ref[...], gains_ref[1:2], cosine, sine)[2]
    value = value_ref[...].astype(BF16)
    seg_row = row_ref[...]

    def body(i, carry):
        rows = pl.ds(pl.multiple_of(i * TILE, TILE), TILE)
        scores = masked_scores(low_ref[rows], key, col_ref[rows], seg_row, factor)
        top = jnp.max(scores, axis=-1, keepdims=True)
        log_total = top + jnp.log(jnp.sum(jnp.exp(scores - top), axis=-1, keepdims=True))
        probs = jnp.exp(scores - log_total).astype(BF16)
        out_ref[rows] = jnp.dot(probs, value, preferred_element_type=F32).astype(BF16)
        log_ref[rows] = jnp.broadcast_to(log_total, (TILE, log_ref.shape[1]))
        return carry

    lax.fori_loop(0, query_ref.shape[0] // TILE, body, 0)


def attend_specs(tokens, size, heads):
    def part(k):
        return pl.BlockSpec((tokens, size), lambda h: (0, k * heads + h))

    whole = [
        pl.BlockSpec(shape, lambda h: (0, 0))
        for shape in ((tokens, size), (tokens, size), (1, tokens), (tokens, 1), (2, size))
    ]
    return [part(0), part(1), part(2)], whole


def attend_forward(qkv, cosine, sine, seg_row, gains):
    tokens, size = cosine.shape
    heads = qkv.shape[1] // (3 * size)
    parts, whole = attend_specs(tokens, size, heads)
    by_head = pl.BlockSpec((tokens, size), lambda h: (0, h))
    return pl.pallas_call(
        partial(attend_kernel, size ** (-0.5)),
        grid=(heads,),
        in_specs=parts + whole,
        out_specs=[by_head, by_head],
        out_shape=[
            jax.ShapeDtypeStruct((tokens, heads * size), BF16),
            jax.ShapeDtypeStruct((tokens, heads * size), F32),
        ],
        scratch_shapes=[pltpu.VMEM((tokens, size), BF16)],
        compiler_params=pltpu.CompilerParams(vmem_limit_bytes=VMEM_BYTES),
        cost_estimate=pl.CostEstimate(
            flops=4 * heads * tokens * tokens * size,
            bytes_accessed=qkv.size * 4 + tokens * heads * size * 6,
            transcendentals=2 * heads * tokens * tokens,
        ),
        name="attend_forward",
    )(qkv, qkv, qkv, cosine, sine, seg_row[None, :], seg_row[:, None], gains)


def attend_back_kernel(
    factor, query_ref, key_ref, value_ref, cos_ref, sin_ref, row_ref, col_ref, gains_ref,
    grad_ref, log_ref, out_ref, gain_ref, low_ref, query_grad, key_grad, value_grad,
):
    head, heads = pl.program_id(0), pl.num_programs(0)
    cosine, sine = cos_ref[...], sin_ref[...]
    gains = gains_ref[...]
    low_ref[...] = head_norm(query_ref[...], gains[0:1], cosine, sine)[2]
    key = head_norm(key_ref[...], gains[1:2], cosine, sine)[2]
    value = value_ref[...].astype(BF16)
    seg_row = row_ref[...]
    size = value.shape[1]
    key_grad[...] = jnp.zeros_like(key_grad)
    value_grad[...] = jnp.zeros_like(value_grad)

    def body(i, carry):
        rows = pl.ds(pl.multiple_of(i * TILE, TILE), TILE)
        query = low_ref[rows]
        grad_out = grad_ref[rows]
        scores = masked_scores(query, key, col_ref[rows], seg_row, factor)
        probs = jnp.exp(scores - log_ref[rows][:, :1])
        grad_probs = lax.dot_general(
            grad_out, value, (((1,), (1,)), ((), ())), preferred_element_type=F32
        )
        weighted = probs * grad_probs
        center = jnp.sum(weighted, axis=-1, keepdims=True)
        grad_scores = (weighted - probs * center).astype(BF16)
        query_grad[rows] = jnp.dot(grad_scores, key, preferred_element_type=F32) * factor
        first = (((0,), (0,)), ((), ()))
        key_grad[...] += lax.dot_general(grad_scores, query, first, preferred_element_type=F32)
        value_grad[...] += lax.dot_general(
            probs.astype(BF16), grad_out, first, preferred_element_type=F32
        )
        return carry

    lax.fori_loop(0, query_ref.shape[0] // TILE, body, 0)

    @pl.when(head == 0)
    def _():
        gain_ref[...] = jnp.zeros_like(gain_ref)

    for k, (raw_ref, grad) in enumerate(
        ((query_ref, query_grad[...]), (key_ref, key_grad[...] * factor))
    ):
        raw = raw_ref[...]
        rate = lax.rsqrt(jnp.mean(raw * raw, axis=-1, keepdims=True) + epsilon)
        normed = raw * rate
        grad_normed = grad * cosine + half_turn(grad * sine, 1.0)
        gain_ref[k : k + 1] += jnp.sum(grad_normed * normed, axis=0, keepdims=True)
        scaled = grad_normed * gains[k : k + 1]
        raw_grad = rate * (
            scaled - normed * jnp.mean(scaled * normed, axis=-1, keepdims=True)
        )
        columns = pl.ds(pl.multiple_of((k * heads + head) * size, size), size)
        out_ref[:, columns] = raw_grad.astype(BF16)
    columns = pl.ds(pl.multiple_of((2 * heads + head) * size, size), size)
    out_ref[:, columns] = value_grad[...].astype(BF16)


def attend_backward(qkv, cosine, sine, seg_row, gains, grad_heads, logs):
    tokens, size = cosine.shape
    heads = qkv.shape[1] // (3 * size)
    parts, whole = attend_specs(tokens, size, heads)
    by_head = pl.BlockSpec((tokens, size), lambda h: (0, h))
    return pl.pallas_call(
        partial(attend_back_kernel, size ** (-0.5)),
        grid=(heads,),
        in_specs=parts + whole + [by_head, by_head],
        out_specs=[
            pl.BlockSpec((tokens, 3 * heads * size), lambda h: (0, 0)),
            pl.BlockSpec((2, size), lambda h: (0, 0)),
        ],
        out_shape=[
            jax.ShapeDtypeStruct((tokens, 3 * heads * size), BF16),
            jax.ShapeDtypeStruct((2, size), F32),
        ],
        scratch_shapes=[
            pltpu.VMEM((tokens, size), BF16),
            pltpu.VMEM((tokens, size), F32),
            pltpu.VMEM((tokens, size), F32),
            pltpu.VMEM((tokens, size), F32),
        ],
        compiler_params=pltpu.CompilerParams(vmem_limit_bytes=VMEM_BYTES),
        cost_estimate=pl.CostEstimate(
            flops=10 * heads * tokens * tokens * size,
            bytes_accessed=qkv.size * 6 + tokens * heads * size * 6,
            transcendentals=heads * tokens * tokens,
        ),
        name="attend_backward",
    )(qkv, qkv, qkv, cosine, sine, seg_row[None, :], seg_row[:, None], gains, grad_heads, logs)


def slot_places(routes, route_gates, expert_ids):
    chosen = routes[None] == expert_ids[:, None, None]
    hit = jnp.any(chosen, axis=-1)
    gate = jnp.sum(jnp.where(chosen, route_gates[None], 0.0), axis=-1)
    count, tok_total = hit.shape
    grouped = hit.astype(BF16).reshape(count, tok_total // 128, 128)
    lane = jnp.arange(128)
    before = (lane[:, None] < lane[None, :]).astype(BF16)
    inside = jnp.einsum("egt,tu->egu", grouped, before, preferred_element_type=F32)
    totals = jnp.sum(grouped.astype(F32), axis=-1).astype(BF16)
    group = jnp.arange(tok_total // 128)
    earlier = (group[:, None] < group[None, :]).astype(BF16)
    offset = jnp.einsum("eg,gh->eh", totals, earlier, preferred_element_type=F32)
    place = (inside + offset[..., None]).reshape(count, tok_total).astype(jnp.int32)
    per_block = jnp.sum(hit.astype(jnp.int32).reshape(count, tok_total // BLOCK, BLOCK), axis=-1)
    begin = place.reshape(count, tok_total // BLOCK, BLOCK)[:, :, 0]
    end = begin + per_block
    low = begin // TILE
    high = jnp.where(end > begin, (end + TILE - 1) // TILE, low)
    return (jnp.where(hit, place, -1), gate, low, high)


def gather_kernel(scaled, each, low_ref, high_ref, *refs):
    rows_refs, place_refs, gate_refs, slots_ref = refs[0:2], refs[2:4], refs[4:6], refs[6]
    chip, piece = pl.program_id(0), pl.program_id(1)
    experts = slots_ref.shape[0]

    @pl.when((chip == 0) & (piece == 0))
    def _():
        slots_ref[...] = jnp.zeros_like(slots_ref)

    for k in range(2):
        rows_ref = rows_refs[k]
        parts, width = rows_ref.shape[1], rows_ref.shape[3]
        block = (2 * chip + k) * each + piece
        for e in range(experts):
            place = place_refs[k][e, 0]
            gate = gate_refs[k][e, 0]

            def body(i, carry):
                base = pl.multiple_of(i * TILE, TILE)
                wanted = lax.broadcasted_iota(jnp.int32, (TILE, BLOCK), 0) + base
                mask = place == wanted
                onehot = mask.astype(F32).astype(BF16)
                if scaled:
                    factor = jnp.sum(jnp.where(mask, gate, 0.0), axis=1, keepdims=True)
                for c in range(parts):
                    picked = jnp.dot(onehot, rows_ref[0, c], preferred_element_type=F32)
                    if scaled:
                        picked = picked * factor
                    where = (e, pl.ds(base, TILE), slice(c * width, (c + 1) * width))
                    slots_ref[where] = slots_ref[where] + picked.astype(BF16)
                return carry

            lax.fori_loop(low_ref[e, block], high_ref[e, block], body, 0)


def gather_slots(rows, place, gate, low, high, capacity, scaled):
    row_count, parts, per_row, width = rows.shape
    experts, tok_total = place.shape
    blocks = tok_total // BLOCK
    each = per_row // BLOCK

    def row_spec(k):
        return pl.BlockSpec(
            (1, parts, BLOCK, width),
            lambda z, j, *_: (2 * z + k, 0, j, 0),
        )

    def token_spec(k):
        return pl.BlockSpec(
            (experts, 1, 1, BLOCK),
            lambda z, j, *_: (0, (2 * z + k) * each + j, 0, 0),
        )

    places = place.reshape(experts, blocks, 1, BLOCK)
    gates = gate.reshape(experts, blocks, 1, BLOCK)
    return pl.pallas_call(
        partial(gather_kernel, scaled, each),
        grid_spec=pltpu.PrefetchScalarGridSpec(
            num_scalar_prefetch=2,
            grid=(row_count // 2, each),
            in_specs=[
                row_spec(0), row_spec(1), token_spec(0), token_spec(1), token_spec(0), token_spec(1),
            ],
            out_specs=pl.BlockSpec((experts, capacity, parts * width), lambda *_: (0, 0, 0)),
        ),
        out_shape=jax.ShapeDtypeStruct((experts, capacity, parts * width), BF16),
        compiler_params=pltpu.CompilerParams(vmem_limit_bytes=VMEM_BYTES),
        cost_estimate=pl.CostEstimate(
            flops=2 * 24 * experts * TILE * BLOCK * parts * width,
            bytes_accessed=(tok_total + experts * capacity) * parts * width * 2,
            transcendentals=0,
        ),
        name="gather_slots",
    )(low, high, rows, rows, places, places, gates, gates)


def combine_kernel(scaled, each, low_ref, high_ref, core_ref, slots_ref, place_ref, gate_ref, *refs):
    out_ref, total_ref = refs[-2:]
    chip, piece = pl.program_id(0), pl.program_id(1)
    block = (2 * chip + core_ref[0]) * each + piece
    experts = slots_ref.shape[0]
    parts, width = out_ref.shape[0], out_ref.shape[3]
    total_ref[...] = jnp.zeros_like(total_ref)
    for e in range(experts):
        place = jnp.broadcast_to(place_ref[e, 0].astype(F32), (8, BLOCK)).T[:, :1]
        if scaled:
            gate = jnp.broadcast_to(gate_ref[e, 0], (8, BLOCK)).T[:, :1]

        def body(i, carry):
            base = pl.multiple_of(i * TILE, TILE)
            wanted = lax.broadcasted_iota(jnp.int32, (BLOCK, TILE), 1) + base
            onehot = (place == wanted.astype(F32)).astype(F32).astype(BF16)
            for c in range(parts):
                columns = slice(c * width, (c + 1) * width)
                picked = jnp.dot(
                    onehot, slots_ref[e, pl.ds(base, TILE), columns], preferred_element_type=F32
                )
                if scaled:
                    picked = picked * gate
                total_ref[:, columns] = total_ref[:, columns] + picked
            return carry

        lax.fori_loop(low_ref[e, block], high_ref[e, block], body, 0)
    for c in range(parts):
        total = total_ref[:, c * width : (c + 1) * width]
        if len(refs) == 3:
            total = total + refs[0][c, 0].astype(F32)
        out_ref[c, 0] = total.astype(BF16)


def combine_slots(slots, place, gate, low, high, core, chips, per_row, parts, scaled, more=()):
    experts, capacity, model_width = slots.shape
    width = model_width // parts
    each = per_row // BLOCK
    blocks = place.shape[1] // BLOCK

    def token_block(z, j, low_ref, high_ref, core_ref):
        return (0, (2 * z + core_ref[0]) * each + j, 0, 0)

    sums = pl.BlockSpec((parts, 1, BLOCK, width), lambda z, j, *_: (0, z, j, 0))
    return pl.pallas_call(
        partial(combine_kernel, scaled, each),
        grid_spec=pltpu.PrefetchScalarGridSpec(
            num_scalar_prefetch=3,
            grid=(chips, each),
            in_specs=[
                pl.BlockSpec(
                    (experts, capacity, model_width),
                    lambda *_: (0, 0, 0),
                    pipeline_mode=pl.Buffered(1),
                ),
                pl.BlockSpec((experts, 1, 1, BLOCK), token_block),
                pl.BlockSpec((experts, 1, 1, BLOCK), token_block),
            ]
            + [sums] * len(more),
            out_specs=sums,
            scratch_shapes=[pltpu.VMEM((BLOCK, model_width), F32)],
        ),
        out_shape=jax.ShapeDtypeStruct((parts, chips, per_row, width), BF16),
        compiler_params=pltpu.CompilerParams(vmem_limit_bytes=VMEM_BYTES),
        cost_estimate=pl.CostEstimate(
            flops=24 * experts * TILE * BLOCK * model_width,
            bytes_accessed=slots.size * 2 + parts * chips * per_row * width * 2,
            transcendentals=0,
        ),
        name="combine_slots",
    )(
        low,
        high,
        core,
        slots,
        place.reshape(experts, blocks, 1, BLOCK),
        gate.reshape(experts, blocks, 1, BLOCK),
        *more,
    )


def swap_cores(values):
    return lax.ppermute(values, "core", [(0, 1), (1, 0)])


def swap_cols(values, mask):
    count = lax.axis_size("col")
    return lax.ppermute(values, "col", [(i, i ^ mask) for i in range(count)])


def fence(*values):
    return lax.optimization_barrier(values)


def plain(values):
    return with_layout_constraint(values, Layout(tuple(range(values.ndim))))


def gather_cols(values):
    count = lax.axis_size("col")
    me = lax.axis_index("col")
    result = jnp.zeros((count,) + values.shape, values.dtype)
    for mask in range(count):
        piece = swap_cols(values, mask) if mask else values
        result = lax.dynamic_update_index_in_dim(result, piece, me ^ mask, 0)
    return result


def sum_cols(parts):
    count = lax.axis_size("col")
    me = lax.axis_index("col")
    total = 0.0
    for mask in range(count):
        piece = lax.dynamic_index_in_dim(parts, me ^ mask, 0, keepdims=False)
        if mask:
            piece = swap_cols(piece, mask)
        total = total + piece.astype(F32)
    return total


def send_parts(parts):
    me = lax.axis_index("col")
    pieces = []
    for mask in range(lax.axis_size("col")):
        piece = plain(lax.dynamic_index_in_dim(parts, me ^ mask, 0, keepdims=False))
        pieces.append(swap_cols(piece, mask) if mask else piece)
    return pieces


def join_parts(pieces, axis, result=None, offset=0):
    me = lax.axis_index("col")
    if result is None:
        shape = list(pieces[0].shape)
        shape[axis] *= len(pieces)
        result = jnp.zeros(shape, pieces[0].dtype)
    size = result.shape[axis] // len(pieces)
    for mask, piece in enumerate(pieces):
        start = (me ^ mask) * size + offset
        result = lax.dynamic_update_slice_in_dim(result, piece, start, axis)
    return result


def swap_chips(values, mask):
    count = lax.axis_size("chip")
    return lax.ppermute(values, "chip", [(i, i ^ mask) for i in range(count)])


def over_chips(values):
    chips = lax.axis_size("chip")
    chip = lax.axis_index("chip")
    same = jnp.zeros((chips,) + values.shape, values.dtype)
    for mask in range(chips):
        piece = swap_chips(values, mask) if mask else values
        same = lax.dynamic_update_index_in_dim(same, piece, chip ^ mask, 0)
    return same


def over_cores(same):
    core = lax.axis_index("core")
    other = swap_cores(same)
    both = jnp.stack([jnp.where(core == 0, same, other), jnp.where(core == 0, other, same)], axis=1)
    return both.reshape(-1, same.shape[-1])


def pick(pieces, index):
    chosen = pieces[0]
    for k in range(1, len(pieces)):
        chosen = jnp.where(index == k, pieces[k], chosen)
    return chosen


def heads_in(weight, ratio):
    chips, cols = lax.axis_size("chip"), lax.axis_size("col")
    rows = 2 * chips
    row = 2 * lax.axis_index("chip") + lax.axis_index("core")
    kinds, features, width = weight.shape
    block = features // ratio
    pieces = []
    for k in range(ratio):
        pairs = []
        for r in range(rows):
            for c in range(cols):
                h = (k + r) % ratio
                pairs.append((r * cols + c, (ratio * c + h) * cols + r // ratio))
        piece = lax.dynamic_slice_in_dim(weight, (k + row) % ratio * block, block, 1)
        pieces.append(lax.ppermute(piece, ALL, pairs))
    joined = jnp.concatenate(
        [pick([p[a] for p in pieces], (row - s) % ratio) for a in range(kinds) for s in range(ratio)],
        axis=1,
    )
    return joined


def heads_out(grad, kinds, ratio):
    chips, cols = lax.axis_size("chip"), lax.axis_size("col")
    rows = 2 * chips
    row = 2 * lax.axis_index("chip") + lax.axis_index("core")
    block = grad.shape[0] // rows
    mine = lax.psum_scatter(grad, ROW, scatter_dimension=0, tiled=True)
    width = grad.shape[1] // (kinds * ratio)
    pieces = []
    for k in range(ratio):
        pairs = []
        for r in range(rows):
            for c in range(cols):
                s = (r - k) % ratio
                pairs.append((r * cols + c, (ratio * c + s) * cols + r // ratio))
        start = (row - k) % ratio * width
        piece = jnp.stack(
            [
                lax.dynamic_slice_in_dim(mine, a * ratio * width + start, width, 1)
                for a in range(kinds)
            ]
        )
        pieces.append(lax.ppermute(piece, ALL, pairs))
    return jnp.concatenate(
        [pick(pieces, (h - row) % ratio) for h in range(ratio)], axis=1
    ).astype(F32)


def sum_rows(values):
    total = values
    for axis in ROW:
        count = lax.axis_size(axis)
        step = 1
        while step < count:
            total = total + lax.ppermute(total, axis, [(i, i ^ step) for i in range(count)])
            step *= 2
    return total


def local(
    tokens,
    attn_gain,
    qkv_weight,
    query_gain,
    key_gain,
    out_weight,
    moe_gain,
    gate_up_weight,
    down_weight,
    segments,
    routes,
    route_gates,
    cotangent,
):
    cols = lax.axis_size("col")
    chips = lax.axis_size("chip")
    rows = 2 * chips
    col = lax.axis_index("col")
    core = lax.axis_index("core")
    row = 2 * lax.axis_index("chip") + core
    per_row, col_width = tokens.shape
    model_width = col_width * cols
    head_size = query_gain.shape[0]
    ratio = rows // cols
    head_width = model_width // cols

    experts_here, _, double_units = gate_up_weight.shape
    units = double_units // 2
    split = max(1, cols // experts_here)
    mine_count = experts_here * split // cols
    part_units = units // split
    capacity = 2 * rows * per_row * routes.shape[1] // (experts_here * rows)

    gate_up_parts = (
        gate_up_weight.reshape(experts_here, col_width, 2, split, part_units)
        .transpose(0, 3, 1, 2, 4)
        .reshape(cols, mine_count, col_width, 2 * part_units)
    )
    down_parts = down_weight.reshape(cols, mine_count, part_units, col_width)

    segs = gather_cols(segments)
    gain_all = gather_cols(attn_gain)
    tokens_all = gather_cols(tokens)
    quarter = col_width // 4
    gate_up_first = send_parts(gate_up_parts[:, :, :quarter])
    gate_up_second = send_parts(gate_up_parts[:, :, quarter : 2 * quarter])
    gate_up_last = send_parts(gate_up_parts[:, :, 2 * quarter :])
    qkv_in, out_in, cot_in, segs, gain_all, tokens_all, gate_up_first = fence(
        qkv_weight, out_weight, cotangent, segs, gain_all, tokens_all, gate_up_first
    )
    qkv_all = over_cores(over_chips(heads_in(qkv_in, ratio)))
    out_all = over_cores(over_chips(out_in))
    seg_row = lax.dynamic_index_in_dim(segs.reshape(rows, per_row), row, 0, keepdims=False)
    cot_all = lax.all_gather(cot_in, ALL, axis=0).reshape(rows, cols, per_row, col_width)

    first = row * experts_here
    expert_ids = first + (col * mine_count + jnp.arange(mine_count, dtype=jnp.int32)) // split
    place, gate, low, high = slot_places(routes, route_gates, expert_ids)

    cosine, sine = rope_tables(seg_row, head_size)
    stream_all = tokens_all.astype(F32)
    rate_one = lax.rsqrt(jnp.sum(stream_all * stream_all, axis=(0, 2)) / model_width + epsilon)
    rate_one = rate_one[:, None]
    normed_all = jnp.concatenate(
        [(stream_all[c] * rate_one * gain_all[c]).astype(BF16) for c in range(cols)], axis=1
    )
    qkv = jnp.dot(normed_all, qkv_all, preferred_element_type=F32)
    head_gains = jnp.stack([query_gain, key_gain])
    heads_low, logs = attend_forward(qkv, cosine, sine, seg_row, head_gains)
    heads_low, gate_up_second = fence(heads_low, gate_up_second)
    heads_all = gather_cols(heads_low)
    out_split = out_all.reshape(cols, head_width, col_width)
    stream = tokens.astype(F32)
    hidden_one = plain(
        stream + jnp.einsum("ctk,ckd->td", heads_all, out_split, preferred_element_type=F32)
    )
    rate_two = lax.rsqrt(
        width_total(jnp.sum(hidden_one * hidden_one, axis=-1)) / model_width + epsilon
    )[:, None]
    moe_in = plain((hidden_one * rate_two * moe_gain).astype(BF16))
    moe_in, gate_up_last, cot_all = fence(moe_in, gate_up_last, cot_all)
    gate_up = jnp.zeros((mine_count, model_width, 2 * part_units), BF16)
    gate_up = join_parts(gate_up_first, 1, gate_up, 0)
    gate_up = join_parts(gate_up_second, 1, gate_up, quarter)
    gate_up = join_parts(gate_up_last, 1, gate_up, 2 * quarter)

    moe_all = lax.all_gather(moe_in, ALL, axis=0).reshape(rows, cols, per_row, col_width)
    mine = jnp.reshape(core, (1,))
    others = 1 - mine
    grad_slot = gather_slots(cot_all, place, gate, low, high, capacity, True)
    moe_all, down_parts, grad_slot = fence(moe_all, down_parts, grad_slot)
    down = join_parts(send_parts(down_parts), 2)
    slot_inputs = gather_slots(moe_all, place, gate, low, high, capacity, False)

    gate_weight = gate_up[..., :part_units]
    up_weight = gate_up[..., part_units:]
    gate_pre = jnp.einsum(
        "ecd,edf->ecf", slot_inputs, gate_weight, preferred_element_type=F32
    ).astype(BF16)
    up_pre = jnp.einsum(
        "ecd,edf->ecf", slot_inputs, up_weight, preferred_element_type=F32
    ).astype(BF16)
    gate_wide = gate_pre.astype(F32)
    up_wide = up_pre.astype(F32)
    sigmoid_gate = jax.nn.sigmoid(gate_wide)
    activated = gate_wide * sigmoid_gate
    hidden = (activated * up_wide).astype(BF16)
    hidden, down = fence(hidden, down)

    combine = partial(
        combine_slots, place=place, gate=gate, low=low, high=high,
        chips=chips, per_row=per_row, parts=cols,
    )

    def feature_block(values, index):
        return lax.dynamic_slice_in_dim(values, index * col_width, col_width, 2)

    down_grads = []
    for mask in range(cols):
        part = jnp.einsum(
            "ecf,ecd->efd", hidden, feature_block(grad_slot, col ^ mask),
            preferred_element_type=F32,
        )
        down_grads.append(part.astype(BF16) if mask else part)
    down_grads, hidden = fence(down_grads, hidden)
    got_down = down_grads[:1] + [swap_cols(down_grads[mask], mask) for mask in range(1, cols)]

    expert_out = jnp.einsum("ecf,efd->ecd", hidden, down, preferred_element_type=F32).astype(BF16)
    out_other = combine(expert_out, core=others, scaled=True)
    out_other, grad_slot = fence(out_other, grad_slot)
    out_other = swap_cores(out_other)
    grad_hidden = jnp.einsum("ecd,efd->ecf", grad_slot, down, preferred_element_type=F32)
    grad_gate_pre = (
        grad_hidden * up_wide * sigmoid_gate * (1.0 + gate_wide * (1.0 - sigmoid_gate))
    ).astype(BF16)
    grad_up_pre = (grad_hidden * activated).astype(BF16)
    grad_inner = jnp.concatenate([grad_gate_pre, grad_up_pre], axis=-1)
    out_other, grad_inner = fence(out_other, grad_inner)
    out_partial = combine(expert_out, core=mine, scaled=True, more=(out_other,))
    out_partial, grad_inner, got_down = fence(out_partial, grad_inner, got_down)
    out_partial = plain(lax.psum_scatter(out_partial, "col", scatter_dimension=0, tiled=True)[0])

    grad_slot_in = jnp.einsum(
        "ecf,edf->ecd", grad_inner, gate_up, preferred_element_type=F32
    ).astype(BF16)
    grad_other = combine(grad_slot_in, core=others, scaled=False)
    grad_other, grad_inner = fence(grad_other, grad_inner)
    grad_other = swap_cores(grad_other)
    inner_parts = []
    for mask in range(cols):
        part = jnp.einsum(
            "ecd,ecf->edf", feature_block(slot_inputs, col ^ mask), grad_inner,
            preferred_element_type=F32,
        )
        inner_parts.append(part.astype(BF16) if mask else part)
    grad_other, inner_parts[1] = fence(grad_other, inner_parts[1])
    grad_partial = combine(grad_slot_in, core=mine, scaled=False, more=(grad_other,))
    grad_partial, out_partial = fence(grad_partial, out_partial)
    grad_partial = plain(lax.psum_scatter(grad_partial, "col", scatter_dimension=0, tiled=True)[0])
    grad_partial, inner_parts, out_partial = fence(grad_partial, inner_parts, out_partial)
    grad_moe_in = plain(lax.psum_scatter(grad_partial, "chip", scatter_dimension=0, tiled=True)[0])
    near = cols // 2 + 1
    far_parts = inner_parts[near:]
    got_inner = inner_parts[:1] + [swap_cols(inner_parts[mask], mask) for mask in range(1, near)]
    grad_moe_in, got_inner, out_partial, far_parts = fence(
        grad_moe_in, got_inner, out_partial, far_parts
    )
    grad_moe_in = grad_moe_in.astype(F32)

    gain_two = jnp.sum(grad_moe_in * hidden_one * rate_two, axis=0)
    grad_hidden_one = cotangent.astype(F32) + norm_back(
        grad_moe_in, hidden_one, rate_two, moe_gain, model_width
    )
    grad_branch = plain(grad_hidden_one.astype(BF16))
    grad_heads = sum_cols(
        jnp.einsum("td,ckd->ctk", grad_branch, out_split, preferred_element_type=F32).astype(BF16)
    ).astype(BF16)
    grad_heads, out_partial, far_parts = fence(grad_heads, out_partial, far_parts)
    far_parts = [swap_cols(part, near + i) for i, part in enumerate(far_parts)]
    moe_result = lax.psum_scatter(out_partial, "chip", scatter_dimension=0, tiled=True)[0]
    grad_out_weight = lax.psum_scatter(
        jnp.einsum("ctk,td->ckd", heads_all, grad_branch, preferred_element_type=F32)
        .astype(BF16)
        .reshape(model_width, col_width),
        ROW,
        scatter_dimension=0,
        tiled=True,
    ).astype(F32)
    grad_projected, grad_gains = attend_backward(
        qkv, cosine, sine, seg_row, head_gains, grad_heads, logs
    )
    grad_projected, far_parts, moe_result = fence(grad_projected, far_parts, moe_result)
    output = (hidden_one + moe_result.astype(F32)).astype(BF16)
    got_inner = got_inner + far_parts
    normed_parts = jnp.einsum(
        "tk,cfk->ctf",
        grad_projected,
        qkv_all.reshape(cols, col_width, 3 * head_width),
        preferred_element_type=F32,
    ).astype(BF16)
    normed_parts, grad_projected, got_inner, got_down = fence(
        normed_parts, grad_projected, got_inner, got_down
    )
    grad_normed = sum_cols(normed_parts)
    grad_qkv = heads_out(
        jnp.einsum("td,tk->dk", normed_all, grad_projected, preferred_element_type=F32).astype(BF16),
        3,
        ratio,
    )

    scaled_grad = grad_normed * attn_gain
    gain_one = jnp.sum(grad_normed * stream * rate_one, axis=0)
    across = jnp.sum(scaled_grad * stream, axis=-1)
    small = width_total(jnp.concatenate([across, grad_gains.reshape(-1)]))
    across = small[:per_row, None]
    gains = sum_rows(jnp.concatenate([gain_one, gain_two, small[per_row:]]))
    grad_attn_gain = gains[:col_width]
    grad_moe_gain = gains[col_width : 2 * col_width]
    grad_query_gain = gains[2 * col_width : 2 * col_width + head_size]
    grad_key_gain = gains[2 * col_width + head_size :]
    grad_tokens = (
        grad_hidden_one
        + rate_one * scaled_grad
        - stream * rate_one * rate_one * rate_one * across / model_width
    ).astype(BF16)

    grad_gate_up = jnp.zeros((cols, mine_count, col_width, 2 * part_units), F32)
    grad_down = jnp.zeros((cols, mine_count, part_units, col_width), F32)
    for mask in range(cols):
        there = col ^ mask
        grad_gate_up = lax.dynamic_update_index_in_dim(
            grad_gate_up, got_inner[mask].astype(F32), there, 0
        )
        grad_down = lax.dynamic_update_index_in_dim(grad_down, got_down[mask].astype(F32), there, 0)
    grad_gate_up = (
        grad_gate_up.reshape(experts_here, split, col_width, 2, part_units)
        .transpose(0, 2, 3, 1, 4)
        .reshape(experts_here, col_width, double_units)
    )
    grad_down = grad_down.reshape(experts_here, units, col_width)
    return (
        output,
        grad_tokens,
        grad_attn_gain,
        grad_qkv,
        grad_query_gain,
        grad_key_gain,
        grad_out_weight,
        grad_moe_gain,
        grad_gate_up,
        grad_down,
    )


def solution(mesh):
    rows, cols = mesh.devices.shape
    fine = Mesh(mesh.devices.reshape(rows // 2, 2, cols), ("chip", "core", "col"))
    return jax.shard_map(
        local,
        mesh=fine,
        in_specs=(
            P(ROW, "col"),
            P("col"),
            P(None, "col", ROW),
            P(),
            P(),
            P(ROW, "col"),
            P("col"),
            P(ROW, "col", None),
            P(ROW, None, "col"),
            P("col", None),
            P(),
            P(),
            P(ROW, "col"),
        ),
        out_specs=(
            P(ROW, "col"),
            P(ROW, "col"),
            P("col"),
            P(None, "col", ROW),
            P(),
            P(),
            P(ROW, "col"),
            P("col"),
            P(ROW, "col", None),
            P(ROW, None, "col"),
        ),
        check_vma=False,
    )
```

```python
from functools import partial

import jax
import jax.numpy as jnp
from jax import lax
from jax.experimental import pallas as pl
from jax.experimental.layout import Layout, with_layout_constraint
from jax.experimental.pallas import tpu as pltpu
from jax.sharding import Mesh, PartitionSpec as P

DOCS = 4
epsilon = 1e-06
rope_base = 10000.0
neg_large = -1e30

ROW = ("chip", "core")
ALL = ("chip", "core", "col")
TILE = 256
BLOCK = 512
VMEM_BYTES = 58 * 1024 * 1024
F32 = jnp.float32
BF16 = jnp.bfloat16


def rope_tables(seg_row, head_size):
    docs = jnp.arange(DOCS, dtype=jnp.int32)
    starts = jnp.sum((seg_row[:, None] < docs[None, :]).astype(jnp.int32), axis=0)
    first_index = jnp.sum(
        jnp.where(seg_row[:, None] == docs[None, :], starts[None, :], 0), axis=-1
    )
    places = (jnp.arange(seg_row.shape[0], dtype=jnp.int32) - first_index).astype(F32)
    rates = rope_base ** (-jnp.arange(0, head_size, 2, dtype=F32) / head_size)
    angles = places[..., None] * rates
    angles = jnp.concatenate([angles, angles], axis=-1)
    return (jnp.cos(angles), jnp.sin(angles))


def width_total(values):
    return lax.psum(values, "col")


def norm_back(grad_normed, stream, rate, gain, model_width):
    scaled_grad = grad_normed * gain
    across = width_total(jnp.sum(scaled_grad * stream, axis=-1))[:, None]
    return rate * scaled_grad - stream * rate * rate * rate * across / model_width


def half_turn(values, sign):
    lane = lax.broadcasted_iota(jnp.int32, values.shape, 1)
    half = values.shape[1] // 2
    return jnp.where(lane < half, sign, -sign) * pltpu.roll(values, half, 1)


def head_norm(raw, gain, cosine, sine):
    rate = lax.rsqrt(jnp.mean(raw * raw, axis=-1, keepdims=True) + epsilon)
    normed = raw * rate
    gained = normed * gain
    return normed, rate, (gained * cosine + half_turn(gained, -1.0) * sine).astype(BF16)


def masked_scores(query, key, seg_col, seg_row, factor):
    scores = lax.dot_general(
        query, key, (((1,), (1,)), ((), ())), preferred_element_type=F32
    ) * factor
    return jnp.where(seg_col == seg_row, scores, neg_large)


def attend_kernel(
    factor, query_ref, key_ref, value_ref, cos_ref, sin_ref, row_ref, col_ref, gains_ref,
    out_ref, log_ref, low_ref,
):
    cosine, sine = cos_ref[...], sin_ref[...]
    low_ref[...] = head_norm(query_ref[...], gains_ref[0:1], cosine, sine)[2]
    key = head_norm(key_ref[...], gains_ref[1:2], cosine, sine)[2]
    value = value_ref[...].astype(BF16)
    seg_row = row_ref[...]

    def body(i, carry):
        rows = pl.ds(pl.multiple_of(i * TILE, TILE), TILE)
        scores = masked_scores(low_ref[rows], key, col_ref[rows], seg_row, factor)
        top = jnp.max(scores, axis=-1, keepdims=True)
        log_total = top + jnp.log(jnp.sum(jnp.exp(scores - top), axis=-1, keepdims=True))
        probs = jnp.exp(scores - log_total).astype(BF16)
        out_ref[rows] = jnp.dot(probs, value, preferred_element_type=F32).astype(BF16)
        log_ref[rows] = jnp.broadcast_to(log_total, (TILE, log_ref.shape[1]))
        return carry

    lax.fori_loop(0, query_ref.shape[0] // TILE, body, 0)


def attend_specs(tokens, size, each):
    def part(k):
        return pl.BlockSpec((None, tokens, size), lambda h: (h // each, 0, k * each + h % each))

    whole = [
        pl.BlockSpec(shape, lambda h: (0, 0))
        for shape in ((tokens, size), (tokens, size), (1, tokens), (tokens, 1), (2, size))
    ]
    return [part(0), part(1), part(2)], whole


def attend_forward(qkv, cosine, sine, seg_row, gains):
    tokens, size = cosine.shape
    each = qkv.shape[2] // (3 * size)
    heads = qkv.shape[0] * each
    parts, whole = attend_specs(tokens, size, each)
    by_head = pl.BlockSpec((tokens, size), lambda h: (0, h))
    return pl.pallas_call(
        partial(attend_kernel, size ** (-0.5)),
        grid=(heads,),
        in_specs=parts + whole,
        out_specs=[by_head, by_head],
        out_shape=[
            jax.ShapeDtypeStruct((tokens, heads * size), BF16),
            jax.ShapeDtypeStruct((tokens, heads * size), F32),
        ],
        scratch_shapes=[pltpu.VMEM((tokens, size), BF16)],
        compiler_params=pltpu.CompilerParams(vmem_limit_bytes=VMEM_BYTES),
        cost_estimate=pl.CostEstimate(
            flops=4 * heads * tokens * tokens * size,
            bytes_accessed=qkv.size * 4 + tokens * heads * size * 6,
            transcendentals=2 * heads * tokens * tokens,
        ),
        name="attend_forward",
    )(qkv, qkv, qkv, cosine, sine, seg_row[None, :], seg_row[:, None], gains)


def attend_back_kernel(
    factor, each, query_ref, key_ref, value_ref, cos_ref, sin_ref, row_ref, col_ref, gains_ref,
    grad_ref, log_ref, out_ref, gain_ref, low_ref, query_grad, key_grad, value_grad,
):
    head = pl.program_id(0)
    group, place = head // each, head % each
    cosine, sine = cos_ref[...], sin_ref[...]
    gains = gains_ref[...]
    low_ref[...] = head_norm(query_ref[...], gains[0:1], cosine, sine)[2]
    key = head_norm(key_ref[...], gains[1:2], cosine, sine)[2]
    value = value_ref[...].astype(BF16)
    seg_row = row_ref[...]
    size = value.shape[1]
    key_grad[...] = jnp.zeros_like(key_grad)
    value_grad[...] = jnp.zeros_like(value_grad)

    def body(i, carry):
        rows = pl.ds(pl.multiple_of(i * TILE, TILE), TILE)
        query = low_ref[rows]
        grad_out = grad_ref[rows]
        scores = masked_scores(query, key, col_ref[rows], seg_row, factor)
        probs = jnp.exp(scores - log_ref[rows][:, :1])
        grad_probs = lax.dot_general(
            grad_out, value, (((1,), (1,)), ((), ())), preferred_element_type=F32
        )
        weighted = probs * grad_probs
        center = jnp.sum(weighted, axis=-1, keepdims=True)
        grad_scores = (weighted - probs * center).astype(BF16)
        query_grad[rows] = jnp.dot(grad_scores, key, preferred_element_type=F32) * factor
        first = (((0,), (0,)), ((), ()))
        key_grad[...] += lax.dot_general(grad_scores, query, first, preferred_element_type=F32)
        value_grad[...] += lax.dot_general(
            probs.astype(BF16), grad_out, first, preferred_element_type=F32
        )
        return carry

    lax.fori_loop(0, query_ref.shape[0] // TILE, body, 0)

    @pl.when(head == 0)
    def _():
        gain_ref[...] = jnp.zeros_like(gain_ref)

    for k, (raw_ref, grad) in enumerate(
        ((query_ref, query_grad[...]), (key_ref, key_grad[...] * factor))
    ):
        raw = raw_ref[...]
        rate = lax.rsqrt(jnp.mean(raw * raw, axis=-1, keepdims=True) + epsilon)
        normed = raw * rate
        grad_normed = grad * cosine + half_turn(grad * sine, 1.0)
        gain_ref[k : k + 1] += jnp.sum(grad_normed * normed, axis=0, keepdims=True)
        scaled = grad_normed * gains[k : k + 1]
        raw_grad = rate * (
            scaled - normed * jnp.mean(scaled * normed, axis=-1, keepdims=True)
        )
        columns = pl.ds(pl.multiple_of((k * each + place) * size, size), size)
        out_ref[group, :, columns] = raw_grad.astype(BF16)
    columns = pl.ds(pl.multiple_of((2 * each + place) * size, size), size)
    out_ref[group, :, columns] = value_grad[...].astype(BF16)


def attend_backward(qkv, cosine, sine, seg_row, gains, grad_heads, logs):
    tokens, size = cosine.shape
    each = qkv.shape[2] // (3 * size)
    heads = qkv.shape[0] * each
    parts, whole = attend_specs(tokens, size, each)
    by_head = pl.BlockSpec((tokens, size), lambda h: (0, h))
    return pl.pallas_call(
        partial(attend_back_kernel, size ** (-0.5), each),
        grid=(heads,),
        in_specs=parts + whole + [by_head, by_head],
        out_specs=[
            pl.BlockSpec(qkv.shape, lambda h: (0, 0, 0)),
            pl.BlockSpec((2, size), lambda h: (0, 0)),
        ],
        out_shape=[
            jax.ShapeDtypeStruct(qkv.shape, BF16),
            jax.ShapeDtypeStruct((2, size), F32),
        ],
        scratch_shapes=[
            pltpu.VMEM((tokens, size), BF16),
            pltpu.VMEM((tokens, size), F32),
            pltpu.VMEM((tokens, size), F32),
            pltpu.VMEM((tokens, size), F32),
        ],
        compiler_params=pltpu.CompilerParams(vmem_limit_bytes=VMEM_BYTES),
        cost_estimate=pl.CostEstimate(
            flops=10 * heads * tokens * tokens * size,
            bytes_accessed=qkv.size * 6 + tokens * heads * size * 6,
            transcendentals=heads * tokens * tokens,
        ),
        name="attend_backward",
    )(qkv, qkv, qkv, cosine, sine, seg_row[None, :], seg_row[:, None], gains, grad_heads, logs)


def slot_places(routes, route_gates, expert_ids):
    chosen = routes[None] == expert_ids[:, None, None]
    hit = jnp.any(chosen, axis=-1)
    gate = jnp.sum(jnp.where(chosen, route_gates[None], 0.0), axis=-1)
    count, tok_total = hit.shape
    grouped = hit.astype(BF16).reshape(count, tok_total // 128, 128)
    lane = jnp.arange(128)
    before = (lane[:, None] < lane[None, :]).astype(BF16)
    inside = jnp.einsum("egt,tu->egu", grouped, before, preferred_element_type=F32)
    totals = jnp.sum(grouped.astype(F32), axis=-1).astype(BF16)
    group = jnp.arange(tok_total // 128)
    earlier = (group[:, None] < group[None, :]).astype(BF16)
    offset = jnp.einsum("eg,gh->eh", totals, earlier, preferred_element_type=F32)
    place = (inside + offset[..., None]).reshape(count, tok_total).astype(jnp.int32)
    per_block = jnp.sum(hit.astype(jnp.int32).reshape(count, tok_total // BLOCK, BLOCK), axis=-1)
    begin = place.reshape(count, tok_total // BLOCK, BLOCK)[:, :, 0]
    end = begin + per_block
    low = begin // TILE
    high = jnp.where(end > begin, (end + TILE - 1) // TILE, low)
    return (jnp.where(hit, place, -1), gate, low, high)


def gather_kernel(scaled, each, low_ref, high_ref, *refs):
    rows_refs, place_refs, gate_refs, slots_ref = refs[0:2], refs[2:4], refs[4:6], refs[6]
    chip, piece = pl.program_id(0), pl.program_id(1)
    experts = slots_ref.shape[0]

    @pl.when((chip == 0) & (piece == 0))
    def _():
        slots_ref[...] = jnp.zeros_like(slots_ref)

    for k in range(2):
        rows_ref = rows_refs[k]
        parts, width = rows_ref.shape[1], rows_ref.shape[3]
        block = (2 * chip + k) * each + piece
        for e in range(experts):
            place = place_refs[k][e, 0]
            gate = gate_refs[k][e, 0]

            def body(i, carry):
                base = pl.multiple_of(i * TILE, TILE)
                wanted = lax.broadcasted_iota(jnp.int32, (TILE, BLOCK), 0) + base
                mask = place == wanted
                onehot = mask.astype(F32).astype(BF16)
                if scaled:
                    factor = jnp.sum(jnp.where(mask, gate, 0.0), axis=1, keepdims=True)
                for c in range(parts):
                    picked = jnp.dot(onehot, rows_ref[0, c], preferred_element_type=F32)
                    if scaled:
                        picked = picked * factor
                    where = (e, pl.ds(base, TILE), slice(c * width, (c + 1) * width))
                    slots_ref[where] = slots_ref[where] + picked.astype(BF16)
                return carry

            lax.fori_loop(low_ref[e, block], high_ref[e, block], body, 0)


def gather_slots(rows, place, gate, low, high, capacity, scaled):
    row_count, parts, per_row, width = rows.shape
    experts, tok_total = place.shape
    blocks = tok_total // BLOCK
    each = per_row // BLOCK

    def row_spec(k):
        return pl.BlockSpec(
            (1, parts, BLOCK, width),
            lambda z, j, *_: (2 * z + k, 0, j, 0),
        )

    def token_spec(k):
        return pl.BlockSpec(
            (experts, 1, 1, BLOCK),
            lambda z, j, *_: (0, (2 * z + k) * each + j, 0, 0),
        )

    places = place.reshape(experts, blocks, 1, BLOCK)
    gates = gate.reshape(experts, blocks, 1, BLOCK)
    return pl.pallas_call(
        partial(gather_kernel, scaled, each),
        grid_spec=pltpu.PrefetchScalarGridSpec(
            num_scalar_prefetch=2,
            grid=(row_count // 2, each),
            in_specs=[
                row_spec(0), row_spec(1), token_spec(0), token_spec(1), token_spec(0), token_spec(1),
            ],
            out_specs=pl.BlockSpec((experts, capacity, parts * width), lambda *_: (0, 0, 0)),
        ),
        out_shape=jax.ShapeDtypeStruct((experts, capacity, parts * width), BF16),
        compiler_params=pltpu.CompilerParams(vmem_limit_bytes=VMEM_BYTES),
        cost_estimate=pl.CostEstimate(
            flops=2 * 24 * experts * TILE * BLOCK * parts * width,
            bytes_accessed=(tok_total + experts * capacity) * parts * width * 2,
            transcendentals=0,
        ),
        name="gather_slots",
    )(low, high, rows, rows, places, places, gates, gates)


def combine_kernel(scaled, each, low_ref, high_ref, core_ref, slots_ref, place_ref, gate_ref, *refs):
    out_ref, total_ref = refs[-2:]
    chip, piece = pl.program_id(0), pl.program_id(1)
    block = (2 * chip + core_ref[0]) * each + piece
    experts = slots_ref.shape[0]
    parts, width = out_ref.shape[0], out_ref.shape[3]
    total_ref[...] = jnp.zeros_like(total_ref)
    for e in range(experts):
        place = jnp.broadcast_to(place_ref[e, 0].astype(F32), (8, BLOCK)).T[:, :1]
        if scaled:
            gate = jnp.broadcast_to(gate_ref[e, 0], (8, BLOCK)).T[:, :1]

        def body(i, carry):
            base = pl.multiple_of(i * TILE, TILE)
            wanted = lax.broadcasted_iota(jnp.int32, (BLOCK, TILE), 1) + base
            onehot = (place == wanted.astype(F32)).astype(F32).astype(BF16)
            for c in range(parts):
                columns = slice(c * width, (c + 1) * width)
                picked = jnp.dot(
                    onehot, slots_ref[e, pl.ds(base, TILE), columns], preferred_element_type=F32
                )
                if scaled:
                    picked = picked * gate
                total_ref[:, columns] = total_ref[:, columns] + picked
            return carry

        lax.fori_loop(low_ref[e, block], high_ref[e, block], body, 0)
    for c in range(parts):
        total = total_ref[:, c * width : (c + 1) * width]
        if len(refs) == 3:
            total = total + refs[0][c, 0].astype(F32)
        out_ref[c, 0] = total.astype(BF16)


def combine_slots(slots, place, gate, low, high, core, chips, per_row, parts, scaled, more=()):
    experts, capacity, model_width = slots.shape
    width = model_width // parts
    each = per_row // BLOCK
    blocks = place.shape[1] // BLOCK

    def token_block(z, j, low_ref, high_ref, core_ref):
        return (0, (2 * z + core_ref[0]) * each + j, 0, 0)

    sums = pl.BlockSpec((parts, 1, BLOCK, width), lambda z, j, *_: (0, z, j, 0))
    return pl.pallas_call(
        partial(combine_kernel, scaled, each),
        grid_spec=pltpu.PrefetchScalarGridSpec(
            num_scalar_prefetch=3,
            grid=(chips, each),
            in_specs=[
                pl.BlockSpec(
                    (experts, capacity, model_width),
                    lambda *_: (0, 0, 0),
                    pipeline_mode=pl.Buffered(1),
                ),
                pl.BlockSpec((experts, 1, 1, BLOCK), token_block),
                pl.BlockSpec((experts, 1, 1, BLOCK), token_block),
            ]
            + [sums] * len(more),
            out_specs=sums,
            scratch_shapes=[pltpu.VMEM((BLOCK, model_width), F32)],
        ),
        out_shape=jax.ShapeDtypeStruct((parts, chips, per_row, width), BF16),
        compiler_params=pltpu.CompilerParams(vmem_limit_bytes=VMEM_BYTES),
        cost_estimate=pl.CostEstimate(
            flops=24 * experts * TILE * BLOCK * model_width,
            bytes_accessed=slots.size * 2 + parts * chips * per_row * width * 2,
            transcendentals=0,
        ),
        name="combine_slots",
    )(
        low,
        high,
        core,
        slots,
        place.reshape(experts, blocks, 1, BLOCK),
        gate.reshape(experts, blocks, 1, BLOCK),
        *more,
    )


def swap_cores(values):
    return lax.ppermute(values, "core", [(0, 1), (1, 0)])


def swap_cols(values, mask):
    count = lax.axis_size("col")
    return lax.ppermute(values, "col", [(i, i ^ mask) for i in range(count)])


def fence(*values):
    return lax.optimization_barrier(values)


def plain(values):
    return with_layout_constraint(values, Layout(tuple(range(values.ndim))))


def gather_cols(values):
    count = lax.axis_size("col")
    me = lax.axis_index("col")
    result = jnp.zeros((count,) + values.shape, values.dtype)
    for mask in range(count):
        piece = swap_cols(values, mask) if mask else values
        result = lax.dynamic_update_index_in_dim(result, piece, me ^ mask, 0)
    return result


def sum_cols(pieces):
    total = 0.0
    for piece in send_parts(pieces):
        total = total + piece.astype(F32)
    return total


def split_parts(parts):
    me = lax.axis_index("col")
    return [
        plain(lax.dynamic_index_in_dim(parts, me ^ mask, 0, keepdims=False))
        for mask in range(lax.axis_size("col"))
    ]


def send_parts(pieces):
    return pieces[:1] + [swap_cols(pieces[mask], mask) for mask in range(1, len(pieces))]


def join_parts(pieces, axis, result=None, offset=0):
    me = lax.axis_index("col")
    if result is None:
        shape = list(pieces[0].shape)
        shape[axis] *= len(pieces)
        result = jnp.zeros(shape, pieces[0].dtype)
    size = result.shape[axis] // len(pieces)
    for mask, piece in enumerate(pieces):
        start = (me ^ mask) * size + offset
        result = lax.dynamic_update_slice_in_dim(result, piece, start, axis)
    return result


def swap_chips(values, mask):
    count = lax.axis_size("chip")
    return lax.ppermute(values, "chip", [(i, i ^ mask) for i in range(count)])


def over_chips(values):
    chips = lax.axis_size("chip")
    chip = lax.axis_index("chip")
    same = jnp.zeros((chips,) + values.shape, values.dtype)
    for mask in range(chips):
        piece = swap_chips(values, mask) if mask else values
        same = lax.dynamic_update_index_in_dim(same, piece, chip ^ mask, 0)
    return same


def over_cores(same):
    core = lax.axis_index("core")
    other = swap_cores(same)
    both = jnp.stack([jnp.where(core == 0, same, other), jnp.where(core == 0, other, same)], axis=1)
    return both.reshape(-1, same.shape[-1])


def pick(pieces, index):
    chosen = pieces[0]
    for k in range(1, len(pieces)):
        chosen = jnp.where(index == k, pieces[k], chosen)
    return chosen


def own_heads(cols, heads_row):
    return 2 * heads_row == cols


def heads_in(weight, ratio, size):
    chips, cols = lax.axis_size("chip"), lax.axis_size("col")
    core, col = lax.axis_index("core"), lax.axis_index("col")
    rows = 2 * chips
    row = 2 * lax.axis_index("chip") + core
    kinds, features, width = weight.shape
    pieces = []
    if own_heads(cols, width // size):
        p = width // size
        for t in range(p):
            pairs = [
                (k * cols + c, c // p * cols + k * p + (t + c) % p)
                for k in range(2)
                for c in range(cols)
            ]
            piece = lax.dynamic_slice_in_dim(weight, (t + col) % p * size, size, 2)
            pieces.append(lax.ppermute(piece, ("core", "col"), pairs))
        pieces = [pick(pieces, (col - b) % p) for b in range(p)]
        return jnp.concatenate(
            [jnp.concatenate([p[a] for a in range(kinds)], axis=1) for p in pieces], axis=0
        )
    block = features // ratio
    for k in range(ratio):
        pairs = []
        for r in range(rows):
            for c in range(cols):
                h = (k + r) % ratio
                pairs.append((r * cols + c, (ratio * c + h) * cols + r // ratio))
        piece = lax.dynamic_slice_in_dim(weight, (k + row) % ratio * block, block, 1)
        pieces.append(lax.ppermute(piece, ALL, pairs))
    return jnp.concatenate(
        [pick([p[a] for p in pieces], (row - s) % ratio) for a in range(kinds) for s in range(ratio)],
        axis=1,
    )


def heads_out(grad, kinds, ratio, heads_row):
    chips, cols = lax.axis_size("chip"), lax.axis_size("col")
    col = lax.axis_index("col")
    rows = 2 * chips
    row = 2 * lax.axis_index("chip") + lax.axis_index("core")
    mine = grad.reshape(rows, -1, grad.shape[2])
    mine = lax.psum_scatter(mine, ROW, scatter_dimension=0, tiled=True)[0]
    block = mine.shape[0]
    pieces = []
    if own_heads(cols, heads_row):
        p = heads_row
        size = mine.shape[1] // kinds
        for t in range(p):
            pairs = [
                (k * cols + c, c // p * cols + k * p + (c - t) % p)
                for k in range(2)
                for c in range(cols)
            ]
            piece = lax.dynamic_slice_in_dim(mine, (col - t) % p * (block // p), block // p, 0)
            pieces.append(lax.ppermute(piece, ("core", "col"), pairs))
        pieces = [pick(pieces, (i - col) % p) for i in range(p)]
        return jnp.stack(
            [
                jnp.concatenate([q[:, a * size : (a + 1) * size] for q in pieces], axis=1)
                for a in range(kinds)
            ]
        ).astype(F32)
    width = mine.shape[1] // (kinds * ratio)
    for k in range(ratio):
        pairs = []
        for r in range(rows):
            for c in range(cols):
                s = (r - k) % ratio
                pairs.append((r * cols + c, (ratio * c + s) * cols + r // ratio))
        start = (row - k) % ratio * width
        piece = jnp.stack(
            [
                lax.dynamic_slice_in_dim(mine, a * ratio * width + start, width, 1)
                for a in range(kinds)
            ]
        )
        pieces.append(lax.ppermute(piece, ALL, pairs))
    return jnp.concatenate(
        [pick(pieces, (h - row) % ratio) for h in range(ratio)], axis=1
    ).astype(F32)


def sum_rows(values):
    total = values
    for axis in ROW:
        count = lax.axis_size(axis)
        step = 1
        while step < count:
            total = total + lax.ppermute(total, axis, [(i, i ^ step) for i in range(count)])
            step *= 2
    return total


def local(
    tokens,
    attn_gain,
    qkv_weight,
    query_gain,
    key_gain,
    out_weight,
    moe_gain,
    gate_up_weight,
    down_weight,
    segments,
    routes,
    route_gates,
    cotangent,
):
    cols = lax.axis_size("col")
    chips = lax.axis_size("chip")
    rows = 2 * chips
    col = lax.axis_index("col")
    core = lax.axis_index("core")
    row = 2 * lax.axis_index("chip") + core
    per_row, col_width = tokens.shape
    model_width = col_width * cols
    head_size = query_gain.shape[0]
    ratio = rows // cols
    head_width = model_width // cols

    experts_here, _, double_units = gate_up_weight.shape
    units = double_units // 2
    split = max(1, cols // experts_here)
    mine_count = experts_here * split // cols
    part_units = units // split
    capacity = 2 * rows * per_row * routes.shape[1] // (experts_here * rows)

    gate_up_parts = (
        gate_up_weight.reshape(experts_here, col_width, 2, split, part_units)
        .transpose(0, 3, 1, 2, 4)
        .reshape(cols, mine_count, col_width, 2 * part_units)
    )
    down_parts = down_weight.reshape(cols, mine_count, part_units, col_width)

    heads_row = qkv_weight.shape[2] // head_size
    groups = chips if own_heads(cols, heads_row) else 1

    def by_col(values):
        if groups == 1:
            return values.reshape(cols, head_width, col_width)
        values = values.reshape(groups, cols, head_width // groups, col_width)
        return values.transpose(1, 0, 2, 3).reshape(cols, head_width, col_width)

    def by_head(values):
        if groups > 1:
            values = values.reshape(cols, groups, head_width // groups, col_width)
            values = values.transpose(1, 0, 2, 3)
        return values.reshape(model_width, col_width)

    segs = gather_cols(segments)
    gain_all = gather_cols(attn_gain)
    tokens_all = gather_cols(tokens)
    qkv_rows, segs, gain_all, tokens_all, out_in = fence(
        heads_in(qkv_weight, ratio, head_size), segs, gain_all, tokens_all, out_weight
    )
    cuts = (0, col_width // 2, 3 * col_width // 4, col_width)
    first, second, last = (
        split_parts(gate_up_parts[:, :, cuts[i] : cuts[i + 1]]) for i in range(3)
    )
    gate_up_first = send_parts(first)
    qkv_rows, out_rows, gate_up_first, second, last, cot_in = fence(
        over_chips(qkv_rows), over_chips(out_in), gate_up_first, second, last, cotangent
    )
    gate_up_second, gate_up_last = send_parts(second), send_parts(last)
    if groups > 1:
        half = model_width // 2
        qkv_halves = [(qkv_rows, core * half), (swap_cores(qkv_rows), (1 - core) * half)]
    else:
        half = model_width
        qkv_halves = [(over_cores(qkv_rows)[None], 0)]
    out_split = by_col(over_cores(out_rows))
    seg_row = lax.dynamic_index_in_dim(segs.reshape(rows, per_row), row, 0, keepdims=False)
    cot_all = lax.all_gather(cot_in, ALL, axis=0).reshape(rows, cols, per_row, col_width)

    first = row * experts_here
    expert_ids = first + (col * mine_count + jnp.arange(mine_count, dtype=jnp.int32)) // split
    place, gate, low, high = slot_places(routes, route_gates, expert_ids)

    cosine, sine = rope_tables(seg_row, head_size)
    stream_all = tokens_all.astype(F32)
    rate_one = lax.rsqrt(jnp.sum(stream_all * stream_all, axis=(0, 2)) / model_width + epsilon)
    rate_one = rate_one[:, None]
    normed_all = jnp.concatenate(
        [(stream_all[c] * rate_one * gain_all[c]).astype(BF16) for c in range(cols)], axis=1
    )
    qkv = sum(
        jnp.einsum(
            "td,gdk->gtk",
            lax.dynamic_slice_in_dim(normed_all, begin, half, 1),
            weight,
            preferred_element_type=F32,
        )
        for weight, begin in qkv_halves
    )
    head_gains = jnp.stack([query_gain, key_gain])
    heads_low, logs = attend_forward(qkv, cosine, sine, seg_row, head_gains)
    heads_low, gate_up_second = fence(heads_low, gate_up_second)
    heads_all = gather_cols(heads_low)
    stream = tokens.astype(F32)
    hidden_one = plain(
        stream + jnp.einsum("ctk,ckd->td", heads_all, out_split, preferred_element_type=F32)
    )
    rate_two = lax.rsqrt(
        width_total(jnp.sum(hidden_one * hidden_one, axis=-1)) / model_width + epsilon
    )[:, None]
    moe_in = plain((hidden_one * rate_two * moe_gain).astype(BF16))
    moe_in, gate_up_last, cot_all, down_first = fence(
        moe_in, gate_up_last, cot_all, split_parts(down_parts)
    )
    gate_up = jnp.zeros((mine_count, model_width, 2 * part_units), BF16)
    gate_up = join_parts(gate_up_first, 1, gate_up, 0)
    gate_up = join_parts(gate_up_second, 1, gate_up, cuts[1])
    gate_up = join_parts(gate_up_last, 1, gate_up, cuts[2])

    moe_all = lax.all_gather(moe_in, ALL, axis=0).reshape(rows, cols, per_row, col_width)
    mine = jnp.reshape(core, (1,))
    others = 1 - mine
    grad_slot = gather_slots(cot_all, place, gate, low, high, capacity, True)
    moe_all, down_first, grad_slot = fence(moe_all, down_first, grad_slot)
    down = join_parts(send_parts(down_first), 2)
    slot_inputs = gather_slots(moe_all, place, gate, low, high, capacity, False)

    gate_weight = gate_up[..., :part_units]
    up_weight = gate_up[..., part_units:]
    gate_pre = jnp.einsum(
        "ecd,edf->ecf", slot_inputs, gate_weight, preferred_element_type=F32
    ).astype(BF16)
    up_pre = jnp.einsum(
        "ecd,edf->ecf", slot_inputs, up_weight, preferred_element_type=F32
    ).astype(BF16)
    gate_wide = gate_pre.astype(F32)
    up_wide = up_pre.astype(F32)
    sigmoid_gate = jax.nn.sigmoid(gate_wide)
    activated = gate_wide * sigmoid_gate
    hidden = (activated * up_wide).astype(BF16)
    hidden, down = fence(hidden, down)

    combine = partial(
        combine_slots, place=place, gate=gate, low=low, high=high,
        chips=chips, per_row=per_row, parts=cols,
    )

    def feature_block(values, index):
        return lax.dynamic_slice_in_dim(values, index * col_width, col_width, 2)

    down_grads = []
    for mask in range(cols):
        part = jnp.einsum(
            "ecf,ecd->efd", hidden, feature_block(grad_slot, col ^ mask),
            preferred_element_type=F32,
        )
        down_grads.append(part.astype(BF16) if mask else part)
    down_grads, hidden = fence(down_grads, hidden)
    got_down = down_grads[:1] + [swap_cols(down_grads[mask], mask) for mask in range(1, cols)]

    expert_out = jnp.einsum("ecf,efd->ecd", hidden, down, preferred_element_type=F32).astype(BF16)
    out_other = combine(expert_out, core=others, scaled=True)
    near = cols // 2 + 1
    out_other, grad_slot, near_down = fence(out_other, grad_slot, got_down[1:near])
    got_down[1:near] = near_down
    out_other = swap_cores(out_other)
    grad_hidden = jnp.einsum("ecd,efd->ecf", grad_slot, down, preferred_element_type=F32)
    grad_gate_pre = (
        grad_hidden * up_wide * sigmoid_gate * (1.0 + gate_wide * (1.0 - sigmoid_gate))
    ).astype(BF16)
    grad_up_pre = (grad_hidden * activated).astype(BF16)
    grad_inner = jnp.concatenate([grad_gate_pre, grad_up_pre], axis=-1)
    out_other, grad_inner = fence(out_other, grad_inner)
    out_partial = combine(expert_out, core=mine, scaled=True, more=(out_other,))
    out_partial, grad_inner, got_down = fence(out_partial, grad_inner, got_down)
    out_partial = plain(lax.psum_scatter(out_partial, "col", scatter_dimension=0, tiled=True)[0])

    grad_slot_in = jnp.einsum(
        "ecf,edf->ecd", grad_inner, gate_up, preferred_element_type=F32
    ).astype(BF16)
    grad_other = combine(grad_slot_in, core=others, scaled=False)
    grad_other, grad_inner = fence(grad_other, grad_inner)
    grad_other = swap_cores(grad_other)
    inner_parts = []
    for mask in range(cols):
        part = jnp.einsum(
            "ecd,ecf->edf", feature_block(slot_inputs, col ^ mask), grad_inner,
            preferred_element_type=F32,
        )
        inner_parts.append(part.astype(BF16) if mask else part)
    grad_other, inner_parts[1] = fence(grad_other, inner_parts[1])
    grad_partial = combine(grad_slot_in, core=mine, scaled=False, more=(grad_other,))
    grad_partial, out_partial = fence(grad_partial, out_partial)
    grad_partial = plain(lax.psum_scatter(grad_partial, "col", scatter_dimension=0, tiled=True)[0])
    grad_partial, inner_parts, out_partial = fence(grad_partial, inner_parts, out_partial)
    grad_moe_in = plain(lax.psum_scatter(grad_partial, "chip", scatter_dimension=0, tiled=True)[0])
    far_parts = inner_parts[near:]
    got_inner = inner_parts[:1] + [swap_cols(inner_parts[mask], mask) for mask in range(1, near)]
    grad_moe_in, got_inner, out_partial, far_parts = fence(
        grad_moe_in, got_inner, out_partial, far_parts
    )
    grad_moe_in = grad_moe_in.astype(F32)

    gain_two = jnp.sum(grad_moe_in * hidden_one * rate_two, axis=0)
    grad_hidden_one = cotangent.astype(F32) + norm_back(
        grad_moe_in, hidden_one, rate_two, moe_gain, model_width
    )
    grad_branch = plain(grad_hidden_one.astype(BF16))
    grad_heads = sum_cols(
        split_parts(
            jnp.einsum("td,ckd->ctk", grad_branch, out_split, preferred_element_type=F32).astype(BF16)
        )
    ).astype(BF16)
    grad_down = jnp.zeros((cols, mine_count, part_units, col_width), F32)
    for mask in range(cols):
        grad_down = lax.dynamic_update_index_in_dim(
            grad_down, got_down[mask].astype(F32), col ^ mask, 0
        )
    grad_heads, out_partial, far_parts, grad_down = fence(
        grad_heads, out_partial, far_parts, grad_down
    )
    far_parts = [swap_cols(part, near + i) for i, part in enumerate(far_parts)]
    moe_result = lax.psum_scatter(out_partial, "chip", scatter_dimension=0, tiled=True)[0]
    grad_out_weight = lax.psum_scatter(
        by_head(
            jnp.einsum("ctk,td->ckd", heads_all, grad_branch, preferred_element_type=F32).astype(BF16)
        ),
        ROW,
        scatter_dimension=0,
        tiled=True,
    ).astype(F32)
    grad_projected, grad_gains = attend_backward(
        qkv, cosine, sine, seg_row, head_gains, grad_heads, logs
    )
    grad_gate_up = jnp.zeros((cols, mine_count, col_width, 2 * part_units), F32)
    for mask in range(near):
        grad_gate_up = lax.dynamic_update_index_in_dim(
            grad_gate_up, got_inner[mask].astype(F32), col ^ mask, 0
        )
    grad_projected, far_parts, moe_result, grad_gate_up = fence(
        grad_projected, far_parts, moe_result, grad_gate_up
    )
    output = (hidden_one + moe_result.astype(F32)).astype(BF16)
    normed_parts = [
        plain(
            jnp.einsum("gtk,gdk->td", grad_projected, weight, preferred_element_type=F32).astype(BF16)
        )
        for weight, _ in qkv_halves
    ]
    if groups > 1:
        mine_first = jnp.concatenate(normed_parts, axis=1)
        mine_last = jnp.concatenate(normed_parts[::-1], axis=1)
        normed_parts = jnp.where(core == 0, mine_first, mine_last)
    else:
        normed_parts = normed_parts[0]
    normed_parts, grad_projected, far_parts = fence(normed_parts, grad_projected, far_parts)
    grad_normed = sum_cols(
        [
            lax.dynamic_slice_in_dim(normed_parts, (col ^ mask) * col_width, col_width, 1)
            for mask in range(cols)
        ]
    )
    grad_qkv = heads_out(
        plain(
            jnp.einsum(
                "td,gtk->gdk", normed_all, grad_projected, preferred_element_type=F32
            ).astype(BF16)
        ),
        3,
        ratio,
        heads_row,
    )

    scaled_grad = grad_normed * attn_gain
    gain_one = jnp.sum(grad_normed * stream * rate_one, axis=0)
    across = jnp.sum(scaled_grad * stream, axis=-1)
    small = width_total(jnp.concatenate([across, grad_gains.reshape(-1)]))
    across = small[:per_row, None]
    gains = sum_rows(jnp.concatenate([gain_one, gain_two, small[per_row:]]))
    grad_attn_gain = gains[:col_width]
    grad_moe_gain = gains[col_width : 2 * col_width]
    grad_query_gain = gains[2 * col_width : 2 * col_width + head_size]
    grad_key_gain = gains[2 * col_width + head_size :]
    grad_tokens = (
        grad_hidden_one
        + rate_one * scaled_grad
        - stream * rate_one * rate_one * rate_one * across / model_width
    ).astype(BF16)

    for mask in range(near, cols):
        grad_gate_up = lax.dynamic_update_index_in_dim(
            grad_gate_up, far_parts[mask - near].astype(F32), col ^ mask, 0
        )
    grad_gate_up = (
        grad_gate_up.reshape(experts_here, split, col_width, 2, part_units)
        .transpose(0, 2, 3, 1, 4)
        .reshape(experts_here, col_width, double_units)
    )
    grad_down = grad_down.reshape(experts_here, units, col_width)
    return (
        output,
        grad_tokens,
        grad_attn_gain,
        grad_qkv,
        grad_query_gain,
        grad_key_gain,
        grad_out_weight,
        grad_moe_gain,
        grad_gate_up,
        grad_down,
    )


def solution(mesh):
    rows, cols = mesh.devices.shape
    fine = Mesh(mesh.devices.reshape(rows // 2, 2, cols), ("chip", "core", "col"))
    return jax.shard_map(
        local,
        mesh=fine,
        in_specs=(
            P(ROW, "col"),
            P("col"),
            P(None, "col", ROW),
            P(),
            P(),
            P(ROW, "col"),
            P("col"),
            P(ROW, "col", None),
            P(ROW, None, "col"),
            P("col", None),
            P(),
            P(),
            P(ROW, "col"),
        ),
        out_specs=(
            P(ROW, "col"),
            P(ROW, "col"),
            P("col"),
            P(None, "col", ROW),
            P(),
            P(),
            P(ROW, "col"),
            P("col"),
            P(ROW, "col", None),
            P(ROW, None, "col"),
        ),
        check_vma=False,
    )
```

```python
from functools import partial

import jax
import jax.numpy as jnp
from jax import lax
from jax.experimental import pallas as pl
from jax.experimental.layout import Layout, with_layout_constraint
from jax.experimental.pallas import tpu as pltpu
from jax.sharding import Mesh, PartitionSpec as P

DOCS = 4
epsilon = 1e-06
rope_base = 10000.0
neg_large = -1e30

ROW = ("chip", "core")
ALL = ("chip", "core", "col")
TILE = 256
BLOCK = 512
VMEM_BYTES = 58 * 1024 * 1024
F32 = jnp.float32
BF16 = jnp.bfloat16


def rope_tables(seg_row, head_size):
    docs = jnp.arange(DOCS, dtype=jnp.int32)
    starts = jnp.sum((seg_row[:, None] < docs[None, :]).astype(jnp.int32), axis=0)
    first_index = jnp.sum(
        jnp.where(seg_row[:, None] == docs[None, :], starts[None, :], 0), axis=-1
    )
    places = (jnp.arange(seg_row.shape[0], dtype=jnp.int32) - first_index).astype(F32)
    rates = rope_base ** (-jnp.arange(0, head_size, 2, dtype=F32) / head_size)
    angles = places[..., None] * rates
    angles = jnp.concatenate([angles, angles], axis=-1)
    return (jnp.cos(angles), jnp.sin(angles))


def width_total(values):
    return lax.psum(values, "col")


def norm_back(grad_normed, stream, rate, gain, model_width):
    scaled_grad = grad_normed * gain
    across = width_total(jnp.sum(scaled_grad * stream, axis=-1))[:, None]
    return rate * scaled_grad - stream * rate * rate * rate * across / model_width


def half_turn(values, sign):
    lane = lax.broadcasted_iota(jnp.int32, values.shape, 1)
    half = values.shape[1] // 2
    return jnp.where(lane < half, sign, -sign) * pltpu.roll(values, half, 1)


def head_norm(raw, gain, cosine, sine):
    rate = lax.rsqrt(jnp.mean(raw * raw, axis=-1, keepdims=True) + epsilon)
    normed = raw * rate
    gained = normed * gain
    return normed, rate, (gained * cosine + half_turn(gained, -1.0) * sine).astype(BF16)


def masked_scores(query, key, seg_col, seg_row, factor):
    scores = lax.dot_general(
        query, key, (((1,), (1,)), ((), ())), preferred_element_type=F32
    ) * factor
    return jnp.where(seg_col == seg_row, scores, neg_large)


def attend_kernel(
    factor, query_ref, key_ref, value_ref, cos_ref, sin_ref, row_ref, col_ref, gains_ref,
    out_ref, log_ref, low_ref,
):
    cosine, sine = cos_ref[...], sin_ref[...]
    low_ref[...] = head_norm(query_ref[...], gains_ref[0:1], cosine, sine)[2]
    key = head_norm(key_ref[...], gains_ref[1:2], cosine, sine)[2]
    value = value_ref[...].astype(BF16)
    seg_row = row_ref[...]

    def body(i, carry):
        rows = pl.ds(pl.multiple_of(i * TILE, TILE), TILE)
        scores = masked_scores(low_ref[rows], key, col_ref[rows], seg_row, factor)
        top = jnp.max(scores, axis=-1, keepdims=True)
        log_total = top + jnp.log(jnp.sum(jnp.exp(scores - top), axis=-1, keepdims=True))
        probs = jnp.exp(scores - log_total).astype(BF16)
        out_ref[rows] = jnp.dot(probs, value, preferred_element_type=F32).astype(BF16)
        log_ref[rows] = jnp.broadcast_to(log_total, (TILE, log_ref.shape[1]))
        return carry

    lax.fori_loop(0, query_ref.shape[0] // TILE, body, 0)


def attend_specs(tokens, size, each):
    def part(k):
        return pl.BlockSpec((None, tokens, size), lambda h: (h // each, 0, k * each + h % each))

    whole = [
        pl.BlockSpec(shape, lambda h: (0, 0))
        for shape in ((tokens, size), (tokens, size), (1, tokens), (tokens, 1), (2, size))
    ]
    return [part(0), part(1), part(2)], whole


def attend_forward(qkv, cosine, sine, seg_row, gains):
    tokens, size = cosine.shape
    each = qkv.shape[2] // (3 * size)
    heads = qkv.shape[0] * each
    parts, whole = attend_specs(tokens, size, each)
    by_head = pl.BlockSpec((tokens, size), lambda h: (0, h))
    return pl.pallas_call(
        partial(attend_kernel, size ** (-0.5)),
        grid=(heads,),
        in_specs=parts + whole,
        out_specs=[by_head, by_head],
        out_shape=[
            jax.ShapeDtypeStruct((tokens, heads * size), BF16),
            jax.ShapeDtypeStruct((tokens, heads * size), F32),
        ],
        scratch_shapes=[pltpu.VMEM((tokens, size), BF16)],
        compiler_params=pltpu.CompilerParams(vmem_limit_bytes=VMEM_BYTES),
        cost_estimate=pl.CostEstimate(
            flops=4 * heads * tokens * tokens * size,
            bytes_accessed=qkv.size * 4 + tokens * heads * size * 6,
            transcendentals=2 * heads * tokens * tokens,
        ),
        name="attend_forward",
    )(qkv, qkv, qkv, cosine, sine, seg_row[None, :], seg_row[:, None], gains)


def attend_back_kernel(
    factor, each, query_ref, key_ref, value_ref, cos_ref, sin_ref, row_ref, col_ref, gains_ref,
    grad_ref, log_ref, out_ref, gain_ref, low_ref, query_grad, key_grad, value_grad,
):
    head = pl.program_id(0)
    group, place = head // each, head % each
    cosine, sine = cos_ref[...], sin_ref[...]
    gains = gains_ref[...]
    low_ref[...] = head_norm(query_ref[...], gains[0:1], cosine, sine)[2]
    key = head_norm(key_ref[...], gains[1:2], cosine, sine)[2]
    value = value_ref[...].astype(BF16)
    seg_row = row_ref[...]
    size = value.shape[1]
    key_grad[...] = jnp.zeros_like(key_grad)
    value_grad[...] = jnp.zeros_like(value_grad)

    def body(i, carry):
        rows = pl.ds(pl.multiple_of(i * TILE, TILE), TILE)
        query = low_ref[rows]
        grad_out = grad_ref[rows]
        scores = masked_scores(query, key, col_ref[rows], seg_row, factor)
        probs = jnp.exp(scores - log_ref[rows][:, :1])
        grad_probs = lax.dot_general(
            grad_out, value, (((1,), (1,)), ((), ())), preferred_element_type=F32
        )
        weighted = probs * grad_probs
        center = jnp.sum(weighted, axis=-1, keepdims=True)
        grad_scores = (weighted - probs * center).astype(BF16)
        query_grad[rows] = jnp.dot(grad_scores, key, preferred_element_type=F32) * factor
        first = (((0,), (0,)), ((), ()))
        key_grad[...] += lax.dot_general(grad_scores, query, first, preferred_element_type=F32)
        value_grad[...] += lax.dot_general(
            probs.astype(BF16), grad_out, first, preferred_element_type=F32
        )
        return carry

    lax.fori_loop(0, query_ref.shape[0] // TILE, body, 0)

    @pl.when(head == 0)
    def _():
        gain_ref[...] = jnp.zeros_like(gain_ref)

    for k, (raw_ref, grad) in enumerate(
        ((query_ref, query_grad[...]), (key_ref, key_grad[...] * factor))
    ):
        raw = raw_ref[...]
        rate = lax.rsqrt(jnp.mean(raw * raw, axis=-1, keepdims=True) + epsilon)
        normed = raw * rate
        grad_normed = grad * cosine + half_turn(grad * sine, 1.0)
        gain_ref[k : k + 1] += jnp.sum(grad_normed * normed, axis=0, keepdims=True)
        scaled = grad_normed * gains[k : k + 1]
        raw_grad = rate * (
            scaled - normed * jnp.mean(scaled * normed, axis=-1, keepdims=True)
        )
        columns = pl.ds(pl.multiple_of((k * each + place) * size, size), size)
        out_ref[group, :, columns] = raw_grad.astype(BF16)
    columns = pl.ds(pl.multiple_of((2 * each + place) * size, size), size)
    out_ref[group, :, columns] = value_grad[...].astype(BF16)


def attend_backward(qkv, cosine, sine, seg_row, gains, grad_heads, logs):
    tokens, size = cosine.shape
    each = qkv.shape[2] // (3 * size)
    heads = qkv.shape[0] * each
    parts, whole = attend_specs(tokens, size, each)
    by_head = pl.BlockSpec((tokens, size), lambda h: (0, h))
    return pl.pallas_call(
        partial(attend_back_kernel, size ** (-0.5), each),
        grid=(heads,),
        in_specs=parts + whole + [by_head, by_head],
        out_specs=[
            pl.BlockSpec(qkv.shape, lambda h: (0, 0, 0)),
            pl.BlockSpec((2, size), lambda h: (0, 0)),
        ],
        out_shape=[
            jax.ShapeDtypeStruct(qkv.shape, BF16),
            jax.ShapeDtypeStruct((2, size), F32),
        ],
        scratch_shapes=[
            pltpu.VMEM((tokens, size), BF16),
            pltpu.VMEM((tokens, size), F32),
            pltpu.VMEM((tokens, size), F32),
            pltpu.VMEM((tokens, size), F32),
        ],
        compiler_params=pltpu.CompilerParams(vmem_limit_bytes=VMEM_BYTES),
        cost_estimate=pl.CostEstimate(
            flops=10 * heads * tokens * tokens * size,
            bytes_accessed=qkv.size * 6 + tokens * heads * size * 6,
            transcendentals=heads * tokens * tokens,
        ),
        name="attend_backward",
    )(qkv, qkv, qkv, cosine, sine, seg_row[None, :], seg_row[:, None], gains, grad_heads, logs)


def slot_places(routes, route_gates, expert_ids):
    chosen = routes[None] == expert_ids[:, None, None]
    hit = jnp.any(chosen, axis=-1)
    gate = jnp.sum(jnp.where(chosen, route_gates[None], 0.0), axis=-1)
    count, tok_total = hit.shape
    grouped = hit.astype(BF16).reshape(count, tok_total // 128, 128)
    lane = jnp.arange(128)
    before = (lane[:, None] < lane[None, :]).astype(BF16)
    inside = jnp.einsum("egt,tu->egu", grouped, before, preferred_element_type=F32)
    totals = jnp.sum(grouped.astype(F32), axis=-1).astype(BF16)
    group = jnp.arange(tok_total // 128)
    earlier = (group[:, None] < group[None, :]).astype(BF16)
    offset = jnp.einsum("eg,gh->eh", totals, earlier, preferred_element_type=F32)
    place = (inside + offset[..., None]).reshape(count, tok_total).astype(jnp.int32)
    per_block = jnp.sum(hit.astype(jnp.int32).reshape(count, tok_total // BLOCK, BLOCK), axis=-1)
    begin = place.reshape(count, tok_total // BLOCK, BLOCK)[:, :, 0]
    end = begin + per_block
    low = begin // TILE
    high = jnp.where(end > begin, (end + TILE - 1) // TILE, low)
    return (jnp.where(hit, place, -1), gate, low, high)


def gather_kernel(scaled, each, low_ref, high_ref, *refs):
    rows_refs, place_refs, gate_refs, slots_ref = refs[0:2], refs[2:4], refs[4:6], refs[6]
    chip, piece = pl.program_id(0), pl.program_id(1)
    experts = slots_ref.shape[0]

    @pl.when((chip == 0) & (piece == 0))
    def _():
        slots_ref[...] = jnp.zeros_like(slots_ref)

    for k in range(2):
        rows_ref = rows_refs[k]
        parts, width = rows_ref.shape[1], rows_ref.shape[3]
        block = (2 * chip + k) * each + piece
        for e in range(experts):
            place = place_refs[k][e, 0]
            gate = gate_refs[k][e, 0]

            def body(i, carry):
                base = pl.multiple_of(i * TILE, TILE)
                wanted = lax.broadcasted_iota(jnp.int32, (TILE, BLOCK), 0) + base
                mask = place == wanted
                onehot = mask.astype(F32).astype(BF16)
                if scaled:
                    factor = jnp.sum(jnp.where(mask, gate, 0.0), axis=1, keepdims=True)
                for c in range(parts):
                    picked = jnp.dot(onehot, rows_ref[0, c], preferred_element_type=F32)
                    if scaled:
                        picked = picked * factor
                    where = (e, pl.ds(base, TILE), slice(c * width, (c + 1) * width))
                    slots_ref[where] = slots_ref[where] + picked.astype(BF16)
                return carry

            lax.fori_loop(low_ref[e, block], high_ref[e, block], body, 0)


def gather_slots(rows, place, gate, low, high, capacity, scaled):
    row_count, parts, per_row, width = rows.shape
    experts, tok_total = place.shape
    blocks = tok_total // BLOCK
    each = per_row // BLOCK

    def row_spec(k):
        return pl.BlockSpec(
            (1, parts, BLOCK, width),
            lambda z, j, *_: (2 * z + k, 0, j, 0),
        )

    def token_spec(k):
        return pl.BlockSpec(
            (experts, 1, 1, BLOCK),
            lambda z, j, *_: (0, (2 * z + k) * each + j, 0, 0),
        )

    places = place.reshape(experts, blocks, 1, BLOCK)
    gates = gate.reshape(experts, blocks, 1, BLOCK)
    return pl.pallas_call(
        partial(gather_kernel, scaled, each),
        grid_spec=pltpu.PrefetchScalarGridSpec(
            num_scalar_prefetch=2,
            grid=(row_count // 2, each),
            in_specs=[
                row_spec(0), row_spec(1), token_spec(0), token_spec(1), token_spec(0), token_spec(1),
            ],
            out_specs=pl.BlockSpec((experts, capacity, parts * width), lambda *_: (0, 0, 0)),
        ),
        out_shape=jax.ShapeDtypeStruct((experts, capacity, parts * width), BF16),
        compiler_params=pltpu.CompilerParams(vmem_limit_bytes=VMEM_BYTES),
        cost_estimate=pl.CostEstimate(
            flops=2 * 24 * experts * TILE * BLOCK * parts * width,
            bytes_accessed=(tok_total + experts * capacity) * parts * width * 2,
            transcendentals=0,
        ),
        name="gather_slots",
    )(low, high, rows, rows, places, places, gates, gates)


def combine_kernel(scaled, each, low_ref, high_ref, core_ref, slots_ref, place_ref, gate_ref, *refs):
    out_ref, total_ref = refs[-2:]
    chip, piece = pl.program_id(0), pl.program_id(1)
    block = (2 * chip + core_ref[0]) * each + piece
    experts = slots_ref.shape[0]
    parts, width = out_ref.shape[0], out_ref.shape[3]
    total_ref[...] = jnp.zeros_like(total_ref)
    for e in range(experts):
        place = jnp.broadcast_to(place_ref[e, 0].astype(F32), (8, BLOCK)).T[:, :1]
        if scaled:
            gate = jnp.broadcast_to(gate_ref[e, 0], (8, BLOCK)).T[:, :1]

        def body(i, carry):
            base = pl.multiple_of(i * TILE, TILE)
            wanted = lax.broadcasted_iota(jnp.int32, (BLOCK, TILE), 1) + base
            onehot = (place == wanted.astype(F32)).astype(F32).astype(BF16)
            for c in range(parts):
                columns = slice(c * width, (c + 1) * width)
                picked = jnp.dot(
                    onehot, slots_ref[e, pl.ds(base, TILE), columns], preferred_element_type=F32
                )
                if scaled:
                    picked = picked * gate
                total_ref[:, columns] = total_ref[:, columns] + picked
            return carry

        lax.fori_loop(low_ref[e, block], high_ref[e, block], body, 0)
    for c in range(parts):
        total = total_ref[:, c * width : (c + 1) * width]
        if len(refs) == 3:
            total = total + refs[0][c, 0].astype(F32)
        out_ref[c, 0] = total.astype(BF16)


def combine_slots(slots, place, gate, low, high, core, chips, per_row, parts, scaled, more=()):
    experts, capacity, model_width = slots.shape
    width = model_width // parts
    each = per_row // BLOCK
    blocks = place.shape[1] // BLOCK

    def token_block(z, j, low_ref, high_ref, core_ref):
        return (0, (2 * z + core_ref[0]) * each + j, 0, 0)

    sums = pl.BlockSpec((parts, 1, BLOCK, width), lambda z, j, *_: (0, z, j, 0))
    return pl.pallas_call(
        partial(combine_kernel, scaled, each),
        grid_spec=pltpu.PrefetchScalarGridSpec(
            num_scalar_prefetch=3,
            grid=(chips, each),
            in_specs=[
                pl.BlockSpec(
                    (experts, capacity, model_width),
                    lambda *_: (0, 0, 0),
                    pipeline_mode=pl.Buffered(1),
                ),
                pl.BlockSpec((experts, 1, 1, BLOCK), token_block),
                pl.BlockSpec((experts, 1, 1, BLOCK), token_block),
            ]
            + [sums] * len(more),
            out_specs=sums,
            scratch_shapes=[pltpu.VMEM((BLOCK, model_width), F32)],
        ),
        out_shape=jax.ShapeDtypeStruct((parts, chips, per_row, width), BF16),
        compiler_params=pltpu.CompilerParams(vmem_limit_bytes=VMEM_BYTES),
        cost_estimate=pl.CostEstimate(
            flops=24 * experts * TILE * BLOCK * model_width,
            bytes_accessed=slots.size * 2 + parts * chips * per_row * width * 2,
            transcendentals=0,
        ),
        name="combine_slots",
    )(
        low,
        high,
        core,
        slots,
        place.reshape(experts, blocks, 1, BLOCK),
        gate.reshape(experts, blocks, 1, BLOCK),
        *more,
    )


def swap_cores(values):
    return lax.ppermute(values, "core", [(0, 1), (1, 0)])


def swap_cols(values, mask):
    count = lax.axis_size("col")
    return lax.ppermute(values, "col", [(i, i ^ mask) for i in range(count)])


def fence(*values):
    return lax.optimization_barrier(values)


def plain(values):
    return with_layout_constraint(values, Layout(tuple(range(values.ndim))))


def gather_cols(values):
    count = lax.axis_size("col")
    me = lax.axis_index("col")
    result = jnp.zeros((count,) + values.shape, values.dtype)
    for mask in range(count):
        piece = swap_cols(values, mask) if mask else values
        result = lax.dynamic_update_index_in_dim(result, piece, me ^ mask, 0)
    return result


def sum_cols(pieces):
    total = 0.0
    for piece in send_parts(pieces):
        total = total + piece.astype(F32)
    return total


def split_parts(parts):
    me = lax.axis_index("col")
    return [
        plain(lax.dynamic_index_in_dim(parts, me ^ mask, 0, keepdims=False))
        for mask in range(lax.axis_size("col"))
    ]


def send_parts(pieces):
    return pieces[:1] + [swap_cols(pieces[mask], mask) for mask in range(1, len(pieces))]


def join_parts(pieces, axis, result=None, offset=0):
    me = lax.axis_index("col")
    if result is None:
        shape = list(pieces[0].shape)
        shape[axis] *= len(pieces)
        result = jnp.zeros(shape, pieces[0].dtype)
    size = result.shape[axis] // len(pieces)
    for mask, piece in enumerate(pieces):
        start = (me ^ mask) * size + offset
        result = lax.dynamic_update_slice_in_dim(result, piece, start, axis)
    return result


def swap_chips(values, mask):
    count = lax.axis_size("chip")
    return lax.ppermute(values, "chip", [(i, i ^ mask) for i in range(count)])


def over_chips(values):
    chips = lax.axis_size("chip")
    chip = lax.axis_index("chip")
    same = jnp.zeros((chips,) + values.shape, values.dtype)
    for mask in range(chips):
        piece = swap_chips(values, mask) if mask else values
        same = lax.dynamic_update_index_in_dim(same, piece, chip ^ mask, 0)
    return same


def over_cores(same):
    core = lax.axis_index("core")
    other = swap_cores(same)
    both = jnp.stack([jnp.where(core == 0, same, other), jnp.where(core == 0, other, same)], axis=1)
    return both.reshape(-1, same.shape[-1])


def pick(pieces, index):
    chosen = pieces[0]
    for k in range(1, len(pieces)):
        chosen = jnp.where(index == k, pieces[k], chosen)
    return chosen


def own_heads(cols, heads_row):
    return 2 * heads_row == cols


def heads_in(weight, ratio, size):
    chips, cols = lax.axis_size("chip"), lax.axis_size("col")
    core, col = lax.axis_index("core"), lax.axis_index("col")
    rows = 2 * chips
    row = 2 * lax.axis_index("chip") + core
    kinds, features, width = weight.shape
    pieces = []
    if own_heads(cols, width // size):
        p = width // size
        for t in range(p):
            pairs = [
                (k * cols + c, c // p * cols + k * p + (t + c) % p)
                for k in range(2)
                for c in range(cols)
            ]
            piece = lax.dynamic_slice_in_dim(weight, (t + col) % p * size, size, 2)
            pieces.append(lax.ppermute(piece, ("core", "col"), pairs))
        pieces = [pick(pieces, (col - b) % p) for b in range(p)]
        return jnp.concatenate(
            [jnp.concatenate([p[a] for a in range(kinds)], axis=1) for p in pieces], axis=0
        )
    block = features // ratio
    for k in range(ratio):
        pairs = []
        for r in range(rows):
            for c in range(cols):
                h = (k + r) % ratio
                pairs.append((r * cols + c, (ratio * c + h) * cols + r // ratio))
        piece = lax.dynamic_slice_in_dim(weight, (k + row) % ratio * block, block, 1)
        pieces.append(lax.ppermute(piece, ALL, pairs))
    return jnp.concatenate(
        [pick([p[a] for p in pieces], (row - s) % ratio) for a in range(kinds) for s in range(ratio)],
        axis=1,
    )


def heads_out(grad, kinds, ratio, heads_row):
    chips, cols = lax.axis_size("chip"), lax.axis_size("col")
    col = lax.axis_index("col")
    rows = 2 * chips
    row = 2 * lax.axis_index("chip") + lax.axis_index("core")
    mine = grad.reshape(rows, -1, grad.shape[2])
    mine = lax.psum_scatter(mine, ROW, scatter_dimension=0, tiled=True)[0]
    block = mine.shape[0]
    pieces = []
    if own_heads(cols, heads_row):
        p = heads_row
        size = mine.shape[1] // kinds
        for t in range(p):
            pairs = [
                (k * cols + c, c // p * cols + k * p + (c - t) % p)
                for k in range(2)
                for c in range(cols)
            ]
            piece = lax.dynamic_slice_in_dim(mine, (col - t) % p * (block // p), block // p, 0)
            pieces.append(lax.ppermute(piece, ("core", "col"), pairs))
        pieces = [pick(pieces, (i - col) % p) for i in range(p)]
        return jnp.stack(
            [
                jnp.concatenate([q[:, a * size : (a + 1) * size] for q in pieces], axis=1)
                for a in range(kinds)
            ]
        ).astype(F32)
    width = mine.shape[1] // (kinds * ratio)
    for k in range(ratio):
        pairs = []
        for r in range(rows):
            for c in range(cols):
                s = (r - k) % ratio
                pairs.append((r * cols + c, (ratio * c + s) * cols + r // ratio))
        start = (row - k) % ratio * width
        piece = jnp.stack(
            [
                lax.dynamic_slice_in_dim(mine, a * ratio * width + start, width, 1)
                for a in range(kinds)
            ]
        )
        pieces.append(lax.ppermute(piece, ALL, pairs))
    return jnp.concatenate(
        [pick(pieces, (h - row) % ratio) for h in range(ratio)], axis=1
    ).astype(F32)


def sum_rows(values):
    total = values
    for axis in ROW:
        count = lax.axis_size(axis)
        step = 1
        while step < count:
            total = total + lax.ppermute(total, axis, [(i, i ^ step) for i in range(count)])
            step *= 2
    return total


def local(
    tokens,
    attn_gain,
    qkv_weight,
    query_gain,
    key_gain,
    out_weight,
    moe_gain,
    gate_up_weight,
    down_weight,
    segments,
    routes,
    route_gates,
    cotangent,
):
    cols = lax.axis_size("col")
    chips = lax.axis_size("chip")
    rows = 2 * chips
    col = lax.axis_index("col")
    core = lax.axis_index("core")
    row = 2 * lax.axis_index("chip") + core
    per_row, col_width = tokens.shape
    model_width = col_width * cols
    head_size = query_gain.shape[0]
    ratio = rows // cols
    head_width = model_width // cols

    experts_here, _, double_units = gate_up_weight.shape
    units = double_units // 2
    split = max(1, cols // experts_here)
    mine_count = experts_here * split // cols
    part_units = units // split
    capacity = 2 * rows * per_row * routes.shape[1] // (experts_here * rows)

    gate_up_parts = (
        gate_up_weight.reshape(experts_here, col_width, 2, split, part_units)
        .transpose(0, 3, 1, 2, 4)
        .reshape(cols, mine_count, col_width, 2 * part_units)
    )
    down_parts = down_weight.reshape(cols, mine_count, part_units, col_width)

    heads_row = qkv_weight.shape[2] // head_size
    groups = chips if own_heads(cols, heads_row) else 1

    def by_col(values):
        if groups == 1:
            return values.reshape(cols, head_width, col_width)
        values = values.reshape(groups, cols, head_width // groups, col_width)
        return values.transpose(1, 0, 2, 3).reshape(cols, head_width, col_width)

    def by_head(values):
        if groups > 1:
            values = values.reshape(cols, groups, head_width // groups, col_width)
            values = values.transpose(1, 0, 2, 3)
        return values.reshape(model_width, col_width)

    tokens_all = gather_cols(tokens)
    small = gather_cols(jnp.concatenate([attn_gain, segments.astype(F32).reshape(-1)]))
    qkv_rows, small, tokens_all, out_in = fence(
        heads_in(qkv_weight, ratio, head_size), small, tokens_all, out_weight
    )
    gain_all = small[:, :col_width]
    segs = small[:, col_width:].astype(jnp.int32)
    cuts = (0, col_width // 2, 3 * col_width // 4, col_width)
    first, second, last = (
        split_parts(gate_up_parts[:, :, cuts[i] : cuts[i + 1]]) for i in range(3)
    )
    gate_up_first = send_parts(first)
    qkv_rows, out_rows, gate_up_first, second, last = fence(
        over_chips(qkv_rows), over_chips(out_in), gate_up_first, second, last
    )
    gate_up_second, gate_up_last = send_parts(second), send_parts(last)
    if groups > 1:
        half = model_width // 2
        qkv_halves = [(qkv_rows, core * half), (swap_cores(qkv_rows), (1 - core) * half)]
    else:
        half = model_width
        qkv_halves = [(over_cores(qkv_rows)[None], 0)]
    out_split = by_col(over_cores(out_rows))
    seg_row = lax.dynamic_index_in_dim(segs.reshape(rows, per_row), row, 0, keepdims=False)

    first = row * experts_here
    expert_ids = first + (col * mine_count + jnp.arange(mine_count, dtype=jnp.int32)) // split
    place, gate, low, high = slot_places(routes, route_gates, expert_ids)

    cosine, sine = rope_tables(seg_row, head_size)
    stream_all = tokens_all.astype(F32)
    rate_one = lax.rsqrt(jnp.sum(stream_all * stream_all, axis=(0, 2)) / model_width + epsilon)
    rate_one = rate_one[:, None]
    normed_all = jnp.concatenate(
        [(stream_all[c] * rate_one * gain_all[c]).astype(BF16) for c in range(cols)], axis=1
    )
    qkv = sum(
        jnp.einsum(
            "td,gdk->gtk",
            lax.dynamic_slice_in_dim(normed_all, begin, half, 1),
            weight,
            preferred_element_type=F32,
        )
        for weight, begin in qkv_halves
    )
    head_gains = jnp.stack([query_gain, key_gain])
    heads_low, logs = attend_forward(qkv, cosine, sine, seg_row, head_gains)
    heads_low, gate_up_second = fence(heads_low, gate_up_second)
    heads_all = gather_cols(heads_low)
    stream = tokens.astype(F32)
    hidden_one = plain(
        stream + jnp.einsum("ctk,ckd->td", heads_all, out_split, preferred_element_type=F32)
    )
    rate_two = lax.rsqrt(
        width_total(jnp.sum(hidden_one * hidden_one, axis=-1)) / model_width + epsilon
    )[:, None]
    moe_in = plain((hidden_one * rate_two * moe_gain).astype(BF16))
    moe_in, gate_up_last, down_first = fence(moe_in, gate_up_last, split_parts(down_parts))
    gate_up = jnp.zeros((mine_count, model_width, 2 * part_units), BF16)
    gate_up = join_parts(gate_up_first, 1, gate_up, 0)
    gate_up = join_parts(gate_up_second, 1, gate_up, cuts[1])
    gate_up = join_parts(gate_up_last, 1, gate_up, cuts[2])

    moe_all = lax.all_gather(moe_in, ALL, axis=0).reshape(rows, cols, per_row, col_width)
    mine = jnp.reshape(core, (1,))
    others = 1 - mine
    moe_all, down_first, cot_in, gate_up, place, gate, low, high = fence(
        moe_all, down_first, cotangent, gate_up, place, gate, low, high
    )
    cot_all = lax.all_gather(cot_in, ALL, axis=0).reshape(rows, cols, per_row, col_width)
    down = join_parts(send_parts(down_first), 2)
    slot_inputs = gather_slots(moe_all, place, gate, low, high, capacity, False)

    gate_weight = gate_up[..., :part_units]
    up_weight = gate_up[..., part_units:]
    gate_pre = jnp.einsum(
        "ecd,edf->ecf", slot_inputs, gate_weight, preferred_element_type=F32
    ).astype(BF16)
    up_pre = jnp.einsum(
        "ecd,edf->ecf", slot_inputs, up_weight, preferred_element_type=F32
    ).astype(BF16)
    gate_wide = gate_pre.astype(F32)
    up_wide = up_pre.astype(F32)
    sigmoid_gate = jax.nn.sigmoid(gate_wide)
    activated = gate_wide * sigmoid_gate
    hidden = (activated * up_wide).astype(BF16)
    hidden, down = fence(hidden, down)

    combine = partial(
        combine_slots, place=place, gate=gate, low=low, high=high,
        chips=chips, per_row=per_row, parts=cols,
    )

    def feature_block(values, index):
        return lax.dynamic_slice_in_dim(values, index * col_width, col_width, 2)

    expert_out = jnp.einsum("ecf,efd->ecd", hidden, down, preferred_element_type=F32).astype(BF16)
    out_other = swap_cores(combine(expert_out, core=others, scaled=True))
    out_partial = combine(expert_out, core=mine, scaled=True, more=(out_other,))
    out_partial, cot_all = fence(out_partial, cot_all)
    out_partial = plain(lax.psum_scatter(out_partial, "col", scatter_dimension=0, tiled=True)[0])

    grad_slot = gather_slots(cot_all, place, gate, low, high, capacity, True)
    down_grads = []
    for mask in range(cols):
        part = jnp.einsum(
            "ecf,ecd->efd", hidden, feature_block(grad_slot, col ^ mask),
            preferred_element_type=F32,
        )
        down_grads.append(part.astype(BF16) if mask else part)
    down_grads, grad_slot = fence(down_grads, grad_slot)
    got_down = send_parts(down_grads)
    grad_hidden = jnp.einsum("ecd,efd->ecf", grad_slot, down, preferred_element_type=F32)
    grad_gate_pre = (
        grad_hidden * up_wide * sigmoid_gate * (1.0 + gate_wide * (1.0 - sigmoid_gate))
    ).astype(BF16)
    grad_up_pre = (grad_hidden * activated).astype(BF16)
    grad_inner = jnp.concatenate([grad_gate_pre, grad_up_pre], axis=-1)

    grad_slot_in = jnp.einsum(
        "ecf,edf->ecd", grad_inner, gate_up, preferred_element_type=F32
    ).astype(BF16)
    grad_other = combine(grad_slot_in, core=others, scaled=False)
    near = cols // 2 + 1
    grad_other, grad_inner, near_down, out_partial = fence(
        grad_other, grad_inner, got_down[1:near], out_partial
    )
    got_down[1:near] = near_down
    grad_other = swap_cores(grad_other)
    inner_parts = []
    for mask in range(cols):
        part = jnp.einsum(
            "ecd,ecf->edf", feature_block(slot_inputs, col ^ mask), grad_inner,
            preferred_element_type=F32,
        )
        inner_parts.append(part.astype(BF16) if mask else part)
    grad_other, inner_parts[1] = fence(grad_other, inner_parts[1])
    grad_partial = combine(grad_slot_in, core=mine, scaled=False, more=(grad_other,))
    grad_partial, got_down = fence(grad_partial, got_down)
    grad_partial = plain(lax.psum_scatter(grad_partial, "col", scatter_dimension=0, tiled=True)[0])
    grad_partial, inner_parts, out_partial = fence(grad_partial, inner_parts, out_partial)
    grad_moe_in = plain(lax.psum_scatter(grad_partial, "chip", scatter_dimension=0, tiled=True)[0])
    far_parts = inner_parts[near:]
    got_inner = inner_parts[:1] + [swap_cols(inner_parts[mask], mask) for mask in range(1, near)]
    grad_moe_in, got_inner, out_partial, far_parts = fence(
        grad_moe_in, got_inner, out_partial, far_parts
    )
    grad_moe_in = grad_moe_in.astype(F32)

    gain_two = jnp.sum(grad_moe_in * hidden_one * rate_two, axis=0)
    grad_hidden_one = cotangent.astype(F32) + norm_back(
        grad_moe_in, hidden_one, rate_two, moe_gain, model_width
    )
    grad_branch = plain(grad_hidden_one.astype(BF16))
    grad_heads = sum_cols(
        split_parts(
            jnp.einsum("td,ckd->ctk", grad_branch, out_split, preferred_element_type=F32).astype(BF16)
        )
    ).astype(BF16)
    grad_down = jnp.zeros((cols, mine_count, part_units, col_width), F32)
    for mask in range(cols):
        grad_down = lax.dynamic_update_index_in_dim(
            grad_down, got_down[mask].astype(F32), col ^ mask, 0
        )
    grad_heads, out_partial, far_parts, grad_down = fence(
        grad_heads, out_partial, far_parts, grad_down
    )
    far_parts = [swap_cols(part, near + i) for i, part in enumerate(far_parts)]
    moe_result = lax.psum_scatter(out_partial, "chip", scatter_dimension=0, tiled=True)[0]
    grad_out_weight = lax.psum_scatter(
        by_head(
            jnp.einsum("ctk,td->ckd", heads_all, grad_branch, preferred_element_type=F32).astype(BF16)
        ),
        ROW,
        scatter_dimension=0,
        tiled=True,
    ).astype(F32)
    grad_projected, grad_gains = attend_backward(
        qkv, cosine, sine, seg_row, head_gains, grad_heads, logs
    )
    grad_gate_up = jnp.zeros((cols, mine_count, col_width, 2 * part_units), F32)
    for mask in range(near):
        grad_gate_up = lax.dynamic_update_index_in_dim(
            grad_gate_up, got_inner[mask].astype(F32), col ^ mask, 0
        )
    grad_projected, far_parts, moe_result, grad_gate_up = fence(
        grad_projected, far_parts, moe_result, grad_gate_up
    )
    output = (hidden_one + moe_result.astype(F32)).astype(BF16)
    normed_parts = [
        plain(
            jnp.einsum("gtk,gdk->td", grad_projected, weight, preferred_element_type=F32).astype(BF16)
        )
        for weight, _ in qkv_halves
    ]
    if groups > 1:
        mine_first = jnp.concatenate(normed_parts, axis=1)
        mine_last = jnp.concatenate(normed_parts[::-1], axis=1)
        normed_parts = jnp.where(core == 0, mine_first, mine_last)
    else:
        normed_parts = normed_parts[0]
    normed_parts, grad_projected, far_parts = fence(normed_parts, grad_projected, far_parts)
    grad_normed = sum_cols(
        [
            lax.dynamic_slice_in_dim(normed_parts, (col ^ mask) * col_width, col_width, 1)
            for mask in range(cols)
        ]
    )
    grad_qkv = heads_out(
        plain(
            jnp.einsum(
                "td,gtk->gdk", normed_all, grad_projected, preferred_element_type=F32
            ).astype(BF16)
        ),
        3,
        ratio,
        heads_row,
    )

    scaled_grad = grad_normed * attn_gain
    gain_one = jnp.sum(grad_normed * stream * rate_one, axis=0)
    across = jnp.sum(scaled_grad * stream, axis=-1)
    small = width_total(jnp.concatenate([across, grad_gains.reshape(-1)]))
    across = small[:per_row, None]
    gains = sum_rows(jnp.concatenate([gain_one, gain_two, small[per_row:]]))
    grad_attn_gain = gains[:col_width]
    grad_moe_gain = gains[col_width : 2 * col_width]
    grad_query_gain = gains[2 * col_width : 2 * col_width + head_size]
    grad_key_gain = gains[2 * col_width + head_size :]
    grad_tokens = (
        grad_hidden_one
        + rate_one * scaled_grad
        - stream * rate_one * rate_one * rate_one * across / model_width
    ).astype(BF16)

    for mask in range(near, cols):
        grad_gate_up = lax.dynamic_update_index_in_dim(
            grad_gate_up, far_parts[mask - near].astype(F32), col ^ mask, 0
        )
    grad_gate_up = (
        grad_gate_up.reshape(experts_here, split, col_width, 2, part_units)
        .transpose(0, 2, 3, 1, 4)
        .reshape(experts_here, col_width, double_units)
    )
    grad_down = grad_down.reshape(experts_here, units, col_width)
    return (
        output,
        grad_tokens,
        grad_attn_gain,
        grad_qkv,
        grad_query_gain,
        grad_key_gain,
        grad_out_weight,
        grad_moe_gain,
        grad_gate_up,
        grad_down,
    )


def solution(mesh):
    rows, cols = mesh.devices.shape
    fine = Mesh(mesh.devices.reshape(rows // 2, 2, cols), ("chip", "core", "col"))
    return jax.shard_map(
        local,
        mesh=fine,
        in_specs=(
            P(ROW, "col"),
            P("col"),
            P(None, "col", ROW),
            P(),
            P(),
            P(ROW, "col"),
            P("col"),
            P(ROW, "col", None),
            P(ROW, None, "col"),
            P("col", None),
            P(),
            P(),
            P(ROW, "col"),
        ),
        out_specs=(
            P(ROW, "col"),
            P(ROW, "col"),
            P("col"),
            P(None, "col", ROW),
            P(),
            P(),
            P(ROW, "col"),
            P("col"),
            P(ROW, "col", None),
            P(ROW, None, "col"),
        ),
        check_vma=False,
    )
```

```python
from functools import partial

import jax
import jax.numpy as jnp
from jax import lax
from jax.experimental import pallas as pl
from jax.experimental.layout import Layout, with_layout_constraint
from jax.experimental.pallas import tpu as pltpu
from jax.sharding import Mesh, PartitionSpec as P

DOCS = 4
epsilon = 1e-06
rope_base = 10000.0
neg_large = -1e30

ROW = ("chip", "core")
ALL = ("chip", "core", "col")
TILE = 256
BLOCK = 512
VMEM_BYTES = 58 * 1024 * 1024
F32 = jnp.float32
BF16 = jnp.bfloat16


def rope_tables(seg_row, head_size):
    docs = jnp.arange(DOCS, dtype=jnp.int32)
    starts = jnp.sum((seg_row[:, None] < docs[None, :]).astype(jnp.int32), axis=0)
    first_index = jnp.sum(
        jnp.where(seg_row[:, None] == docs[None, :], starts[None, :], 0), axis=-1
    )
    places = (jnp.arange(seg_row.shape[0], dtype=jnp.int32) - first_index).astype(F32)
    rates = rope_base ** (-jnp.arange(0, head_size, 2, dtype=F32) / head_size)
    angles = places[..., None] * rates
    angles = jnp.concatenate([angles, angles], axis=-1)
    return (jnp.cos(angles), jnp.sin(angles))


def width_total(values):
    return lax.psum(values, "col")


def norm_back(grad_normed, stream, rate, gain, model_width):
    scaled_grad = grad_normed * gain
    across = width_total(jnp.sum(scaled_grad * stream, axis=-1))[:, None]
    return rate * scaled_grad - stream * rate * rate * rate * across / model_width


def half_turn(values, sign):
    lane = lax.broadcasted_iota(jnp.int32, values.shape, 1)
    half = values.shape[1] // 2
    return jnp.where(lane < half, sign, -sign) * pltpu.roll(values, half, 1)


def head_norm(raw, gain, cosine, sine):
    rate = lax.rsqrt(jnp.mean(raw * raw, axis=-1, keepdims=True) + epsilon)
    normed = raw * rate
    gained = normed * gain
    return normed, rate, (gained * cosine + half_turn(gained, -1.0) * sine).astype(BF16)


def masked_scores(query, key, seg_col, seg_row, factor):
    scores = lax.dot_general(
        query, key, (((1,), (1,)), ((), ())), preferred_element_type=F32
    ) * factor
    return jnp.where(seg_col == seg_row, scores, neg_large)


def attend_kernel(
    factor, query_ref, key_ref, value_ref, cos_ref, sin_ref, row_ref, col_ref, gains_ref,
    out_ref, log_ref, low_ref,
):
    cosine, sine = cos_ref[...], sin_ref[...]
    low_ref[...] = head_norm(query_ref[...], gains_ref[0:1], cosine, sine)[2]
    key = head_norm(key_ref[...], gains_ref[1:2], cosine, sine)[2]
    value = value_ref[...].astype(BF16)
    seg_row = row_ref[...]

    def body(i, carry):
        rows = pl.ds(pl.multiple_of(i * TILE, TILE), TILE)
        scores = masked_scores(low_ref[rows], key, col_ref[rows], seg_row, factor)
        top = jnp.max(scores, axis=-1, keepdims=True)
        log_total = top + jnp.log(jnp.sum(jnp.exp(scores - top), axis=-1, keepdims=True))
        probs = jnp.exp(scores - log_total).astype(BF16)
        out_ref[rows] = jnp.dot(probs, value, preferred_element_type=F32).astype(BF16)
        log_ref[rows] = jnp.broadcast_to(log_total, (TILE, log_ref.shape[1]))
        return carry

    lax.fori_loop(0, query_ref.shape[0] // TILE, body, 0)


def attend_specs(tokens, size, each):
    def part(k):
        return pl.BlockSpec((None, tokens, size), lambda h: (h // each, 0, k * each + h % each))

    whole = [
        pl.BlockSpec(shape, lambda h: (0, 0))
        for shape in ((tokens, size), (tokens, size), (1, tokens), (tokens, 1), (2, size))
    ]
    return [part(0), part(1), part(2)], whole


def attend_forward(qkv, cosine, sine, seg_row, gains):
    tokens, size = cosine.shape
    each = qkv.shape[2] // (3 * size)
    heads = qkv.shape[0] * each
    parts, whole = attend_specs(tokens, size, each)
    by_head = pl.BlockSpec((tokens, size), lambda h: (0, h))
    return pl.pallas_call(
        partial(attend_kernel, size ** (-0.5)),
        grid=(heads,),
        in_specs=parts + whole,
        out_specs=[by_head, by_head],
        out_shape=[
            jax.ShapeDtypeStruct((tokens, heads * size), BF16),
            jax.ShapeDtypeStruct((tokens, heads * size), F32),
        ],
        scratch_shapes=[pltpu.VMEM((tokens, size), BF16)],
        compiler_params=pltpu.CompilerParams(vmem_limit_bytes=VMEM_BYTES),
        cost_estimate=pl.CostEstimate(
            flops=4 * heads * tokens * tokens * size,
            bytes_accessed=qkv.size * 4 + tokens * heads * size * 6,
            transcendentals=2 * heads * tokens * tokens,
        ),
        name="attend_forward",
    )(qkv, qkv, qkv, cosine, sine, seg_row[None, :], seg_row[:, None], gains)


def attend_back_kernel(
    factor, each, query_ref, key_ref, value_ref, cos_ref, sin_ref, row_ref, col_ref, gains_ref,
    grad_ref, log_ref, out_ref, gain_ref, low_ref, query_grad, key_grad, value_grad,
):
    head = pl.program_id(0)
    group, place = head // each, head % each
    cosine, sine = cos_ref[...], sin_ref[...]
    gains = gains_ref[...]
    low_ref[...] = head_norm(query_ref[...], gains[0:1], cosine, sine)[2]
    key = head_norm(key_ref[...], gains[1:2], cosine, sine)[2]
    value = value_ref[...].astype(BF16)
    seg_row = row_ref[...]
    size = value.shape[1]
    key_grad[...] = jnp.zeros_like(key_grad)
    value_grad[...] = jnp.zeros_like(value_grad)

    def body(i, carry):
        rows = pl.ds(pl.multiple_of(i * TILE, TILE), TILE)
        query = low_ref[rows]
        grad_out = grad_ref[rows]
        scores = masked_scores(query, key, col_ref[rows], seg_row, factor)
        probs = jnp.exp(scores - log_ref[rows][:, :1])
        grad_probs = lax.dot_general(
            grad_out, value, (((1,), (1,)), ((), ())), preferred_element_type=F32
        )
        weighted = probs * grad_probs
        center = jnp.sum(weighted, axis=-1, keepdims=True)
        grad_scores = (weighted - probs * center).astype(BF16)
        query_grad[rows] = jnp.dot(grad_scores, key, preferred_element_type=F32) * factor
        first = (((0,), (0,)), ((), ()))
        key_grad[...] += lax.dot_general(grad_scores, query, first, preferred_element_type=F32)
        value_grad[...] += lax.dot_general(
            probs.astype(BF16), grad_out, first, preferred_element_type=F32
        )
        return carry

    lax.fori_loop(0, query_ref.shape[0] // TILE, body, 0)

    @pl.when(head == 0)
    def _():
        gain_ref[...] = jnp.zeros_like(gain_ref)

    for k, (raw_ref, grad) in enumerate(
        ((query_ref, query_grad[...]), (key_ref, key_grad[...] * factor))
    ):
        raw = raw_ref[...]
        rate = lax.rsqrt(jnp.mean(raw * raw, axis=-1, keepdims=True) + epsilon)
        normed = raw * rate
        grad_normed = grad * cosine + half_turn(grad * sine, 1.0)
        gain_ref[k : k + 1] += jnp.sum(grad_normed * normed, axis=0, keepdims=True)
        scaled = grad_normed * gains[k : k + 1]
        raw_grad = rate * (
            scaled - normed * jnp.mean(scaled * normed, axis=-1, keepdims=True)
        )
        columns = pl.ds(pl.multiple_of((k * each + place) * size, size), size)
        out_ref[group, :, columns] = raw_grad.astype(BF16)
    columns = pl.ds(pl.multiple_of((2 * each + place) * size, size), size)
    out_ref[group, :, columns] = value_grad[...].astype(BF16)


def attend_backward(qkv, cosine, sine, seg_row, gains, grad_heads, logs):
    tokens, size = cosine.shape
    each = qkv.shape[2] // (3 * size)
    heads = qkv.shape[0] * each
    parts, whole = attend_specs(tokens, size, each)
    by_head = pl.BlockSpec((tokens, size), lambda h: (0, h))
    return pl.pallas_call(
        partial(attend_back_kernel, size ** (-0.5), each),
        grid=(heads,),
        in_specs=parts + whole + [by_head, by_head],
        out_specs=[
            pl.BlockSpec(qkv.shape, lambda h: (0, 0, 0)),
            pl.BlockSpec((2, size), lambda h: (0, 0)),
        ],
        out_shape=[
            jax.ShapeDtypeStruct(qkv.shape, BF16),
            jax.ShapeDtypeStruct((2, size), F32),
        ],
        scratch_shapes=[
            pltpu.VMEM((tokens, size), BF16),
            pltpu.VMEM((tokens, size), F32),
            pltpu.VMEM((tokens, size), F32),
            pltpu.VMEM((tokens, size), F32),
        ],
        compiler_params=pltpu.CompilerParams(vmem_limit_bytes=VMEM_BYTES),
        cost_estimate=pl.CostEstimate(
            flops=10 * heads * tokens * tokens * size,
            bytes_accessed=qkv.size * 6 + tokens * heads * size * 6,
            transcendentals=heads * tokens * tokens,
        ),
        name="attend_backward",
    )(qkv, qkv, qkv, cosine, sine, seg_row[None, :], seg_row[:, None], gains, grad_heads, logs)


def slot_places(routes, route_gates, expert_ids):
    chosen = routes[None] == expert_ids[:, None, None]
    hit = jnp.any(chosen, axis=-1)
    gate = jnp.sum(jnp.where(chosen, route_gates[None], 0.0), axis=-1)
    count, tok_total = hit.shape
    grouped = hit.astype(BF16).reshape(count, tok_total // 128, 128)
    lane = jnp.arange(128)
    before = (lane[:, None] < lane[None, :]).astype(BF16)
    inside = jnp.einsum("egt,tu->egu", grouped, before, preferred_element_type=F32)
    totals = jnp.sum(grouped.astype(F32), axis=-1).astype(BF16)
    group = jnp.arange(tok_total // 128)
    earlier = (group[:, None] < group[None, :]).astype(BF16)
    offset = jnp.einsum("eg,gh->eh", totals, earlier, preferred_element_type=F32)
    place = (inside + offset[..., None]).reshape(count, tok_total).astype(jnp.int32)
    per_block = jnp.sum(hit.astype(jnp.int32).reshape(count, tok_total // BLOCK, BLOCK), axis=-1)
    begin = place.reshape(count, tok_total // BLOCK, BLOCK)[:, :, 0]
    end = begin + per_block
    low = begin // TILE
    high = jnp.where(end > begin, (end + TILE - 1) // TILE, low)
    return (jnp.where(hit, place, -1), gate, low, high)


def gather_kernel(scaled, each, low_ref, high_ref, *refs):
    rows_refs, place_refs, gate_refs, slots_ref = refs[0:2], refs[2:4], refs[4:6], refs[6]
    chip, piece = pl.program_id(0), pl.program_id(1)
    experts = slots_ref.shape[0]

    @pl.when((chip == 0) & (piece == 0))
    def _():
        slots_ref[...] = jnp.zeros_like(slots_ref)

    for k in range(2):
        rows_ref = rows_refs[k]
        parts, width = rows_ref.shape[1], rows_ref.shape[3]
        block = (2 * chip + k) * each + piece
        for e in range(experts):
            place = place_refs[k][e, 0]
            gate = gate_refs[k][e, 0]

            def body(i, carry):
                base = pl.multiple_of(i * TILE, TILE)
                wanted = lax.broadcasted_iota(jnp.int32, (TILE, BLOCK), 0) + base
                mask = place == wanted
                onehot = mask.astype(F32).astype(BF16)
                if scaled:
                    factor = jnp.sum(jnp.where(mask, gate, 0.0), axis=1, keepdims=True)
                for c in range(parts):
                    picked = jnp.dot(onehot, rows_ref[0, c], preferred_element_type=F32)
                    if scaled:
                        picked = picked * factor
                    where = (e, pl.ds(base, TILE), slice(c * width, (c + 1) * width))
                    slots_ref[where] = slots_ref[where] + picked.astype(BF16)
                return carry

            lax.fori_loop(low_ref[e, block], high_ref[e, block], body, 0)


def gather_slots(rows, place, gate, low, high, capacity, scaled):
    row_count, parts, per_row, width = rows.shape
    experts, tok_total = place.shape
    blocks = tok_total // BLOCK
    each = per_row // BLOCK

    def row_spec(k):
        return pl.BlockSpec(
            (1, parts, BLOCK, width),
            lambda z, j, *_: (2 * z + k, 0, j, 0),
        )

    def token_spec(k):
        return pl.BlockSpec(
            (experts, 1, 1, BLOCK),
            lambda z, j, *_: (0, (2 * z + k) * each + j, 0, 0),
        )

    places = place.reshape(experts, blocks, 1, BLOCK)
    gates = gate.reshape(experts, blocks, 1, BLOCK)
    return pl.pallas_call(
        partial(gather_kernel, scaled, each),
        grid_spec=pltpu.PrefetchScalarGridSpec(
            num_scalar_prefetch=2,
            grid=(row_count // 2, each),
            in_specs=[
                row_spec(0), row_spec(1), token_spec(0), token_spec(1), token_spec(0), token_spec(1),
            ],
            out_specs=pl.BlockSpec((experts, capacity, parts * width), lambda *_: (0, 0, 0)),
        ),
        out_shape=jax.ShapeDtypeStruct((experts, capacity, parts * width), BF16),
        compiler_params=pltpu.CompilerParams(vmem_limit_bytes=VMEM_BYTES),
        cost_estimate=pl.CostEstimate(
            flops=2 * 24 * experts * TILE * BLOCK * parts * width,
            bytes_accessed=(tok_total + experts * capacity) * parts * width * 2,
            transcendentals=0,
        ),
        name="gather_slots",
    )(low, high, rows, rows, places, places, gates, gates)


def combine_kernel(scaled, each, low_ref, high_ref, core_ref, slots_ref, place_ref, gate_ref, *refs):
    out_ref, total_ref = refs[-2:]
    chip, piece = pl.program_id(0), pl.program_id(1)
    block = (2 * chip + core_ref[0]) * each + piece
    experts = slots_ref.shape[0]
    parts, width = out_ref.shape[0], out_ref.shape[3]
    total_ref[...] = jnp.zeros_like(total_ref)
    for e in range(experts):
        place = jnp.broadcast_to(place_ref[e, 0].astype(F32), (8, BLOCK)).T[:, :1]
        if scaled:
            gate = jnp.broadcast_to(gate_ref[e, 0], (8, BLOCK)).T[:, :1]

        def body(i, carry):
            base = pl.multiple_of(i * TILE, TILE)
            wanted = lax.broadcasted_iota(jnp.int32, (BLOCK, TILE), 1) + base
            onehot = (place == wanted.astype(F32)).astype(F32).astype(BF16)
            for c in range(parts):
                columns = slice(c * width, (c + 1) * width)
                picked = jnp.dot(
                    onehot, slots_ref[e, pl.ds(base, TILE), columns], preferred_element_type=F32
                )
                if scaled:
                    picked = picked * gate
                total_ref[:, columns] = total_ref[:, columns] + picked
            return carry

        lax.fori_loop(low_ref[e, block], high_ref[e, block], body, 0)
    for c in range(parts):
        total = total_ref[:, c * width : (c + 1) * width]
        if len(refs) == 3:
            total = total + refs[0][c, 0].astype(F32)
        out_ref[c, 0] = total.astype(BF16)


def combine_slots(slots, place, gate, low, high, core, chips, per_row, parts, scaled, more=()):
    experts, capacity, model_width = slots.shape
    width = model_width // parts
    each = per_row // BLOCK
    blocks = place.shape[1] // BLOCK

    def token_block(z, j, low_ref, high_ref, core_ref):
        return (0, (2 * z + core_ref[0]) * each + j, 0, 0)

    sums = pl.BlockSpec((parts, 1, BLOCK, width), lambda z, j, *_: (0, z, j, 0))
    return pl.pallas_call(
        partial(combine_kernel, scaled, each),
        grid_spec=pltpu.PrefetchScalarGridSpec(
            num_scalar_prefetch=3,
            grid=(chips, each),
            in_specs=[
                pl.BlockSpec(
                    (experts, capacity, model_width),
                    lambda *_: (0, 0, 0),
                    pipeline_mode=pl.Buffered(1),
                ),
                pl.BlockSpec((experts, 1, 1, BLOCK), token_block),
                pl.BlockSpec((experts, 1, 1, BLOCK), token_block),
            ]
            + [sums] * len(more),
            out_specs=sums,
            scratch_shapes=[pltpu.VMEM((BLOCK, model_width), F32)],
        ),
        out_shape=jax.ShapeDtypeStruct((parts, chips, per_row, width), BF16),
        compiler_params=pltpu.CompilerParams(vmem_limit_bytes=VMEM_BYTES),
        cost_estimate=pl.CostEstimate(
            flops=24 * experts * TILE * BLOCK * model_width,
            bytes_accessed=slots.size * 2 + parts * chips * per_row * width * 2,
            transcendentals=0,
        ),
        name="combine_slots",
    )(
        low,
        high,
        core,
        slots,
        place.reshape(experts, blocks, 1, BLOCK),
        gate.reshape(experts, blocks, 1, BLOCK),
        *more,
    )


def swap_cores(values):
    return lax.ppermute(values, "core", [(0, 1), (1, 0)])


def swap_cols(values, mask):
    count = lax.axis_size("col")
    return lax.ppermute(values, "col", [(i, i ^ mask) for i in range(count)])


def fence(*values):
    return lax.optimization_barrier(values)


def plain(values):
    return with_layout_constraint(values, Layout(tuple(range(values.ndim))))


def gather_cols(values):
    count = lax.axis_size("col")
    me = lax.axis_index("col")
    result = jnp.zeros((count,) + values.shape, values.dtype)
    for mask in range(count):
        piece = swap_cols(values, mask) if mask else values
        result = lax.dynamic_update_index_in_dim(result, piece, me ^ mask, 0)
    return result


def sum_cols(pieces):
    total = 0.0
    for piece in send_parts(pieces):
        total = total + piece.astype(F32)
    return total


def split_parts(parts):
    me = lax.axis_index("col")
    return [
        plain(lax.dynamic_index_in_dim(parts, me ^ mask, 0, keepdims=False))
        for mask in range(lax.axis_size("col"))
    ]


def send_parts(pieces):
    return pieces[:1] + [swap_cols(pieces[mask], mask) for mask in range(1, len(pieces))]


def join_parts(pieces, axis, result=None, offset=0):
    me = lax.axis_index("col")
    if result is None:
        shape = list(pieces[0].shape)
        shape[axis] *= len(pieces)
        result = jnp.zeros(shape, pieces[0].dtype)
    size = result.shape[axis] // len(pieces)
    for mask, piece in enumerate(pieces):
        start = (me ^ mask) * size + offset
        result = lax.dynamic_update_slice_in_dim(result, piece, start, axis)
    return result


def swap_chips(values, mask):
    count = lax.axis_size("chip")
    return lax.ppermute(values, "chip", [(i, i ^ mask) for i in range(count)])


def over_chips(values):
    chips = lax.axis_size("chip")
    chip = lax.axis_index("chip")
    same = jnp.zeros((chips,) + values.shape, values.dtype)
    for mask in range(chips):
        piece = swap_chips(values, mask) if mask else values
        same = lax.dynamic_update_index_in_dim(same, piece, chip ^ mask, 0)
    return same


def over_cores(same):
    core = lax.axis_index("core")
    other = swap_cores(same)
    both = jnp.stack([jnp.where(core == 0, same, other), jnp.where(core == 0, other, same)], axis=1)
    return both.reshape(-1, same.shape[-1])


def pick(pieces, index):
    chosen = pieces[0]
    for k in range(1, len(pieces)):
        chosen = jnp.where(index == k, pieces[k], chosen)
    return chosen


def own_heads(cols, heads_row):
    return 2 * heads_row == cols


def heads_in(weight, ratio, size):
    chips, cols = lax.axis_size("chip"), lax.axis_size("col")
    core, col = lax.axis_index("core"), lax.axis_index("col")
    rows = 2 * chips
    row = 2 * lax.axis_index("chip") + core
    kinds, features, width = weight.shape
    pieces = []
    if own_heads(cols, width // size):
        p = width // size
        for t in range(p):
            pairs = [
                (k * cols + c, c // p * cols + k * p + (t + c) % p)
                for k in range(2)
                for c in range(cols)
            ]
            piece = lax.dynamic_slice_in_dim(weight, (t + col) % p * size, size, 2)
            pieces.append(lax.ppermute(piece, ("core", "col"), pairs))
        pieces = [pick(pieces, (col - b) % p) for b in range(p)]
        return jnp.concatenate(
            [jnp.concatenate([p[a] for a in range(kinds)], axis=1) for p in pieces], axis=0
        )
    block = features // ratio
    for k in range(ratio):
        pairs = []
        for r in range(rows):
            for c in range(cols):
                h = (k + r) % ratio
                pairs.append((r * cols + c, (ratio * c + h) * cols + r // ratio))
        piece = lax.dynamic_slice_in_dim(weight, (k + row) % ratio * block, block, 1)
        pieces.append(lax.ppermute(piece, ALL, pairs))
    return jnp.concatenate(
        [pick([p[a] for p in pieces], (row - s) % ratio) for a in range(kinds) for s in range(ratio)],
        axis=1,
    )


def heads_out(grad, kinds, ratio, heads_row):
    chips, cols = lax.axis_size("chip"), lax.axis_size("col")
    col = lax.axis_index("col")
    rows = 2 * chips
    row = 2 * lax.axis_index("chip") + lax.axis_index("core")
    mine = grad.reshape(rows, -1, grad.shape[2])
    mine = lax.psum_scatter(mine, ROW, scatter_dimension=0, tiled=True)[0]
    block = mine.shape[0]
    pieces = []
    if own_heads(cols, heads_row):
        p = heads_row
        size = mine.shape[1] // kinds
        for t in range(p):
            pairs = [
                (k * cols + c, c // p * cols + k * p + (c - t) % p)
                for k in range(2)
                for c in range(cols)
            ]
            piece = lax.dynamic_slice_in_dim(mine, (col - t) % p * (block // p), block // p, 0)
            pieces.append(lax.ppermute(piece, ("core", "col"), pairs))
        pieces = [pick(pieces, (i - col) % p) for i in range(p)]
        return jnp.stack(
            [
                jnp.concatenate([q[:, a * size : (a + 1) * size] for q in pieces], axis=1)
                for a in range(kinds)
            ]
        ).astype(F32)
    width = mine.shape[1] // (kinds * ratio)
    for k in range(ratio):
        pairs = []
        for r in range(rows):
            for c in range(cols):
                s = (r - k) % ratio
                pairs.append((r * cols + c, (ratio * c + s) * cols + r // ratio))
        start = (row - k) % ratio * width
        piece = jnp.stack(
            [
                lax.dynamic_slice_in_dim(mine, a * ratio * width + start, width, 1)
                for a in range(kinds)
            ]
        )
        pieces.append(lax.ppermute(piece, ALL, pairs))
    return jnp.concatenate(
        [pick(pieces, (h - row) % ratio) for h in range(ratio)], axis=1
    ).astype(F32)


def sum_rows(values):
    total = values
    for axis in ROW:
        count = lax.axis_size(axis)
        step = 1
        while step < count:
            total = total + lax.ppermute(total, axis, [(i, i ^ step) for i in range(count)])
            step *= 2
    return total


def local(
    tokens,
    attn_gain,
    qkv_weight,
    query_gain,
    key_gain,
    out_weight,
    moe_gain,
    gate_up_weight,
    down_weight,
    segments,
    routes,
    route_gates,
    cotangent,
):
    cols = lax.axis_size("col")
    chips = lax.axis_size("chip")
    rows = 2 * chips
    col = lax.axis_index("col")
    core = lax.axis_index("core")
    row = 2 * lax.axis_index("chip") + core
    per_row, col_width = tokens.shape
    model_width = col_width * cols
    head_size = query_gain.shape[0]
    ratio = rows // cols
    head_width = model_width // cols

    experts_here, _, double_units = gate_up_weight.shape
    units = double_units // 2
    split = max(1, cols // experts_here)
    mine_count = experts_here * split // cols
    part_units = units // split
    capacity = 2 * rows * per_row * routes.shape[1] // (experts_here * rows)

    gate_up_parts = (
        gate_up_weight.reshape(experts_here, col_width, 2, split, part_units)
        .transpose(0, 3, 1, 2, 4)
        .reshape(cols, mine_count, col_width, 2 * part_units)
    )
    down_parts = down_weight.reshape(cols, mine_count, part_units, col_width)

    heads_row = qkv_weight.shape[2] // head_size
    groups = chips if own_heads(cols, heads_row) else 1

    def by_col(values):
        if groups == 1:
            return values.reshape(cols, head_width, col_width)
        values = values.reshape(groups, cols, head_width // groups, col_width)
        return values.transpose(1, 0, 2, 3).reshape(cols, head_width, col_width)

    def by_head(values):
        if groups > 1:
            values = values.reshape(cols, groups, head_width // groups, col_width)
            values = values.transpose(1, 0, 2, 3)
        return values.reshape(model_width, col_width)

    tokens_all = gather_cols(tokens)
    small = gather_cols(jnp.concatenate([attn_gain, segments.astype(F32).reshape(-1)]))
    cuts = (0, col_width // 2, 3 * col_width // 4, col_width)
    first, second, last = (
        split_parts(gate_up_parts[:, :, cuts[i] : cuts[i + 1]]) for i in range(3)
    )
    qkv_rows, small, tokens_all, out_in, first, second, last = fence(
        heads_in(qkv_weight, ratio, head_size), small, tokens_all, out_weight, first, second, last
    )
    gain_all = small[:, :col_width]
    segs = small[:, col_width:].astype(jnp.int32)
    gate_up_first = send_parts(first)
    qkv_rows, out_rows, gate_up_first, last = fence(
        over_chips(qkv_rows), over_chips(out_in), gate_up_first, last
    )
    gate_up_second, gate_up_last = send_parts(second), send_parts(last)
    if groups > 1:
        half = model_width // 2
        qkv_halves = [(qkv_rows, core * half), (swap_cores(qkv_rows), (1 - core) * half)]
    else:
        half = model_width
        qkv_halves = [(over_cores(qkv_rows)[None], 0)]
    out_split = by_col(over_cores(out_rows))
    seg_row = lax.dynamic_index_in_dim(segs.reshape(rows, per_row), row, 0, keepdims=False)

    first = row * experts_here
    expert_ids = first + (col * mine_count + jnp.arange(mine_count, dtype=jnp.int32)) // split
    place, gate, low, high = slot_places(routes, route_gates, expert_ids)

    cosine, sine = rope_tables(seg_row, head_size)
    stream_all = tokens_all.astype(F32)
    rate_one = lax.rsqrt(jnp.sum(stream_all * stream_all, axis=(0, 2)) / model_width + epsilon)
    rate_one = rate_one[:, None]
    normed_all = jnp.concatenate(
        [(stream_all[c] * rate_one * gain_all[c]).astype(BF16) for c in range(cols)], axis=1
    )
    qkv = sum(
        jnp.einsum(
            "td,gdk->gtk",
            lax.dynamic_slice_in_dim(normed_all, begin, half, 1),
            weight,
            preferred_element_type=F32,
        )
        for weight, begin in qkv_halves
    )
    head_gains = jnp.stack([query_gain, key_gain])
    heads_low, logs = attend_forward(qkv, cosine, sine, seg_row, head_gains)
    heads_low, gate_up_second = fence(heads_low, gate_up_second)
    heads_all = gather_cols(heads_low)
    stream = tokens.astype(F32)
    hidden_one = plain(
        stream + jnp.einsum("ctk,ckd->td", heads_all, out_split, preferred_element_type=F32)
    )
    rate_two = lax.rsqrt(
        width_total(jnp.sum(hidden_one * hidden_one, axis=-1)) / model_width + epsilon
    )[:, None]
    moe_in = plain((hidden_one * rate_two * moe_gain).astype(BF16))
    moe_in, gate_up_last, down_first = fence(moe_in, gate_up_last, split_parts(down_parts))
    gate_up = jnp.zeros((mine_count, model_width, 2 * part_units), BF16)
    gate_up = join_parts(gate_up_first, 1, gate_up, 0)
    gate_up = join_parts(gate_up_second, 1, gate_up, cuts[1])
    gate_up = join_parts(gate_up_last, 1, gate_up, cuts[2])

    moe_all = lax.all_gather(moe_in, ALL, axis=0).reshape(rows, cols, per_row, col_width)
    mine = jnp.reshape(core, (1,))
    others = 1 - mine
    moe_all, down_first, cot_in, gate_up, place, gate, low, high = fence(
        moe_all, down_first, cotangent, gate_up, place, gate, low, high
    )
    cot_all = lax.all_gather(cot_in, ALL, axis=0).reshape(rows, cols, per_row, col_width)
    down = join_parts(send_parts(down_first), 2)
    slot_inputs = gather_slots(moe_all, place, gate, low, high, capacity, False)

    gate_weight = gate_up[..., :part_units]
    up_weight = gate_up[..., part_units:]
    gate_pre = jnp.einsum(
        "ecd,edf->ecf", slot_inputs, gate_weight, preferred_element_type=F32
    ).astype(BF16)
    up_pre = jnp.einsum(
        "ecd,edf->ecf", slot_inputs, up_weight, preferred_element_type=F32
    ).astype(BF16)
    gate_wide = gate_pre.astype(F32)
    up_wide = up_pre.astype(F32)
    sigmoid_gate = jax.nn.sigmoid(gate_wide)
    activated = gate_wide * sigmoid_gate
    hidden = (activated * up_wide).astype(BF16)
    hidden, down = fence(hidden, down)

    combine = partial(
        combine_slots, place=place, gate=gate, low=low, high=high,
        chips=chips, per_row=per_row, parts=cols,
    )

    def feature_block(values, index):
        return lax.dynamic_slice_in_dim(values, index * col_width, col_width, 2)

    expert_out = jnp.einsum("ecf,efd->ecd", hidden, down, preferred_element_type=F32).astype(BF16)
    out_other = swap_cores(combine(expert_out, core=others, scaled=True))
    out_partial = combine(expert_out, core=mine, scaled=True, more=(out_other,))
    out_partial, cot_all = fence(out_partial, cot_all)
    out_partial = plain(lax.psum_scatter(out_partial, "col", scatter_dimension=0, tiled=True)[0])

    near = cols // 2 + 1
    grad_slot = gather_slots(cot_all, place, gate, low, high, capacity, True)

    def down_grad(mask, hidden, grad_slot):
        part = jnp.einsum(
            "ecf,ecd->efd", hidden, feature_block(grad_slot, col ^ mask),
            preferred_element_type=F32,
        )
        return part.astype(BF16) if mask else part

    near_down = [down_grad(mask, hidden, grad_slot) for mask in range(1, near)]
    near_down, grad_slot = fence(near_down, grad_slot)
    near_down = [swap_cols(part, 1 + i) for i, part in enumerate(near_down)]
    grad_hidden = jnp.einsum("ecd,efd->ecf", grad_slot, down, preferred_element_type=F32)
    grad_gate_pre = (
        grad_hidden * up_wide * sigmoid_gate * (1.0 + gate_wide * (1.0 - sigmoid_gate))
    ).astype(BF16)
    grad_up_pre = (grad_hidden * activated).astype(BF16)

    grad_slot_in = jnp.einsum(
        "ecf,edf->ecd",
        jnp.concatenate([grad_gate_pre, grad_up_pre], axis=-1),
        gate_up,
        preferred_element_type=F32,
    ).astype(BF16)
    grad_other = combine(grad_slot_in, core=others, scaled=False)
    grad_other, grad_gate_pre, grad_up_pre, near_down, out_partial, hidden, grad_slot = fence(
        grad_other, grad_gate_pre, grad_up_pre, near_down, out_partial, hidden, grad_slot
    )
    grad_other = swap_cores(grad_other)
    grad_inner = jnp.concatenate([grad_gate_pre, grad_up_pre], axis=-1)
    far_down = [down_grad(mask, hidden, grad_slot) for mask in range(near, cols)]
    grad_other, grad_inner, far_down, hidden, grad_slot = fence(
        grad_other, grad_inner, far_down, hidden, grad_slot
    )
    far_down = [swap_cols(part, near + i) for i, part in enumerate(far_down)]
    grad_partial = combine(grad_slot_in, core=mine, scaled=False, more=(grad_other,))
    grad_partial, grad_inner, hidden, grad_slot = fence(
        grad_partial, grad_inner, hidden, grad_slot
    )
    grad_partial = plain(lax.psum_scatter(grad_partial, "col", scatter_dimension=0, tiled=True)[0])
    fourth = col_width // 4

    def inner_grad(mask, begin=0, count=col_width):
        features = lax.dynamic_slice_in_dim(
            slot_inputs, (col ^ mask) * col_width + begin, count, 2
        )
        part = jnp.einsum("ecd,ecf->edf", features, grad_inner, preferred_element_type=F32)
        return part.astype(BF16) if mask else part

    inner_parts = [inner_grad(mask) for mask in range(near)]
    far_first = [inner_grad(mask, 0, fourth) for mask in range(near, cols)]
    far_rest = [inner_grad(mask, fourth, col_width - fourth) for mask in range(near, cols)]
    own_down = down_grad(0, hidden, grad_slot)
    grad_partial, inner_parts, far_first, far_rest, own_down, far_down = fence(
        grad_partial, inner_parts, far_first, far_rest, own_down, far_down
    )
    grad_moe_in = plain(lax.psum_scatter(grad_partial, "chip", scatter_dimension=0, tiled=True)[0])
    got_inner = inner_parts[:1] + [swap_cols(inner_parts[mask], mask) for mask in range(1, near)]
    grad_down = jnp.zeros((cols, mine_count, part_units, col_width), F32)
    for mask, part in enumerate([own_down] + near_down + far_down):
        grad_down = lax.dynamic_update_index_in_dim(grad_down, part.astype(F32), col ^ mask, 0)
    grad_moe_in, got_inner, out_partial, far_first, far_rest, grad_down = fence(
        grad_moe_in, got_inner, out_partial, far_first, far_rest, grad_down
    )
    far_first = [swap_cols(part, near + i) for i, part in enumerate(far_first)]
    grad_moe_in = grad_moe_in.astype(F32)

    gain_two = jnp.sum(grad_moe_in * hidden_one * rate_two, axis=0)
    grad_hidden_one = cotangent.astype(F32) + norm_back(
        grad_moe_in, hidden_one, rate_two, moe_gain, model_width
    )
    grad_branch = plain(grad_hidden_one.astype(BF16))
    head_parts = split_parts(
        jnp.einsum("td,ckd->ctk", grad_branch, out_split, preferred_element_type=F32).astype(BF16)
    )
    head_parts, far_first, got_inner = fence(head_parts, far_first, got_inner)
    grad_heads = sum_cols(head_parts).astype(BF16)
    grad_gate_up = jnp.zeros((cols, mine_count, col_width, 2 * part_units), F32)
    for mask in range(near):
        grad_gate_up = lax.dynamic_update_index_in_dim(
            grad_gate_up, got_inner[mask].astype(F32), col ^ mask, 0
        )

    def place_far(result, parts, begin):
        for mask in range(near, cols):
            part = parts[mask - near].astype(F32)[None]
            result = lax.dynamic_update_slice(result, part, (col ^ mask, 0, begin, 0))
        return result

    grad_gate_up = place_far(grad_gate_up, far_first, 0)
    grad_heads, out_partial, grad_gate_up, far_rest = fence(
        grad_heads, out_partial, grad_gate_up, far_rest
    )
    far_rest = [swap_cols(part, near + i) for i, part in enumerate(far_rest)]
    moe_result = lax.psum_scatter(out_partial, "chip", scatter_dimension=0, tiled=True)[0]
    grad_out_weight = lax.psum_scatter(
        by_head(
            jnp.einsum("ctk,td->ckd", heads_all, grad_branch, preferred_element_type=F32).astype(BF16)
        ),
        ROW,
        scatter_dimension=0,
        tiled=True,
    ).astype(F32)
    grad_projected, grad_gains = attend_backward(
        qkv, cosine, sine, seg_row, head_gains, grad_heads, logs
    )
    grad_projected, far_rest, moe_result = fence(grad_projected, far_rest, moe_result)
    output = (hidden_one + moe_result.astype(F32)).astype(BF16)
    normed_parts = [
        plain(
            jnp.einsum("gtk,gdk->td", grad_projected, weight, preferred_element_type=F32).astype(BF16)
        )
        for weight, _ in qkv_halves
    ]
    if groups > 1:
        mine_first = jnp.concatenate(normed_parts, axis=1)
        mine_last = jnp.concatenate(normed_parts[::-1], axis=1)
        normed_parts = jnp.where(core == 0, mine_first, mine_last)
    else:
        normed_parts = normed_parts[0]
    normed_parts, grad_projected, far_rest = fence(normed_parts, grad_projected, far_rest)
    grad_normed = sum_cols(
        [
            lax.dynamic_slice_in_dim(normed_parts, (col ^ mask) * col_width, col_width, 1)
            for mask in range(cols)
        ]
    )
    grad_qkv = heads_out(
        plain(
            jnp.einsum(
                "td,gtk->gdk", normed_all, grad_projected, preferred_element_type=F32
            ).astype(BF16)
        ),
        3,
        ratio,
        heads_row,
    )

    scaled_grad = grad_normed * attn_gain
    gain_one = jnp.sum(grad_normed * stream * rate_one, axis=0)
    across = jnp.sum(scaled_grad * stream, axis=-1)
    small = width_total(jnp.concatenate([across, grad_gains.reshape(-1)]))
    across = small[:per_row, None]
    gains = sum_rows(jnp.concatenate([gain_one, gain_two, small[per_row:]]))
    grad_attn_gain = gains[:col_width]
    grad_moe_gain = gains[col_width : 2 * col_width]
    grad_query_gain = gains[2 * col_width : 2 * col_width + head_size]
    grad_key_gain = gains[2 * col_width + head_size :]
    grad_tokens = (
        grad_hidden_one
        + rate_one * scaled_grad
        - stream * rate_one * rate_one * rate_one * across / model_width
    ).astype(BF16)

    grad_gate_up = place_far(grad_gate_up, far_rest, fourth)
    grad_gate_up = (
        grad_gate_up.reshape(experts_here, split, col_width, 2, part_units)
        .transpose(0, 2, 3, 1, 4)
        .reshape(experts_here, col_width, double_units)
    )
    grad_down = grad_down.reshape(experts_here, units, col_width)
    return (
        output,
        grad_tokens,
        grad_attn_gain,
        grad_qkv,
        grad_query_gain,
        grad_key_gain,
        grad_out_weight,
        grad_moe_gain,
        grad_gate_up,
        grad_down,
    )


def solution(mesh):
    rows, cols = mesh.devices.shape
    fine = Mesh(mesh.devices.reshape(rows // 2, 2, cols), ("chip", "core", "col"))
    return jax.shard_map(
        local,
        mesh=fine,
        in_specs=(
            P(ROW, "col"),
            P("col"),
            P(None, "col", ROW),
            P(),
            P(),
            P(ROW, "col"),
            P("col"),
            P(ROW, "col", None),
            P(ROW, None, "col"),
            P("col", None),
            P(),
            P(),
            P(ROW, "col"),
        ),
        out_specs=(
            P(ROW, "col"),
            P(ROW, "col"),
            P("col"),
            P(None, "col", ROW),
            P(),
            P(),
            P(ROW, "col"),
            P("col"),
            P(ROW, "col", None),
            P(ROW, None, "col"),
        ),
        check_vma=False,
    )
```

```python
from functools import partial

import jax
import jax.numpy as jnp
from jax import lax
from jax.experimental import pallas as pl
from jax.experimental.layout import Layout, with_layout_constraint
from jax.experimental.pallas import tpu as pltpu
from jax.sharding import Mesh, PartitionSpec as P

DOCS = 4
epsilon = 1e-06
rope_base = 10000.0
neg_large = -1e30

ROW = ("chip", "core")
ALL = ("chip", "core", "col")
TILE = 256
BLOCK = 512
VMEM_BYTES = 58 * 1024 * 1024
F32 = jnp.float32
BF16 = jnp.bfloat16


def rope_tables(seg_row, head_size):
    docs = jnp.arange(DOCS, dtype=jnp.int32)
    starts = jnp.sum((seg_row[:, None] < docs[None, :]).astype(jnp.int32), axis=0)
    first_index = jnp.sum(
        jnp.where(seg_row[:, None] == docs[None, :], starts[None, :], 0), axis=-1
    )
    places = (jnp.arange(seg_row.shape[0], dtype=jnp.int32) - first_index).astype(F32)
    rates = rope_base ** (-jnp.arange(0, head_size, 2, dtype=F32) / head_size)
    angles = places[..., None] * rates
    angles = jnp.concatenate([angles, angles], axis=-1)
    return (jnp.cos(angles), jnp.sin(angles))


def width_total(values):
    return lax.psum(values, "col")


def norm_back(grad_normed, stream, rate, gain, model_width):
    scaled_grad = grad_normed * gain
    across = width_total(jnp.sum(scaled_grad * stream, axis=-1))[:, None]
    return rate * scaled_grad - stream * rate * rate * rate * across / model_width


def half_turn(values, sign):
    lane = lax.broadcasted_iota(jnp.int32, values.shape, 1)
    half = values.shape[1] // 2
    return jnp.where(lane < half, sign, -sign) * pltpu.roll(values, half, 1)


def head_norm(raw, gain, cosine, sine):
    rate = lax.rsqrt(jnp.mean(raw * raw, axis=-1, keepdims=True) + epsilon)
    normed = raw * rate
    gained = normed * gain
    return normed, rate, (gained * cosine + half_turn(gained, -1.0) * sine).astype(BF16)


def masked_scores(query, key, seg_col, seg_row, factor):
    scores = lax.dot_general(
        query, key, (((1,), (1,)), ((), ())), preferred_element_type=F32
    ) * factor
    return jnp.where(seg_col == seg_row, scores, neg_large)


def attend_kernel(
    factor, query_ref, key_ref, value_ref, cos_ref, sin_ref, row_ref, col_ref, gains_ref,
    out_ref, log_ref, low_ref,
):
    cosine, sine = cos_ref[...], sin_ref[...]
    low_ref[...] = head_norm(query_ref[...], gains_ref[0:1], cosine, sine)[2]
    key = head_norm(key_ref[...], gains_ref[1:2], cosine, sine)[2]
    value = value_ref[...].astype(BF16)
    seg_row = row_ref[...]

    def body(i, carry):
        rows = pl.ds(pl.multiple_of(i * TILE, TILE), TILE)
        scores = masked_scores(low_ref[rows], key, col_ref[rows], seg_row, factor)
        top = jnp.max(scores, axis=-1, keepdims=True)
        log_total = top + jnp.log(jnp.sum(jnp.exp(scores - top), axis=-1, keepdims=True))
        probs = jnp.exp(scores - log_total).astype(BF16)
        out_ref[rows] = jnp.dot(probs, value, preferred_element_type=F32).astype(BF16)
        log_ref[rows] = jnp.broadcast_to(log_total, (TILE, log_ref.shape[1]))
        return carry

    lax.fori_loop(0, query_ref.shape[0] // TILE, body, 0)


def attend_specs(tokens, size, each):
    def part(k):
        return pl.BlockSpec((None, tokens, size), lambda h: (h // each, 0, k * each + h % each))

    whole = [
        pl.BlockSpec(shape, lambda h: (0, 0))
        for shape in ((tokens, size), (tokens, size), (1, tokens), (tokens, 1), (2, size))
    ]
    return [part(0), part(1), part(2)], whole


def attend_forward(qkv, cosine, sine, seg_row, gains):
    tokens, size = cosine.shape
    each = qkv.shape[2] // (3 * size)
    heads = qkv.shape[0] * each
    parts, whole = attend_specs(tokens, size, each)
    by_head = pl.BlockSpec((tokens, size), lambda h: (0, h))
    return pl.pallas_call(
        partial(attend_kernel, size ** (-0.5)),
        grid=(heads,),
        in_specs=parts + whole,
        out_specs=[by_head, by_head],
        out_shape=[
            jax.ShapeDtypeStruct((tokens, heads * size), BF16),
            jax.ShapeDtypeStruct((tokens, heads * size), F32),
        ],
        scratch_shapes=[pltpu.VMEM((tokens, size), BF16)],
        compiler_params=pltpu.CompilerParams(vmem_limit_bytes=VMEM_BYTES),
        cost_estimate=pl.CostEstimate(
            flops=4 * heads * tokens * tokens * size,
            bytes_accessed=qkv.size * 4 + tokens * heads * size * 6,
            transcendentals=2 * heads * tokens * tokens,
        ),
        name="attend_forward",
    )(qkv, qkv, qkv, cosine, sine, seg_row[None, :], seg_row[:, None], gains)


def attend_back_kernel(
    factor, each, query_ref, key_ref, value_ref, cos_ref, sin_ref, row_ref, col_ref, gains_ref,
    grad_ref, log_ref, out_ref, gain_ref, low_ref, query_grad, key_grad, value_grad,
):
    head = pl.program_id(0)
    group, place = head // each, head % each
    cosine, sine = cos_ref[...], sin_ref[...]
    gains = gains_ref[...]
    low_ref[...] = head_norm(query_ref[...], gains[0:1], cosine, sine)[2]
    key = head_norm(key_ref[...], gains[1:2], cosine, sine)[2]
    value = value_ref[...].astype(BF16)
    seg_row = row_ref[...]
    size = value.shape[1]
    key_grad[...] = jnp.zeros_like(key_grad)
    value_grad[...] = jnp.zeros_like(value_grad)

    def body(i, carry):
        rows = pl.ds(pl.multiple_of(i * TILE, TILE), TILE)
        query = low_ref[rows]
        grad_out = grad_ref[rows]
        scores = masked_scores(query, key, col_ref[rows], seg_row, factor)
        probs = jnp.exp(scores - log_ref[rows][:, :1])
        grad_probs = lax.dot_general(
            grad_out, value, (((1,), (1,)), ((), ())), preferred_element_type=F32
        )
        weighted = probs * grad_probs
        center = jnp.sum(weighted, axis=-1, keepdims=True)
        grad_scores = (weighted - probs * center).astype(BF16)
        query_grad[rows] = jnp.dot(grad_scores, key, preferred_element_type=F32) * factor
        first = (((0,), (0,)), ((), ()))
        key_grad[...] += lax.dot_general(grad_scores, query, first, preferred_element_type=F32)
        value_grad[...] += lax.dot_general(
            probs.astype(BF16), grad_out, first, preferred_element_type=F32
        )
        return carry

    lax.fori_loop(0, query_ref.shape[0] // TILE, body, 0)

    @pl.when(head == 0)
    def _():
        gain_ref[...] = jnp.zeros_like(gain_ref)

    for k, (raw_ref, grad) in enumerate(
        ((query_ref, query_grad[...]), (key_ref, key_grad[...] * factor))
    ):
        raw = raw_ref[...]
        rate = lax.rsqrt(jnp.mean(raw * raw, axis=-1, keepdims=True) + epsilon)
        normed = raw * rate
        grad_normed = grad * cosine + half_turn(grad * sine, 1.0)
        gain_ref[k : k + 1] += jnp.sum(grad_normed * normed, axis=0, keepdims=True)
        scaled = grad_normed * gains[k : k + 1]
        raw_grad = rate * (
            scaled - normed * jnp.mean(scaled * normed, axis=-1, keepdims=True)
        )
        columns = pl.ds(pl.multiple_of((k * each + place) * size, size), size)
        out_ref[group, :, columns] = raw_grad.astype(BF16)
    columns = pl.ds(pl.multiple_of((2 * each + place) * size, size), size)
    out_ref[group, :, columns] = value_grad[...].astype(BF16)


def attend_backward(qkv, cosine, sine, seg_row, gains, grad_heads, logs):
    tokens, size = cosine.shape
    each = qkv.shape[2] // (3 * size)
    heads = qkv.shape[0] * each
    parts, whole = attend_specs(tokens, size, each)
    by_head = pl.BlockSpec((tokens, size), lambda h: (0, h))
    return pl.pallas_call(
        partial(attend_back_kernel, size ** (-0.5), each),
        grid=(heads,),
        in_specs=parts + whole + [by_head, by_head],
        out_specs=[
            pl.BlockSpec(qkv.shape, lambda h: (0, 0, 0)),
            pl.BlockSpec((2, size), lambda h: (0, 0)),
        ],
        out_shape=[
            jax.ShapeDtypeStruct(qkv.shape, BF16),
            jax.ShapeDtypeStruct((2, size), F32),
        ],
        scratch_shapes=[
            pltpu.VMEM((tokens, size), BF16),
            pltpu.VMEM((tokens, size), F32),
            pltpu.VMEM((tokens, size), F32),
            pltpu.VMEM((tokens, size), F32),
        ],
        compiler_params=pltpu.CompilerParams(vmem_limit_bytes=VMEM_BYTES),
        cost_estimate=pl.CostEstimate(
            flops=10 * heads * tokens * tokens * size,
            bytes_accessed=qkv.size * 6 + tokens * heads * size * 6,
            transcendentals=heads * tokens * tokens,
        ),
        name="attend_backward",
    )(qkv, qkv, qkv, cosine, sine, seg_row[None, :], seg_row[:, None], gains, grad_heads, logs)


def slot_places(routes, route_gates, expert_ids):
    chosen = routes[None] == expert_ids[:, None, None]
    hit = jnp.any(chosen, axis=-1)
    gate = jnp.sum(jnp.where(chosen, route_gates[None], 0.0), axis=-1)
    count, tok_total = hit.shape
    grouped = hit.astype(BF16).reshape(count, tok_total // 128, 128)
    lane = jnp.arange(128)
    before = (lane[:, None] < lane[None, :]).astype(BF16)
    inside = jnp.einsum("egt,tu->egu", grouped, before, preferred_element_type=F32)
    totals = jnp.sum(grouped.astype(F32), axis=-1).astype(BF16)
    group = jnp.arange(tok_total // 128)
    earlier = (group[:, None] < group[None, :]).astype(BF16)
    offset = jnp.einsum("eg,gh->eh", totals, earlier, preferred_element_type=F32)
    place = (inside + offset[..., None]).reshape(count, tok_total).astype(jnp.int32)
    per_block = jnp.sum(hit.astype(jnp.int32).reshape(count, tok_total // BLOCK, BLOCK), axis=-1)
    begin = place.reshape(count, tok_total // BLOCK, BLOCK)[:, :, 0]
    end = begin + per_block
    low = begin // TILE
    high = jnp.where(end > begin, (end + TILE - 1) // TILE, low)
    return (jnp.where(hit, place, -1), gate, low, high)


def gather_kernel(scaled, each, low_ref, high_ref, *refs):
    rows_refs, place_refs, gate_refs, slots_ref = refs[0:2], refs[2:4], refs[4:6], refs[6]
    chip, piece = pl.program_id(0), pl.program_id(1)
    experts = slots_ref.shape[0]

    @pl.when((chip == 0) & (piece == 0))
    def _():
        slots_ref[...] = jnp.zeros_like(slots_ref)

    for k in range(2):
        rows_ref = rows_refs[k]
        parts, width = rows_ref.shape[1], rows_ref.shape[3]
        block = (2 * chip + k) * each + piece
        for e in range(experts):
            place = place_refs[k][e, 0]
            gate = gate_refs[k][e, 0]

            def body(i, carry):
                base = pl.multiple_of(i * TILE, TILE)
                wanted = lax.broadcasted_iota(jnp.int32, (TILE, BLOCK), 0) + base
                mask = place == wanted
                onehot = mask.astype(F32).astype(BF16)
                if scaled:
                    factor = jnp.sum(jnp.where(mask, gate, 0.0), axis=1, keepdims=True)
                for c in range(parts):
                    picked = jnp.dot(onehot, rows_ref[0, c], preferred_element_type=F32)
                    if scaled:
                        picked = picked * factor
                    where = (e, pl.ds(base, TILE), slice(c * width, (c + 1) * width))
                    slots_ref[where] = slots_ref[where] + picked.astype(BF16)
                return carry

            lax.fori_loop(low_ref[e, block], high_ref[e, block], body, 0)


def gather_slots(rows, place, gate, low, high, capacity, scaled):
    row_count, parts, per_row, width = rows.shape
    experts, tok_total = place.shape
    blocks = tok_total // BLOCK
    each = per_row // BLOCK

    def row_spec(k):
        return pl.BlockSpec(
            (1, parts, BLOCK, width),
            lambda z, j, *_: (2 * z + k, 0, j, 0),
        )

    def token_spec(k):
        return pl.BlockSpec(
            (experts, 1, 1, BLOCK),
            lambda z, j, *_: (0, (2 * z + k) * each + j, 0, 0),
        )

    places = place.reshape(experts, blocks, 1, BLOCK)
    gates = gate.reshape(experts, blocks, 1, BLOCK)
    return pl.pallas_call(
        partial(gather_kernel, scaled, each),
        grid_spec=pltpu.PrefetchScalarGridSpec(
            num_scalar_prefetch=2,
            grid=(row_count // 2, each),
            in_specs=[
                row_spec(0), row_spec(1), token_spec(0), token_spec(1), token_spec(0), token_spec(1),
            ],
            out_specs=pl.BlockSpec((experts, capacity, parts * width), lambda *_: (0, 0, 0)),
        ),
        out_shape=jax.ShapeDtypeStruct((experts, capacity, parts * width), BF16),
        compiler_params=pltpu.CompilerParams(vmem_limit_bytes=VMEM_BYTES),
        cost_estimate=pl.CostEstimate(
            flops=2 * 24 * experts * TILE * BLOCK * parts * width,
            bytes_accessed=(tok_total + experts * capacity) * parts * width * 2,
            transcendentals=0,
        ),
        name="gather_slots",
    )(low, high, rows, rows, places, places, gates, gates)


def combine_kernel(
    scaled, added, each, begin, low_ref, high_ref, core_ref, slots_ref, place_ref, gate_ref, *refs
):
    out_ref, total_ref = refs[-2:]
    chip, piece = pl.program_id(0) + begin, pl.program_id(1)
    block = (2 * chip + core_ref[0]) * each + piece
    experts = slots_ref.shape[0]
    parts, width = out_ref.shape[0], out_ref.shape[3]
    total_ref[...] = jnp.zeros_like(total_ref)
    for e in range(experts):
        place = jnp.broadcast_to(place_ref[e, 0].astype(F32), (8, BLOCK)).T[:, :1]
        if scaled:
            gate = jnp.broadcast_to(gate_ref[e, 0], (8, BLOCK)).T[:, :1]

        def body(i, carry):
            base = pl.multiple_of(i * TILE, TILE)
            wanted = lax.broadcasted_iota(jnp.int32, (BLOCK, TILE), 1) + base
            onehot = (place == wanted.astype(F32)).astype(F32).astype(BF16)
            for c in range(parts):
                columns = slice(c * width, (c + 1) * width)
                picked = jnp.dot(
                    onehot, slots_ref[e, pl.ds(base, TILE), columns], preferred_element_type=F32
                )
                if scaled:
                    picked = picked * gate
                total_ref[:, columns] = total_ref[:, columns] + picked
            return carry

        lax.fori_loop(low_ref[e, block], high_ref[e, block], body, 0)
    for c in range(parts):
        total = total_ref[:, c * width : (c + 1) * width]
        if added:
            total = total + refs[0][c, 0].astype(F32)
        out_ref[c, 0] = total.astype(BF16)


def combine_slots(
    slots, place, gate, low, high, core, chips, per_row, parts, scaled, begin=0, more=None, into=None
):
    experts, capacity, model_width = slots.shape
    width = model_width // parts
    each = per_row // BLOCK
    blocks = place.shape[1] // BLOCK
    count = chips // 2

    def token_block(z, j, low_ref, high_ref, core_ref):
        return (0, (2 * (z + begin) + core_ref[0]) * each + j, 0, 0)

    half = pl.BlockSpec((parts, 1, BLOCK, width), lambda z, j, *_: (0, z, j, 0))
    whole = pl.BlockSpec((parts, 1, BLOCK, width), lambda z, j, *_: (0, z + begin, j, 0))
    added = more is not None
    in_specs = [
        pl.BlockSpec(
            (experts, capacity, model_width),
            lambda *_: (0, 0, 0),
            pipeline_mode=pl.Buffered(1),
        ),
        pl.BlockSpec((experts, 1, 1, BLOCK), token_block),
        pl.BlockSpec((experts, 1, 1, BLOCK), token_block),
    ]
    inputs = [
        low,
        high,
        core,
        slots,
        place.reshape(experts, blocks, 1, BLOCK),
        gate.reshape(experts, blocks, 1, BLOCK),
    ]
    aliases = {}
    if added:
        in_specs.append(half)
        inputs.append(more)
    if into is not None:
        aliases = {len(inputs): 0}
        in_specs.append(pl.BlockSpec(memory_space=pl.ANY))
        inputs.append(into)
    return pl.pallas_call(
        partial(combine_kernel, scaled, added, each, begin),
        grid_spec=pltpu.PrefetchScalarGridSpec(
            num_scalar_prefetch=3,
            grid=(count, each),
            in_specs=in_specs,
            out_specs=whole if added else half,
            scratch_shapes=[pltpu.VMEM((BLOCK, model_width), F32)],
        ),
        out_shape=jax.ShapeDtypeStruct(
            (parts, chips if added else count, per_row, width), BF16
        ),
        input_output_aliases=aliases,
        compiler_params=pltpu.CompilerParams(vmem_limit_bytes=VMEM_BYTES),
        cost_estimate=pl.CostEstimate(
            flops=12 * experts * TILE * BLOCK * model_width,
            bytes_accessed=slots.size * 2 + parts * count * per_row * width * 2,
            transcendentals=0,
        ),
        name="combine_slots",
    )(*inputs)


def swap_cores(values):
    return lax.ppermute(values, "core", [(0, 1), (1, 0)])


def swap_cols(values, mask):
    count = lax.axis_size("col")
    return lax.ppermute(values, "col", [(i, i ^ mask) for i in range(count)])


def fence(*values):
    return lax.optimization_barrier(values)


def plain(values):
    return with_layout_constraint(values, Layout(tuple(range(values.ndim))))


def gather_cols(values):
    count = lax.axis_size("col")
    me = lax.axis_index("col")
    result = jnp.zeros((count,) + values.shape, values.dtype)
    for mask in range(count):
        piece = swap_cols(values, mask) if mask else values
        result = lax.dynamic_update_index_in_dim(result, piece, me ^ mask, 0)
    return result


def sum_cols(pieces):
    total = 0.0
    for piece in send_parts(pieces):
        total = total + piece.astype(F32)
    return total


def split_parts(parts):
    me = lax.axis_index("col")
    return [
        plain(lax.dynamic_index_in_dim(parts, me ^ mask, 0, keepdims=False))
        for mask in range(lax.axis_size("col"))
    ]


def send_parts(pieces):
    return pieces[:1] + [swap_cols(pieces[mask], mask) for mask in range(1, len(pieces))]


def join_parts(pieces, axis, result=None, offset=0):
    me = lax.axis_index("col")
    if result is None:
        shape = list(pieces[0].shape)
        shape[axis] *= len(pieces)
        result = jnp.zeros(shape, pieces[0].dtype)
    size = result.shape[axis] // len(pieces)
    for mask, piece in enumerate(pieces):
        start = (me ^ mask) * size + offset
        result = lax.dynamic_update_slice_in_dim(result, piece, start, axis)
    return result


def swap_chips(values, mask):
    count = lax.axis_size("chip")
    return lax.ppermute(values, "chip", [(i, i ^ mask) for i in range(count)])


def over_chips(values):
    chips = lax.axis_size("chip")
    chip = lax.axis_index("chip")
    same = jnp.zeros((chips,) + values.shape, values.dtype)
    for mask in range(chips):
        piece = swap_chips(values, mask) if mask else values
        same = lax.dynamic_update_index_in_dim(same, piece, chip ^ mask, 0)
    return same


def over_cores(same):
    core = lax.axis_index("core")
    other = swap_cores(same)
    both = jnp.stack([jnp.where(core == 0, same, other), jnp.where(core == 0, other, same)], axis=1)
    return both.reshape(-1, same.shape[-1])


def pick(pieces, index):
    chosen = pieces[0]
    for k in range(1, len(pieces)):
        chosen = jnp.where(index == k, pieces[k], chosen)
    return chosen


def own_heads(cols, heads_row):
    return 2 * heads_row == cols


def heads_in(weight, ratio, size):
    chips, cols = lax.axis_size("chip"), lax.axis_size("col")
    core, col = lax.axis_index("core"), lax.axis_index("col")
    rows = 2 * chips
    row = 2 * lax.axis_index("chip") + core
    kinds, features, width = weight.shape
    pieces = []
    if own_heads(cols, width // size):
        p = width // size
        for t in range(p):
            pairs = [
                (k * cols + c, c // p * cols + k * p + (t + c) % p)
                for k in range(2)
                for c in range(cols)
            ]
            piece = lax.dynamic_slice_in_dim(weight, (t + col) % p * size, size, 2)
            pieces.append(lax.ppermute(piece, ("core", "col"), pairs))
        pieces = [pick(pieces, (col - b) % p) for b in range(p)]
        return jnp.concatenate(
            [jnp.concatenate([p[a] for a in range(kinds)], axis=1) for p in pieces], axis=0
        )
    block = features // ratio
    for k in range(ratio):
        pairs = []
        for r in range(rows):
            for c in range(cols):
                h = (k + r) % ratio
                pairs.append((r * cols + c, (ratio * c + h) * cols + r // ratio))
        piece = lax.dynamic_slice_in_dim(weight, (k + row) % ratio * block, block, 1)
        pieces.append(lax.ppermute(piece, ALL, pairs))
    return jnp.concatenate(
        [pick([p[a] for p in pieces], (row - s) % ratio) for a in range(kinds) for s in range(ratio)],
        axis=1,
    )


def heads_out(grad, kinds, ratio, heads_row):
    chips, cols = lax.axis_size("chip"), lax.axis_size("col")
    col = lax.axis_index("col")
    rows = 2 * chips
    row = 2 * lax.axis_index("chip") + lax.axis_index("core")
    mine = grad.reshape(rows, -1, grad.shape[2])
    mine = lax.psum_scatter(mine, ROW, scatter_dimension=0, tiled=True)[0]
    block = mine.shape[0]
    pieces = []
    if own_heads(cols, heads_row):
        p = heads_row
        size = mine.shape[1] // kinds
        for t in range(p):
            pairs = [
                (k * cols + c, c // p * cols + k * p + (c - t) % p)
                for k in range(2)
                for c in range(cols)
            ]
            piece = lax.dynamic_slice_in_dim(mine, (col - t) % p * (block // p), block // p, 0)
            pieces.append(lax.ppermute(piece, ("core", "col"), pairs))
        pieces = [pick(pieces, (i - col) % p) for i in range(p)]
        return jnp.stack(
            [
                jnp.concatenate([q[:, a * size : (a + 1) * size] for q in pieces], axis=1)
                for a in range(kinds)
            ]
        ).astype(F32)
    width = mine.shape[1] // (kinds * ratio)
    for k in range(ratio):
        pairs = []
        for r in range(rows):
            for c in range(cols):
                s = (r - k) % ratio
                pairs.append((r * cols + c, (ratio * c + s) * cols + r // ratio))
        start = (row - k) % ratio * width
        piece = jnp.stack(
            [
                lax.dynamic_slice_in_dim(mine, a * ratio * width + start, width, 1)
                for a in range(kinds)
            ]
        )
        pieces.append(lax.ppermute(piece, ALL, pairs))
    return jnp.concatenate(
        [pick(pieces, (h - row) % ratio) for h in range(ratio)], axis=1
    ).astype(F32)


def sum_rows(values):
    total = values
    for axis in ROW:
        count = lax.axis_size(axis)
        step = 1
        while step < count:
            total = total + lax.ppermute(total, axis, [(i, i ^ step) for i in range(count)])
            step *= 2
    return total


def local(
    tokens,
    attn_gain,
    qkv_weight,
    query_gain,
    key_gain,
    out_weight,
    moe_gain,
    gate_up_weight,
    down_weight,
    segments,
    routes,
    route_gates,
    cotangent,
):
    cols = lax.axis_size("col")
    chips = lax.axis_size("chip")
    rows = 2 * chips
    col = lax.axis_index("col")
    core = lax.axis_index("core")
    row = 2 * lax.axis_index("chip") + core
    per_row, col_width = tokens.shape
    model_width = col_width * cols
    head_size = query_gain.shape[0]
    ratio = rows // cols
    head_width = model_width // cols

    experts_here, _, double_units = gate_up_weight.shape
    units = double_units // 2
    split = max(1, cols // experts_here)
    mine_count = experts_here * split // cols
    part_units = units // split
    capacity = 2 * rows * per_row * routes.shape[1] // (experts_here * rows)

    gate_up_parts = (
        gate_up_weight.reshape(experts_here, col_width, 2, split, part_units)
        .transpose(0, 3, 1, 2, 4)
        .reshape(cols, mine_count, col_width, 2 * part_units)
    )
    down_parts = down_weight.reshape(cols, mine_count, part_units, col_width)

    heads_row = qkv_weight.shape[2] // head_size
    groups = chips if own_heads(cols, heads_row) else 1

    def by_col(values):
        if groups == 1:
            return values.reshape(cols, head_width, col_width)
        values = values.reshape(groups, cols, head_width // groups, col_width)
        return values.transpose(1, 0, 2, 3).reshape(cols, head_width, col_width)

    def by_head(values):
        if groups > 1:
            values = values.reshape(cols, groups, head_width // groups, col_width)
            values = values.transpose(1, 0, 2, 3)
        return values.reshape(model_width, col_width)

    tokens_all = gather_cols(tokens)
    small = gather_cols(jnp.concatenate([attn_gain, segments.astype(F32).reshape(-1)]))
    qkv_rows, small, tokens_all, out_in = fence(
        heads_in(qkv_weight, ratio, head_size), small, tokens_all, out_weight
    )
    gain_all = small[:, :col_width]
    segs = small[:, col_width:].astype(jnp.int32)
    cuts = (0, col_width // 2, 3 * col_width // 4, col_width)
    first, second, last = (
        split_parts(gate_up_parts[:, :, cuts[i] : cuts[i + 1]]) for i in range(3)
    )
    gate_up_first = send_parts(first)
    qkv_rows, out_rows, gate_up_first, second, last = fence(
        over_chips(qkv_rows), over_chips(out_in), gate_up_first, second, last
    )
    gate_up_second, gate_up_last = send_parts(second), send_parts(last)
    if groups > 1:
        half = model_width // 2
        qkv_halves = [(qkv_rows, core * half), (swap_cores(qkv_rows), (1 - core) * half)]
    else:
        half = model_width
        qkv_halves = [(over_cores(qkv_rows)[None], 0)]
    out_split = by_col(over_cores(out_rows))
    seg_row = lax.dynamic_index_in_dim(segs.reshape(rows, per_row), row, 0, keepdims=False)

    first = row * experts_here
    expert_ids = first + (col * mine_count + jnp.arange(mine_count, dtype=jnp.int32)) // split
    place, gate, low, high = slot_places(routes, route_gates, expert_ids)

    cosine, sine = rope_tables(seg_row, head_size)
    stream_all = tokens_all.astype(F32)
    rate_one = lax.rsqrt(jnp.sum(stream_all * stream_all, axis=(0, 2)) / model_width + epsilon)
    rate_one = rate_one[:, None]
    normed_all = jnp.concatenate(
        [(stream_all[c] * rate_one * gain_all[c]).astype(BF16) for c in range(cols)], axis=1
    )
    qkv = sum(
        jnp.einsum(
            "td,gdk->gtk",
            lax.dynamic_slice_in_dim(normed_all, begin, half, 1),
            weight,
            preferred_element_type=F32,
        )
        for weight, begin in qkv_halves
    )
    head_gains = jnp.stack([query_gain, key_gain])
    heads_low, logs = attend_forward(qkv, cosine, sine, seg_row, head_gains)
    heads_low, gate_up_second = fence(heads_low, gate_up_second)
    heads_all = gather_cols(heads_low)
    stream = tokens.astype(F32)
    hidden_one = plain(
        stream + jnp.einsum("ctk,ckd->td", heads_all, out_split, preferred_element_type=F32)
    )
    rate_two = lax.rsqrt(
        width_total(jnp.sum(hidden_one * hidden_one, axis=-1)) / model_width + epsilon
    )[:, None]
    moe_in = plain((hidden_one * rate_two * moe_gain).astype(BF16))
    moe_in, gate_up_last, down_first = fence(moe_in, gate_up_last, split_parts(down_parts))
    gate_up = jnp.zeros((mine_count, model_width, 2 * part_units), BF16)
    gate_up = join_parts(gate_up_first, 1, gate_up, 0)
    gate_up = join_parts(gate_up_second, 1, gate_up, cuts[1])
    gate_up = join_parts(gate_up_last, 1, gate_up, cuts[2])

    moe_all = lax.all_gather(moe_in, ALL, axis=0).reshape(rows, cols, per_row, col_width)
    mine = jnp.reshape(core, (1,))
    others = 1 - mine
    moe_all, down_first, cot_in, gate_up, place, gate, low, high = fence(
        moe_all, down_first, cotangent, gate_up, place, gate, low, high
    )
    cot_all = lax.all_gather(cot_in, ALL, axis=0).reshape(rows, cols, per_row, col_width)
    down = join_parts(send_parts(down_first), 2)
    slot_inputs = gather_slots(moe_all, place, gate, low, high, capacity, False)

    gate_weight = gate_up[..., :part_units]
    up_weight = gate_up[..., part_units:]
    gate_pre = jnp.einsum(
        "ecd,edf->ecf", slot_inputs, gate_weight, preferred_element_type=F32
    ).astype(BF16)
    up_pre = jnp.einsum(
        "ecd,edf->ecf", slot_inputs, up_weight, preferred_element_type=F32
    ).astype(BF16)
    gate_wide = gate_pre.astype(F32)
    up_wide = up_pre.astype(F32)
    sigmoid_gate = jax.nn.sigmoid(gate_wide)
    activated = gate_wide * sigmoid_gate
    hidden = (activated * up_wide).astype(BF16)
    hidden, down = fence(hidden, down)

    combine = partial(
        combine_slots, place=place, gate=gate, low=low, high=high,
        chips=chips, per_row=per_row, parts=cols,
    )

    def feature_block(values, index):
        return lax.dynamic_slice_in_dim(values, index * col_width, col_width, 2)

    expert_out = jnp.einsum("ecf,efd->ecd", hidden, down, preferred_element_type=F32).astype(BF16)
    middle = chips // 2
    out_first = combine(expert_out, core=others, scaled=True)
    out_last = combine(expert_out, core=others, scaled=True, begin=middle)
    out_partial = combine(expert_out, core=mine, scaled=True, more=swap_cores(out_first))
    out_partial = combine(
        expert_out, core=mine, scaled=True, begin=middle, more=swap_cores(out_last), into=out_partial
    )
    out_partial, cot_all = fence(out_partial, cot_all)
    out_partial = plain(lax.psum_scatter(out_partial, "col", scatter_dimension=0, tiled=True)[0])

    grad_slot = gather_slots(cot_all, place, gate, low, high, capacity, True)

    def down_grad(mask, hidden, grad_slot):
        part = jnp.einsum(
            "ecf,ecd->efd", hidden, feature_block(grad_slot, col ^ mask),
            preferred_element_type=F32,
        )
        return part.astype(BF16) if mask else part

    near = cols // 2 + 1
    down_grads = [down_grad(mask, hidden, grad_slot) for mask in range(1, cols)]
    down_grads, grad_slot = fence(down_grads, grad_slot)
    near_down = [swap_cols(part, 1 + i) for i, part in enumerate(down_grads[: near - 1])]
    far_down = [swap_cols(part, near + i) for i, part in enumerate(down_grads[near - 1 :])]
    grad_hidden = jnp.einsum("ecd,efd->ecf", grad_slot, down, preferred_element_type=F32)
    grad_gate_pre = (
        grad_hidden * up_wide * sigmoid_gate * (1.0 + gate_wide * (1.0 - sigmoid_gate))
    ).astype(BF16)
    grad_up_pre = (grad_hidden * activated).astype(BF16)

    grad_slot_in = jnp.einsum(
        "ecf,edf->ecd",
        jnp.concatenate([grad_gate_pre, grad_up_pre], axis=-1),
        gate_up,
        preferred_element_type=F32,
    ).astype(BF16)
    grad_first = swap_cores(combine(grad_slot_in, core=others, scaled=False))
    grad_last = combine(grad_slot_in, core=others, scaled=False, begin=middle)
    grad_last, grad_gate_pre, grad_up_pre, near_down, out_partial = fence(
        grad_last, grad_gate_pre, grad_up_pre, near_down, out_partial
    )
    grad_last = swap_cores(grad_last)
    grad_inner = jnp.concatenate([grad_gate_pre, grad_up_pre], axis=-1)
    grad_first, grad_inner = fence(grad_first, grad_inner)
    grad_partial = combine(grad_slot_in, core=mine, scaled=False, more=grad_first)
    grad_partial = combine(
        grad_slot_in, core=mine, scaled=False, begin=middle, more=grad_last, into=grad_partial
    )
    grad_partial, grad_inner, far_down, hidden, grad_slot = fence(
        grad_partial, grad_inner, far_down, hidden, grad_slot
    )
    grad_partial = plain(lax.psum_scatter(grad_partial, "col", scatter_dimension=0, tiled=True)[0])
    inner_parts = []
    for mask in range(cols):
        part = jnp.einsum(
            "ecd,ecf->edf", feature_block(slot_inputs, col ^ mask), grad_inner,
            preferred_element_type=F32,
        )
        inner_parts.append(part.astype(BF16) if mask else part)
    own_down = down_grad(0, hidden, grad_slot)
    grad_partial, inner_parts, own_down = fence(grad_partial, inner_parts, own_down)
    got_down = [own_down] + near_down + far_down
    grad_moe_in = plain(lax.psum_scatter(grad_partial, "chip", scatter_dimension=0, tiled=True)[0])
    far_parts = inner_parts[near:]
    got_inner = inner_parts[:1] + [swap_cols(inner_parts[mask], mask) for mask in range(1, near)]
    grad_moe_in, got_inner, out_partial, far_parts = fence(
        grad_moe_in, got_inner, out_partial, far_parts
    )
    grad_moe_in = grad_moe_in.astype(F32)

    gain_two = jnp.sum(grad_moe_in * hidden_one * rate_two, axis=0)
    grad_hidden_one = cotangent.astype(F32) + norm_back(
        grad_moe_in, hidden_one, rate_two, moe_gain, model_width
    )
    grad_branch = plain(grad_hidden_one.astype(BF16))
    grad_heads = sum_cols(
        split_parts(
            jnp.einsum("td,ckd->ctk", grad_branch, out_split, preferred_element_type=F32).astype(BF16)
        )
    ).astype(BF16)
    grad_down = jnp.zeros((cols, mine_count, part_units, col_width), F32)
    for mask in range(cols):
        grad_down = lax.dynamic_update_index_in_dim(
            grad_down, got_down[mask].astype(F32), col ^ mask, 0
        )
    grad_heads, out_partial, far_parts, grad_down = fence(
        grad_heads, out_partial, far_parts, grad_down
    )
    far_parts = [swap_cols(part, near + i) for i, part in enumerate(far_parts)]
    moe_result = lax.psum_scatter(out_partial, "chip", scatter_dimension=0, tiled=True)[0]
    grad_out_weight = lax.psum_scatter(
        by_head(
            jnp.einsum("ctk,td->ckd", heads_all, grad_branch, preferred_element_type=F32).astype(BF16)
        ),
        ROW,
        scatter_dimension=0,
        tiled=True,
    ).astype(F32)
    grad_projected, grad_gains = attend_backward(
        qkv, cosine, sine, seg_row, head_gains, grad_heads, logs
    )
    grad_gate_up = jnp.zeros((cols, mine_count, col_width, 2 * part_units), F32)
    for mask in range(near):
        grad_gate_up = lax.dynamic_update_index_in_dim(
            grad_gate_up, got_inner[mask].astype(F32), col ^ mask, 0
        )
    grad_projected, far_parts, moe_result, grad_gate_up = fence(
        grad_projected, far_parts, moe_result, grad_gate_up
    )
    output = (hidden_one + moe_result.astype(F32)).astype(BF16)
    normed_parts = [
        plain(
            jnp.einsum("gtk,gdk->td", grad_projected, weight, preferred_element_type=F32).astype(BF16)
        )
        for weight, _ in qkv_halves
    ]
    if groups > 1:
        mine_first = jnp.concatenate(normed_parts, axis=1)
        mine_last = jnp.concatenate(normed_parts[::-1], axis=1)
        normed_parts = jnp.where(core == 0, mine_first, mine_last)
    else:
        normed_parts = normed_parts[0]
    normed_parts, grad_projected, far_parts = fence(normed_parts, grad_projected, far_parts)
    grad_normed = sum_cols(
        [
            lax.dynamic_slice_in_dim(normed_parts, (col ^ mask) * col_width, col_width, 1)
            for mask in range(cols)
        ]
    )
    grad_qkv = heads_out(
        plain(
            jnp.einsum(
                "td,gtk->gdk", normed_all, grad_projected, preferred_element_type=F32
            ).astype(BF16)
        ),
        3,
        ratio,
        heads_row,
    )

    scaled_grad = grad_normed * attn_gain
    gain_one = jnp.sum(grad_normed * stream * rate_one, axis=0)
    across = jnp.sum(scaled_grad * stream, axis=-1)
    small = width_total(jnp.concatenate([across, grad_gains.reshape(-1)]))
    across = small[:per_row, None]
    gains = sum_rows(jnp.concatenate([gain_one, gain_two, small[per_row:]]))
    grad_attn_gain = gains[:col_width]
    grad_moe_gain = gains[col_width : 2 * col_width]
    grad_query_gain = gains[2 * col_width : 2 * col_width + head_size]
    grad_key_gain = gains[2 * col_width + head_size :]
    grad_tokens = (
        grad_hidden_one
        + rate_one * scaled_grad
        - stream * rate_one * rate_one * rate_one * across / model_width
    ).astype(BF16)

    for mask in range(near, cols):
        grad_gate_up = lax.dynamic_update_index_in_dim(
            grad_gate_up, far_parts[mask - near].astype(F32), col ^ mask, 0
        )
    grad_gate_up = (
        grad_gate_up.reshape(experts_here, split, col_width, 2, part_units)
        .transpose(0, 2, 3, 1, 4)
        .reshape(experts_here, col_width, double_units)
    )
    grad_down = grad_down.reshape(experts_here, units, col_width)
    return (
        output,
        grad_tokens,
        grad_attn_gain,
        grad_qkv,
        grad_query_gain,
        grad_key_gain,
        grad_out_weight,
        grad_moe_gain,
        grad_gate_up,
        grad_down,
    )


def solution(mesh):
    rows, cols = mesh.devices.shape
    fine = Mesh(mesh.devices.reshape(rows // 2, 2, cols), ("chip", "core", "col"))
    return jax.shard_map(
        local,
        mesh=fine,
        in_specs=(
            P(ROW, "col"),
            P("col"),
            P(None, "col", ROW),
            P(),
            P(),
            P(ROW, "col"),
            P("col"),
            P(ROW, "col", None),
            P(ROW, None, "col"),
            P("col", None),
            P(),
            P(),
            P(ROW, "col"),
        ),
        out_specs=(
            P(ROW, "col"),
            P(ROW, "col"),
            P("col"),
            P(None, "col", ROW),
            P(),
            P(),
            P(ROW, "col"),
            P("col"),
            P(ROW, "col", None),
            P(ROW, None, "col"),
        ),
        check_vma=False,
    )
```

```python
from functools import partial

import jax
import jax.numpy as jnp
from jax import lax
from jax.experimental import pallas as pl
from jax.experimental.layout import Layout, with_layout_constraint
from jax.experimental.pallas import tpu as pltpu
from jax.sharding import Mesh, PartitionSpec as P

DOCS = 4
epsilon = 1e-06
rope_base = 10000.0
neg_large = -1e30

ROW = ("chip", "core")
ALL = ("chip", "core", "col")
TILE = 256
BLOCK = 512
VMEM_BYTES = 58 * 1024 * 1024
F32 = jnp.float32
BF16 = jnp.bfloat16


def rope_tables(seg_row, head_size):
    docs = jnp.arange(DOCS, dtype=jnp.int32)
    starts = jnp.sum((seg_row[:, None] < docs[None, :]).astype(jnp.int32), axis=0)
    first_index = jnp.sum(
        jnp.where(seg_row[:, None] == docs[None, :], starts[None, :], 0), axis=-1
    )
    places = (jnp.arange(seg_row.shape[0], dtype=jnp.int32) - first_index).astype(F32)
    rates = rope_base ** (-jnp.arange(0, head_size, 2, dtype=F32) / head_size)
    angles = places[..., None] * rates
    angles = jnp.concatenate([angles, angles], axis=-1)
    return (jnp.cos(angles), jnp.sin(angles))


def width_total(values):
    return lax.psum(values, "col")


def norm_back(grad_normed, stream, rate, gain, model_width):
    scaled_grad = grad_normed * gain
    across = width_total(jnp.sum(scaled_grad * stream, axis=-1))[:, None]
    return rate * scaled_grad - stream * rate * rate * rate * across / model_width


def half_turn(values, sign):
    lane = lax.broadcasted_iota(jnp.int32, values.shape, 1)
    half = values.shape[1] // 2
    return jnp.where(lane < half, sign, -sign) * pltpu.roll(values, half, 1)


def head_norm(raw, gain, cosine, sine):
    rate = lax.rsqrt(jnp.mean(raw * raw, axis=-1, keepdims=True) + epsilon)
    normed = raw * rate
    gained = normed * gain
    return normed, rate, (gained * cosine + half_turn(gained, -1.0) * sine).astype(BF16)


def masked_scores(query, key, seg_col, seg_row, factor):
    scores = lax.dot_general(
        query, key, (((1,), (1,)), ((), ())), preferred_element_type=F32
    ) * factor
    return jnp.where(seg_col == seg_row, scores, neg_large)


def attend_kernel(
    factor, query_ref, key_ref, value_ref, cos_ref, sin_ref, row_ref, col_ref, gains_ref,
    out_ref, log_ref, low_ref,
):
    cosine, sine = cos_ref[...], sin_ref[...]
    low_ref[...] = head_norm(query_ref[...], gains_ref[0:1], cosine, sine)[2]
    key = head_norm(key_ref[...], gains_ref[1:2], cosine, sine)[2]
    value = value_ref[...].astype(BF16)
    seg_row = row_ref[...]

    def body(i, carry):
        rows = pl.ds(pl.multiple_of(i * TILE, TILE), TILE)
        scores = masked_scores(low_ref[rows], key, col_ref[rows], seg_row, factor)
        top = jnp.max(scores, axis=-1, keepdims=True)
        log_total = top + jnp.log(jnp.sum(jnp.exp(scores - top), axis=-1, keepdims=True))
        probs = jnp.exp(scores - log_total).astype(BF16)
        out_ref[rows] = jnp.dot(probs, value, preferred_element_type=F32).astype(BF16)
        log_ref[rows] = jnp.broadcast_to(log_total, (TILE, log_ref.shape[1]))
        return carry

    lax.fori_loop(0, query_ref.shape[0] // TILE, body, 0)


def attend_specs(tokens, size, each):
    def part(k):
        return pl.BlockSpec((None, tokens, size), lambda h: (h // each, 0, k * each + h % each))

    whole = [
        pl.BlockSpec(shape, lambda h: (0, 0))
        for shape in ((tokens, size), (tokens, size), (1, tokens), (tokens, 1), (2, size))
    ]
    return [part(0), part(1), part(2)], whole


def attend_forward(qkv, cosine, sine, seg_row, gains):
    tokens, size = cosine.shape
    each = qkv.shape[2] // (3 * size)
    heads = qkv.shape[0] * each
    parts, whole = attend_specs(tokens, size, each)
    by_head = pl.BlockSpec((tokens, size), lambda h: (0, h))
    return pl.pallas_call(
        partial(attend_kernel, size ** (-0.5)),
        grid=(heads,),
        in_specs=parts + whole,
        out_specs=[by_head, by_head],
        out_shape=[
            jax.ShapeDtypeStruct((tokens, heads * size), BF16),
            jax.ShapeDtypeStruct((tokens, heads * size), F32),
        ],
        scratch_shapes=[pltpu.VMEM((tokens, size), BF16)],
        compiler_params=pltpu.CompilerParams(vmem_limit_bytes=VMEM_BYTES),
        cost_estimate=pl.CostEstimate(
            flops=4 * heads * tokens * tokens * size,
            bytes_accessed=qkv.size * 4 + tokens * heads * size * 6,
            transcendentals=2 * heads * tokens * tokens,
        ),
        name="attend_forward",
    )(qkv, qkv, qkv, cosine, sine, seg_row[None, :], seg_row[:, None], gains)


def attend_back_kernel(
    factor, each, query_ref, key_ref, value_ref, cos_ref, sin_ref, row_ref, col_ref, gains_ref,
    grad_ref, log_ref, out_ref, gain_ref, low_ref, query_grad, key_grad, value_grad,
):
    head = pl.program_id(0)
    group, place = head // each, head % each
    cosine, sine = cos_ref[...], sin_ref[...]
    gains = gains_ref[...]
    low_ref[...] = head_norm(query_ref[...], gains[0:1], cosine, sine)[2]
    key = head_norm(key_ref[...], gains[1:2], cosine, sine)[2]
    value = value_ref[...].astype(BF16)
    seg_row = row_ref[...]
    size = value.shape[1]
    key_grad[...] = jnp.zeros_like(key_grad)
    value_grad[...] = jnp.zeros_like(value_grad)

    def body(i, carry):
        rows = pl.ds(pl.multiple_of(i * TILE, TILE), TILE)
        query = low_ref[rows]
        grad_out = grad_ref[rows]
        scores = masked_scores(query, key, col_ref[rows], seg_row, factor)
        probs = jnp.exp(scores - log_ref[rows][:, :1])
        grad_probs = lax.dot_general(
            grad_out, value, (((1,), (1,)), ((), ())), preferred_element_type=F32
        )
        weighted = probs * grad_probs
        center = jnp.sum(weighted, axis=-1, keepdims=True)
        grad_scores = (weighted - probs * center).astype(BF16)
        query_grad[rows] = jnp.dot(grad_scores, key, preferred_element_type=F32) * factor
        first = (((0,), (0,)), ((), ()))
        key_grad[...] += lax.dot_general(grad_scores, query, first, preferred_element_type=F32)
        value_grad[...] += lax.dot_general(
            probs.astype(BF16), grad_out, first, preferred_element_type=F32
        )
        return carry

    lax.fori_loop(0, query_ref.shape[0] // TILE, body, 0)

    @pl.when(head == 0)
    def _():
        gain_ref[...] = jnp.zeros_like(gain_ref)

    for k, (raw_ref, grad) in enumerate(
        ((query_ref, query_grad[...]), (key_ref, key_grad[...] * factor))
    ):
        raw = raw_ref[...]
        rate = lax.rsqrt(jnp.mean(raw * raw, axis=-1, keepdims=True) + epsilon)
        normed = raw * rate
        grad_normed = grad * cosine + half_turn(grad * sine, 1.0)
        gain_ref[k : k + 1] += jnp.sum(grad_normed * normed, axis=0, keepdims=True)
        scaled = grad_normed * gains[k : k + 1]
        raw_grad = rate * (
            scaled - normed * jnp.mean(scaled * normed, axis=-1, keepdims=True)
        )
        columns = pl.ds(pl.multiple_of((k * each + place) * size, size), size)
        out_ref[group, :, columns] = raw_grad.astype(BF16)
    columns = pl.ds(pl.multiple_of((2 * each + place) * size, size), size)
    out_ref[group, :, columns] = value_grad[...].astype(BF16)


def attend_backward(qkv, cosine, sine, seg_row, gains, grad_heads, logs):
    tokens, size = cosine.shape
    each = qkv.shape[2] // (3 * size)
    heads = qkv.shape[0] * each
    parts, whole = attend_specs(tokens, size, each)
    by_head = pl.BlockSpec((tokens, size), lambda h: (0, h))
    return pl.pallas_call(
        partial(attend_back_kernel, size ** (-0.5), each),
        grid=(heads,),
        in_specs=parts + whole + [by_head, by_head],
        out_specs=[
            pl.BlockSpec(qkv.shape, lambda h: (0, 0, 0)),
            pl.BlockSpec((2, size), lambda h: (0, 0)),
        ],
        out_shape=[
            jax.ShapeDtypeStruct(qkv.shape, BF16),
            jax.ShapeDtypeStruct((2, size), F32),
        ],
        scratch_shapes=[
            pltpu.VMEM((tokens, size), BF16),
            pltpu.VMEM((tokens, size), F32),
            pltpu.VMEM((tokens, size), F32),
            pltpu.VMEM((tokens, size), F32),
        ],
        compiler_params=pltpu.CompilerParams(vmem_limit_bytes=VMEM_BYTES),
        cost_estimate=pl.CostEstimate(
            flops=10 * heads * tokens * tokens * size,
            bytes_accessed=qkv.size * 6 + tokens * heads * size * 6,
            transcendentals=heads * tokens * tokens,
        ),
        name="attend_backward",
    )(qkv, qkv, qkv, cosine, sine, seg_row[None, :], seg_row[:, None], gains, grad_heads, logs)


def slot_places(routes, route_gates, expert_ids):
    chosen = routes[None] == expert_ids[:, None, None]
    hit = jnp.any(chosen, axis=-1)
    gate = jnp.sum(jnp.where(chosen, route_gates[None], 0.0), axis=-1)
    count, tok_total = hit.shape
    grouped = hit.astype(BF16).reshape(count, tok_total // 128, 128)
    lane = jnp.arange(128)
    before = (lane[:, None] < lane[None, :]).astype(BF16)
    inside = jnp.einsum("egt,tu->egu", grouped, before, preferred_element_type=F32)
    totals = jnp.sum(grouped.astype(F32), axis=-1).astype(BF16)
    group = jnp.arange(tok_total // 128)
    earlier = (group[:, None] < group[None, :]).astype(BF16)
    offset = jnp.einsum("eg,gh->eh", totals, earlier, preferred_element_type=F32)
    place = (inside + offset[..., None]).reshape(count, tok_total).astype(jnp.int32)
    per_block = jnp.sum(hit.astype(jnp.int32).reshape(count, tok_total // BLOCK, BLOCK), axis=-1)
    begin = place.reshape(count, tok_total // BLOCK, BLOCK)[:, :, 0]
    end = begin + per_block
    low = begin // TILE
    high = jnp.where(end > begin, (end + TILE - 1) // TILE, low)
    return (jnp.where(hit, place, -1), gate, low, high)


def gather_kernel(scaled, each, low_ref, high_ref, *refs):
    rows_refs, place_refs, gate_refs, slots_ref = refs[0:2], refs[2:4], refs[4:6], refs[6]
    chip, piece = pl.program_id(0), pl.program_id(1)
    experts = slots_ref.shape[0]

    @pl.when((chip == 0) & (piece == 0))
    def _():
        slots_ref[...] = jnp.zeros_like(slots_ref)

    for k in range(2):
        rows_ref = rows_refs[k]
        parts, width = rows_ref.shape[1], rows_ref.shape[3]
        block = (2 * chip + k) * each + piece
        for e in range(experts):
            place = place_refs[k][e, 0]
            gate = gate_refs[k][e, 0]

            def body(i, carry):
                base = pl.multiple_of(i * TILE, TILE)
                wanted = lax.broadcasted_iota(jnp.int32, (TILE, BLOCK), 0) + base
                mask = place == wanted
                onehot = mask.astype(F32).astype(BF16)
                if scaled:
                    factor = jnp.sum(jnp.where(mask, gate, 0.0), axis=1, keepdims=True)
                for c in range(parts):
                    picked = jnp.dot(onehot, rows_ref[0, c], preferred_element_type=F32)
                    if scaled:
                        picked = picked * factor
                    where = (e, pl.ds(base, TILE), slice(c * width, (c + 1) * width))
                    slots_ref[where] = slots_ref[where] + picked.astype(BF16)
                return carry

            lax.fori_loop(low_ref[e, block], high_ref[e, block], body, 0)


def gather_slots(rows, place, gate, low, high, capacity, scaled):
    row_count, parts, per_row, width = rows.shape
    experts, tok_total = place.shape
    blocks = tok_total // BLOCK
    each = per_row // BLOCK

    def row_spec(k):
        return pl.BlockSpec(
            (1, parts, BLOCK, width),
            lambda z, j, *_: (2 * z + k, 0, j, 0),
        )

    def token_spec(k):
        return pl.BlockSpec(
            (experts, 1, 1, BLOCK),
            lambda z, j, *_: (0, (2 * z + k) * each + j, 0, 0),
        )

    places = place.reshape(experts, blocks, 1, BLOCK)
    gates = gate.reshape(experts, blocks, 1, BLOCK)
    return pl.pallas_call(
        partial(gather_kernel, scaled, each),
        grid_spec=pltpu.PrefetchScalarGridSpec(
            num_scalar_prefetch=2,
            grid=(row_count // 2, each),
            in_specs=[
                row_spec(0), row_spec(1), token_spec(0), token_spec(1), token_spec(0), token_spec(1),
            ],
            out_specs=pl.BlockSpec((experts, capacity, parts * width), lambda *_: (0, 0, 0)),
        ),
        out_shape=jax.ShapeDtypeStruct((experts, capacity, parts * width), BF16),
        compiler_params=pltpu.CompilerParams(vmem_limit_bytes=VMEM_BYTES),
        cost_estimate=pl.CostEstimate(
            flops=2 * 24 * experts * TILE * BLOCK * parts * width,
            bytes_accessed=(tok_total + experts * capacity) * parts * width * 2,
            transcendentals=0,
        ),
        name="gather_slots",
    )(low, high, rows, rows, places, places, gates, gates)


def combine_kernel(
    scaled, added, each, begin, low_ref, high_ref, core_ref, slots_ref, place_ref, gate_ref, *refs
):
    out_ref, total_ref = refs[-2:]
    chip, piece = pl.program_id(0) + begin, pl.program_id(1)
    block = (2 * chip + core_ref[0]) * each + piece
    experts = slots_ref.shape[0]
    parts, width = out_ref.shape[0], out_ref.shape[3]
    total_ref[...] = jnp.zeros_like(total_ref)
    for e in range(experts):
        place = jnp.broadcast_to(place_ref[e, 0].astype(F32), (8, BLOCK)).T[:, :1]
        if scaled:
            gate = jnp.broadcast_to(gate_ref[e, 0], (8, BLOCK)).T[:, :1]

        def body(i, carry):
            base = pl.multiple_of(i * TILE, TILE)
            wanted = lax.broadcasted_iota(jnp.int32, (BLOCK, TILE), 1) + base
            onehot = (place == wanted.astype(F32)).astype(F32).astype(BF16)
            for c in range(parts):
                columns = slice(c * width, (c + 1) * width)
                picked = jnp.dot(
                    onehot, slots_ref[e, pl.ds(base, TILE), columns], preferred_element_type=F32
                )
                if scaled:
                    picked = picked * gate
                total_ref[:, columns] = total_ref[:, columns] + picked
            return carry

        lax.fori_loop(low_ref[e, block], high_ref[e, block], body, 0)
    for c in range(parts):
        total = total_ref[:, c * width : (c + 1) * width]
        if added:
            total = total + refs[0][c, 0].astype(F32)
        out_ref[c, 0] = total.astype(BF16)


def combine_slots(
    slots, place, gate, low, high, core, chips, per_row, parts, scaled, begin=0, more=None, into=None
):
    experts, capacity, model_width = slots.shape
    width = model_width // parts
    each = per_row // BLOCK
    blocks = place.shape[1] // BLOCK
    count = chips // 2

    def token_block(z, j, low_ref, high_ref, core_ref):
        return (0, (2 * (z + begin) + core_ref[0]) * each + j, 0, 0)

    half = pl.BlockSpec((parts, 1, BLOCK, width), lambda z, j, *_: (0, z, j, 0))
    whole = pl.BlockSpec((parts, 1, BLOCK, width), lambda z, j, *_: (0, z + begin, j, 0))
    added = more is not None
    in_specs = [
        pl.BlockSpec(
            (experts, capacity, model_width),
            lambda *_: (0, 0, 0),
            pipeline_mode=pl.Buffered(1),
        ),
        pl.BlockSpec((experts, 1, 1, BLOCK), token_block),
        pl.BlockSpec((experts, 1, 1, BLOCK), token_block),
    ]
    inputs = [
        low,
        high,
        core,
        slots,
        place.reshape(experts, blocks, 1, BLOCK),
        gate.reshape(experts, blocks, 1, BLOCK),
    ]
    aliases = {}
    if added:
        in_specs.append(half)
        inputs.append(more)
    if into is not None:
        aliases = {len(inputs): 0}
        in_specs.append(pl.BlockSpec(memory_space=pl.ANY))
        inputs.append(into)
    return pl.pallas_call(
        partial(combine_kernel, scaled, added, each, begin),
        grid_spec=pltpu.PrefetchScalarGridSpec(
            num_scalar_prefetch=3,
            grid=(count, each),
            in_specs=in_specs,
            out_specs=whole if added else half,
            scratch_shapes=[pltpu.VMEM((BLOCK, model_width), F32)],
        ),
        out_shape=jax.ShapeDtypeStruct(
            (parts, chips if added else count, per_row, width), BF16
        ),
        input_output_aliases=aliases,
        compiler_params=pltpu.CompilerParams(vmem_limit_bytes=VMEM_BYTES),
        cost_estimate=pl.CostEstimate(
            flops=12 * experts * TILE * BLOCK * model_width,
            bytes_accessed=slots.size * 2 + parts * count * per_row * width * 2,
            transcendentals=0,
        ),
        name="combine_slots",
    )(*inputs)


def swap_cores(values):
    return lax.ppermute(values, "core", [(0, 1), (1, 0)])


def swap_cols(values, mask):
    count = lax.axis_size("col")
    return lax.ppermute(values, "col", [(i, i ^ mask) for i in range(count)])


def fence(*values):
    return lax.optimization_barrier(values)


def plain(values):
    return with_layout_constraint(values, Layout(tuple(range(values.ndim))))


def gather_cols(values):
    count = lax.axis_size("col")
    me = lax.axis_index("col")
    result = jnp.zeros((count,) + values.shape, values.dtype)
    for mask in range(count):
        piece = swap_cols(values, mask) if mask else values
        result = lax.dynamic_update_index_in_dim(result, piece, me ^ mask, 0)
    return result


def sum_cols(pieces):
    total = 0.0
    for piece in send_parts(pieces):
        total = total + piece.astype(F32)
    return total


def split_parts(parts):
    me = lax.axis_index("col")
    return [
        plain(lax.dynamic_index_in_dim(parts, me ^ mask, 0, keepdims=False))
        for mask in range(lax.axis_size("col"))
    ]


def send_parts(pieces):
    return pieces[:1] + [swap_cols(pieces[mask], mask) for mask in range(1, len(pieces))]


def join_parts(pieces, axis, result=None, offset=0):
    me = lax.axis_index("col")
    if result is None:
        shape = list(pieces[0].shape)
        shape[axis] *= len(pieces)
        result = jnp.zeros(shape, pieces[0].dtype)
    size = result.shape[axis] // len(pieces)
    for mask, piece in enumerate(pieces):
        start = (me ^ mask) * size + offset
        result = lax.dynamic_update_slice_in_dim(result, piece, start, axis)
    return result


def swap_chips(values, mask):
    count = lax.axis_size("chip")
    return lax.ppermute(values, "chip", [(i, i ^ mask) for i in range(count)])


def over_chips(values):
    chips = lax.axis_size("chip")
    chip = lax.axis_index("chip")
    same = jnp.zeros((chips,) + values.shape, values.dtype)
    for mask in range(chips):
        piece = swap_chips(values, mask) if mask else values
        same = lax.dynamic_update_index_in_dim(same, piece, chip ^ mask, 0)
    return same


def over_cores(same):
    core = lax.axis_index("core")
    other = swap_cores(same)
    both = jnp.stack([jnp.where(core == 0, same, other), jnp.where(core == 0, other, same)], axis=1)
    return both.reshape(-1, same.shape[-1])


def pick(pieces, index):
    chosen = pieces[0]
    for k in range(1, len(pieces)):
        chosen = jnp.where(index == k, pieces[k], chosen)
    return chosen


def own_heads(cols, heads_row):
    return 2 * heads_row == cols


def heads_in(weight, ratio, size):
    chips, cols = lax.axis_size("chip"), lax.axis_size("col")
    core, col = lax.axis_index("core"), lax.axis_index("col")
    rows = 2 * chips
    row = 2 * lax.axis_index("chip") + core
    kinds, features, width = weight.shape
    pieces = []
    if own_heads(cols, width // size):
        p = width // size
        for t in range(p):
            pairs = [
                (k * cols + c, c // p * cols + k * p + (t + c) % p)
                for k in range(2)
                for c in range(cols)
            ]
            piece = lax.dynamic_slice_in_dim(weight, (t + col) % p * size, size, 2)
            pieces.append(lax.ppermute(piece, ("core", "col"), pairs))
        pieces = [pick(pieces, (col - b) % p) for b in range(p)]
        return jnp.concatenate(
            [jnp.concatenate([p[a] for a in range(kinds)], axis=1) for p in pieces], axis=0
        )
    block = features // ratio
    for k in range(ratio):
        pairs = []
        for r in range(rows):
            for c in range(cols):
                h = (k + r) % ratio
                pairs.append((r * cols + c, (ratio * c + h) * cols + r // ratio))
        piece = lax.dynamic_slice_in_dim(weight, (k + row) % ratio * block, block, 1)
        pieces.append(lax.ppermute(piece, ALL, pairs))
    return jnp.concatenate(
        [pick([p[a] for p in pieces], (row - s) % ratio) for a in range(kinds) for s in range(ratio)],
        axis=1,
    )


def heads_out(grad, kinds, ratio, heads_row):
    chips, cols = lax.axis_size("chip"), lax.axis_size("col")
    col = lax.axis_index("col")
    rows = 2 * chips
    row = 2 * lax.axis_index("chip") + lax.axis_index("core")
    mine = grad.reshape(rows, -1, grad.shape[2])
    mine = lax.psum_scatter(mine, ROW, scatter_dimension=0, tiled=True)[0]
    block = mine.shape[0]
    pieces = []
    if own_heads(cols, heads_row):
        p = heads_row
        size = mine.shape[1] // kinds
        for t in range(p):
            pairs = [
                (k * cols + c, c // p * cols + k * p + (c - t) % p)
                for k in range(2)
                for c in range(cols)
            ]
            piece = lax.dynamic_slice_in_dim(mine, (col - t) % p * (block // p), block // p, 0)
            pieces.append(lax.ppermute(piece, ("core", "col"), pairs))
        pieces = [pick(pieces, (i - col) % p) for i in range(p)]
        return jnp.stack(
            [
                jnp.concatenate([q[:, a * size : (a + 1) * size] for q in pieces], axis=1)
                for a in range(kinds)
            ]
        ).astype(F32)
    width = mine.shape[1] // (kinds * ratio)
    for k in range(ratio):
        pairs = []
        for r in range(rows):
            for c in range(cols):
                s = (r - k) % ratio
                pairs.append((r * cols + c, (ratio * c + s) * cols + r // ratio))
        start = (row - k) % ratio * width
        piece = jnp.stack(
            [
                lax.dynamic_slice_in_dim(mine, a * ratio * width + start, width, 1)
                for a in range(kinds)
            ]
        )
        pieces.append(lax.ppermute(piece, ALL, pairs))
    return jnp.concatenate(
        [pick(pieces, (h - row) % ratio) for h in range(ratio)], axis=1
    ).astype(F32)


def sum_rows(values):
    total = values
    for axis in ROW:
        count = lax.axis_size(axis)
        step = 1
        while step < count:
            total = total + lax.ppermute(total, axis, [(i, i ^ step) for i in range(count)])
            step *= 2
    return total


def local(
    tokens,
    attn_gain,
    qkv_weight,
    query_gain,
    key_gain,
    out_weight,
    moe_gain,
    gate_up_weight,
    down_weight,
    segments,
    routes,
    route_gates,
    cotangent,
):
    cols = lax.axis_size("col")
    chips = lax.axis_size("chip")
    rows = 2 * chips
    col = lax.axis_index("col")
    core = lax.axis_index("core")
    row = 2 * lax.axis_index("chip") + core
    per_row, col_width = tokens.shape
    model_width = col_width * cols
    head_size = query_gain.shape[0]
    ratio = rows // cols
    head_width = model_width // cols

    experts_here, _, double_units = gate_up_weight.shape
    units = double_units // 2
    split = max(1, cols // experts_here)
    mine_count = experts_here * split // cols
    part_units = units // split
    capacity = 2 * rows * per_row * routes.shape[1] // (experts_here * rows)

    gate_up_parts = (
        gate_up_weight.reshape(experts_here, col_width, 2, split, part_units)
        .transpose(0, 3, 1, 2, 4)
        .reshape(cols, mine_count, col_width, 2 * part_units)
    )
    down_parts = down_weight.reshape(cols, mine_count, part_units, col_width)

    heads_row = qkv_weight.shape[2] // head_size
    groups = chips if own_heads(cols, heads_row) else 1

    def by_col(values):
        if groups == 1:
            return values.reshape(cols, head_width, col_width)
        values = values.reshape(groups, cols, head_width // groups, col_width)
        return values.transpose(1, 0, 2, 3).reshape(cols, head_width, col_width)

    def by_head(values):
        if groups > 1:
            values = values.reshape(cols, groups, head_width // groups, col_width)
            values = values.transpose(1, 0, 2, 3)
        return values.reshape(model_width, col_width)

    tokens_all = gather_cols(tokens)
    small = gather_cols(jnp.concatenate([attn_gain, segments.astype(F32).reshape(-1)]))
    qkv_rows, small, tokens_all, out_in = fence(
        heads_in(qkv_weight, ratio, head_size), small, tokens_all, out_weight
    )
    gain_all = small[:, :col_width]
    segs = small[:, col_width:].astype(jnp.int32)
    cuts = (0, col_width // 2, 3 * col_width // 4, col_width)
    first, second, last = (
        split_parts(gate_up_parts[:, :, cuts[i] : cuts[i + 1]]) for i in range(3)
    )
    gate_up_first = send_parts(first)
    qkv_rows, out_rows, gate_up_first, second, last = fence(
        over_chips(qkv_rows), over_chips(out_in), gate_up_first, second, last
    )
    gate_up_second, gate_up_last = send_parts(second), send_parts(last)
    if groups > 1:
        half = model_width // 2
        qkv_halves = [(qkv_rows, core * half), (swap_cores(qkv_rows), (1 - core) * half)]
    else:
        half = model_width
        qkv_halves = [(over_cores(qkv_rows)[None], 0)]
    out_split = by_col(over_cores(out_rows))
    seg_row = lax.dynamic_index_in_dim(segs.reshape(rows, per_row), row, 0, keepdims=False)

    first = row * experts_here
    expert_ids = first + (col * mine_count + jnp.arange(mine_count, dtype=jnp.int32)) // split
    place, gate, low, high = slot_places(routes, route_gates, expert_ids)

    cosine, sine = rope_tables(seg_row, head_size)
    stream_all = tokens_all.astype(F32)
    rate_one = lax.rsqrt(jnp.sum(stream_all * stream_all, axis=(0, 2)) / model_width + epsilon)
    rate_one = rate_one[:, None]
    normed_all = jnp.concatenate(
        [(stream_all[c] * rate_one * gain_all[c]).astype(BF16) for c in range(cols)], axis=1
    )
    qkv = sum(
        jnp.einsum(
            "td,gdk->gtk",
            lax.dynamic_slice_in_dim(normed_all, begin, half, 1),
            weight,
            preferred_element_type=F32,
        )
        for weight, begin in qkv_halves
    )
    head_gains = jnp.stack([query_gain, key_gain])
    heads_low, logs = attend_forward(qkv, cosine, sine, seg_row, head_gains)
    heads_low, gate_up_second = fence(heads_low, gate_up_second)
    heads_all = gather_cols(heads_low)
    stream = tokens.astype(F32)
    hidden_one = plain(
        stream + jnp.einsum("ctk,ckd->td", heads_all, out_split, preferred_element_type=F32)
    )
    rate_two = lax.rsqrt(
        width_total(jnp.sum(hidden_one * hidden_one, axis=-1)) / model_width + epsilon
    )[:, None]
    moe_in = plain((hidden_one * rate_two * moe_gain).astype(BF16))
    moe_in, gate_up_last, down_first = fence(moe_in, gate_up_last, split_parts(down_parts))
    gate_up = jnp.zeros((mine_count, model_width, 2 * part_units), BF16)
    gate_up = join_parts(gate_up_first, 1, gate_up, 0)
    gate_up = join_parts(gate_up_second, 1, gate_up, cuts[1])
    gate_up = join_parts(gate_up_last, 1, gate_up, cuts[2])

    moe_all = lax.all_gather(moe_in, ALL, axis=0).reshape(rows, cols, per_row, col_width)
    mine = jnp.reshape(core, (1,))
    others = 1 - mine
    moe_all, down_first, cot_in, gate_up, place, gate, low, high = fence(
        moe_all, down_first, cotangent, gate_up, place, gate, low, high
    )
    cot_all = lax.all_gather(cot_in, ALL, axis=0).reshape(rows, cols, per_row, col_width)
    down = join_parts(send_parts(down_first), 2)
    slot_inputs = gather_slots(moe_all, place, gate, low, high, capacity, False)

    gate_weight = gate_up[..., :part_units]
    up_weight = gate_up[..., part_units:]
    gate_pre = jnp.einsum(
        "ecd,edf->ecf", slot_inputs, gate_weight, preferred_element_type=F32
    ).astype(BF16)
    up_pre = jnp.einsum(
        "ecd,edf->ecf", slot_inputs, up_weight, preferred_element_type=F32
    ).astype(BF16)
    gate_wide = gate_pre.astype(F32)
    up_wide = up_pre.astype(F32)
    sigmoid_gate = jax.nn.sigmoid(gate_wide)
    activated = gate_wide * sigmoid_gate
    hidden = (activated * up_wide).astype(BF16)
    hidden, down = fence(hidden, down)

    combine = partial(
        combine_slots, place=place, gate=gate, low=low, high=high,
        chips=chips, per_row=per_row, parts=cols,
    )

    def feature_block(values, index):
        return lax.dynamic_slice_in_dim(values, index * col_width, col_width, 2)

    expert_out = jnp.einsum("ecf,efd->ecd", hidden, down, preferred_element_type=F32).astype(BF16)
    middle = chips // 2
    out_first = combine(expert_out, core=others, scaled=True)
    out_last = combine(expert_out, core=others, scaled=True, begin=middle)
    out_partial = combine(expert_out, core=mine, scaled=True, more=swap_cores(out_first))
    out_partial = combine(
        expert_out, core=mine, scaled=True, begin=middle, more=swap_cores(out_last), into=out_partial
    )
    out_partial, cot_all = fence(out_partial, cot_all)
    out_partial = plain(lax.psum_scatter(out_partial, "col", scatter_dimension=0, tiled=True)[0])

    grad_slot = gather_slots(cot_all, place, gate, low, high, capacity, True)

    def down_grad(mask, hidden, grad_slot):
        part = jnp.einsum(
            "ecf,ecd->efd", hidden, feature_block(grad_slot, col ^ mask),
            preferred_element_type=F32,
        )
        return part.astype(BF16) if mask else part

    near = cols // 2 + 1
    down_grads = [down_grad(mask, hidden, grad_slot) for mask in range(1, cols)]
    down_grads, grad_slot = fence(down_grads, grad_slot)
    near_down = [swap_cols(part, 1 + i) for i, part in enumerate(down_grads[: near - 1])]
    far_down = [swap_cols(part, near + i) for i, part in enumerate(down_grads[near - 1 :])]
    grad_hidden = jnp.einsum("ecd,efd->ecf", grad_slot, down, preferred_element_type=F32)
    grad_gate_pre = (
        grad_hidden * up_wide * sigmoid_gate * (1.0 + gate_wide * (1.0 - sigmoid_gate))
    ).astype(BF16)
    grad_up_pre = (grad_hidden * activated).astype(BF16)

    grad_slot_in = jnp.einsum(
        "ecf,edf->ecd",
        jnp.concatenate([grad_gate_pre, grad_up_pre], axis=-1),
        gate_up,
        preferred_element_type=F32,
    ).astype(BF16)
    grad_first = swap_cores(combine(grad_slot_in, core=others, scaled=False))
    grad_last = combine(grad_slot_in, core=others, scaled=False, begin=middle)
    grad_last, grad_gate_pre, grad_up_pre, near_down, out_partial = fence(
        grad_last, grad_gate_pre, grad_up_pre, near_down, out_partial
    )
    grad_last = swap_cores(grad_last)
    grad_inner = jnp.concatenate([grad_gate_pre, grad_up_pre], axis=-1)
    grad_first, grad_inner = fence(grad_first, grad_inner)
    grad_partial = combine(grad_slot_in, core=mine, scaled=False, more=grad_first)
    grad_partial = combine(
        grad_slot_in, core=mine, scaled=False, begin=middle, more=grad_last, into=grad_partial
    )
    grad_partial, grad_inner, far_down, hidden, grad_slot = fence(
        grad_partial, grad_inner, far_down, hidden, grad_slot
    )
    grad_partial = plain(lax.psum_scatter(grad_partial, "col", scatter_dimension=0, tiled=True)[0])
    inner_parts = []
    for mask in range(cols):
        part = jnp.einsum(
            "ecd,ecf->edf", feature_block(slot_inputs, col ^ mask), grad_inner,
            preferred_element_type=F32,
        )
        inner_parts.append(part.astype(BF16) if mask else part)
    own_down = down_grad(0, hidden, grad_slot)
    grad_partial, inner_parts, own_down = fence(grad_partial, inner_parts, own_down)
    got_down = [own_down] + near_down + far_down
    grad_moe_in = plain(lax.psum_scatter(grad_partial, "chip", scatter_dimension=0, tiled=True)[0])
    far_parts = inner_parts[near:]
    got_inner = inner_parts[:1] + [swap_cols(inner_parts[mask], mask) for mask in range(1, near)]
    grad_moe_in, got_inner, out_partial, far_parts = fence(
        grad_moe_in, got_inner, out_partial, far_parts
    )
    grad_moe_in = grad_moe_in.astype(F32)

    gain_two = jnp.sum(grad_moe_in * hidden_one * rate_two, axis=0)
    grad_hidden_one = cotangent.astype(F32) + norm_back(
        grad_moe_in, hidden_one, rate_two, moe_gain, model_width
    )
    grad_branch = plain(grad_hidden_one.astype(BF16))
    grad_heads = sum_cols(
        split_parts(
            jnp.einsum("td,ckd->ctk", grad_branch, out_split, preferred_element_type=F32).astype(BF16)
        )
    ).astype(BF16)
    grad_down = jnp.zeros((cols, mine_count, part_units, col_width), F32)
    for mask in range(cols):
        grad_down = lax.dynamic_update_index_in_dim(
            grad_down, got_down[mask].astype(F32), col ^ mask, 0
        )
    grad_heads, out_partial, far_parts, grad_down = fence(
        grad_heads, out_partial, far_parts, grad_down
    )
    far_parts = [swap_cols(part, near + i) for i, part in enumerate(far_parts)]
    moe_result = lax.psum_scatter(out_partial, "chip", scatter_dimension=0, tiled=True)[0]
    grad_out_weight = lax.psum_scatter(
        by_head(
            jnp.einsum("ctk,td->ckd", heads_all, grad_branch, preferred_element_type=F32).astype(BF16)
        ),
        ROW,
        scatter_dimension=0,
        tiled=True,
    ).astype(F32)
    grad_projected, grad_gains = attend_backward(
        qkv, cosine, sine, seg_row, head_gains, grad_heads, logs
    )
    grad_gate_up = jnp.zeros((cols, mine_count, col_width, 2 * part_units), F32)
    for mask in range(near):
        grad_gate_up = lax.dynamic_update_index_in_dim(
            grad_gate_up, got_inner[mask].astype(F32), col ^ mask, 0
        )
    grad_projected, moe_result, grad_gate_up = fence(grad_projected, moe_result, grad_gate_up)
    output = (hidden_one + moe_result.astype(F32)).astype(BF16)
    normed_parts = [
        plain(
            jnp.einsum("gtk,gdk->td", grad_projected, weight, preferred_element_type=F32).astype(BF16)
        )
        for weight, _ in qkv_halves
    ]
    if groups > 1:
        mine_first = jnp.concatenate(normed_parts, axis=1)
        mine_last = jnp.concatenate(normed_parts[::-1], axis=1)
        normed_parts = jnp.where(core == 0, mine_first, mine_last)
    else:
        normed_parts = normed_parts[0]
    normed_parts, grad_projected, far_parts = fence(normed_parts, grad_projected, far_parts)
    grad_normed = sum_cols(
        [
            lax.dynamic_slice_in_dim(normed_parts, (col ^ mask) * col_width, col_width, 1)
            for mask in range(cols)
        ]
    )
    grad_qkv = heads_out(
        plain(
            jnp.einsum(
                "td,gtk->gdk", normed_all, grad_projected, preferred_element_type=F32
            ).astype(BF16)
        ),
        3,
        ratio,
        heads_row,
    )

    scaled_grad = grad_normed * attn_gain
    gain_one = jnp.sum(grad_normed * stream * rate_one, axis=0)
    across = jnp.sum(scaled_grad * stream, axis=-1)
    small = width_total(jnp.concatenate([across, grad_gains.reshape(-1)]))
    across = small[:per_row, None]
    gains = sum_rows(jnp.concatenate([gain_one, gain_two, small[per_row:]]))
    grad_attn_gain = gains[:col_width]
    grad_moe_gain = gains[col_width : 2 * col_width]
    grad_query_gain = gains[2 * col_width : 2 * col_width + head_size]
    grad_key_gain = gains[2 * col_width + head_size :]
    grad_tokens = (
        grad_hidden_one
        + rate_one * scaled_grad
        - stream * rate_one * rate_one * rate_one * across / model_width
    ).astype(BF16)

    for mask in range(near, cols):
        grad_gate_up = lax.dynamic_update_index_in_dim(
            grad_gate_up, far_parts[mask - near].astype(F32), col ^ mask, 0
        )
    grad_gate_up = (
        grad_gate_up.reshape(experts_here, split, col_width, 2, part_units)
        .transpose(0, 2, 3, 1, 4)
        .reshape(experts_here, col_width, double_units)
    )
    grad_down = grad_down.reshape(experts_here, units, col_width)
    return (
        output,
        grad_tokens,
        grad_attn_gain,
        grad_qkv,
        grad_query_gain,
        grad_key_gain,
        grad_out_weight,
        grad_moe_gain,
        grad_gate_up,
        grad_down,
    )


def solution(mesh):
    rows, cols = mesh.devices.shape
    fine = Mesh(mesh.devices.reshape(rows // 2, 2, cols), ("chip", "core", "col"))
    return jax.shard_map(
        local,
        mesh=fine,
        in_specs=(
            P(ROW, "col"),
            P("col"),
            P(None, "col", ROW),
            P(),
            P(),
            P(ROW, "col"),
            P("col"),
            P(ROW, "col", None),
            P(ROW, None, "col"),
            P("col", None),
            P(),
            P(),
            P(ROW, "col"),
        ),
        out_specs=(
            P(ROW, "col"),
            P(ROW, "col"),
            P("col"),
            P(None, "col", ROW),
            P(),
            P(),
            P(ROW, "col"),
            P("col"),
            P(ROW, "col", None),
            P(ROW, None, "col"),
        ),
        check_vma=False,
    )
```
